32 devices in a mesh: space: 8 (over y, x, core), snap: 4 (over z).
Axes of the slice: x: 2, y: 2, z: 4, core: 2. Of those that a mesh axis runs over, the one named last changes fastest.
Arguments:
- owned_x: bfloat16 [1024, 128, 512], P('space', None, 'snap'), may hold values from -600 to 600
- owned_y: bfloat16 [1024, 128, 512], P('space', None, 'snap'), may hold values from -6 to 6
- patch_dest: int32 [1024], P('space'), may hold values from -1 to 511, as said below
Outputs:
- q_basis: float32 [512, 128, 512], P('space', 'snap')
- r_factor: float32 [512, 512], replicated
- projection: float32 [512, 512], replicated
The draws below stay inside these ranges and needn't reach their ends.
Inputs may be any that keep to these rules, and one draw needn't show every extreme that they name: `patch_dest`: every row block 0 to 511 is named by exactly one slot; -1 marks an empty slot. The 128 slots of one owner (one aligned block of 128 slots) name at most 16 row blocks of any one slab d * 64 to (d + 1) * 64 - 1, and some owner names exactly 16 of every slab.
All inputs are finite; a program needn't handle non-finite values.
Results may differ from the reference program's by a relative error of at most 0.0003.
Values may be sent and summed in bfloat16 or wider, within the bound.
No kernel may reach another device: no remote copies, remote signals or barrier semaphores. Data moves between devices by JAX's collectives and lax.ppermute only.
A program may use at most 128 MiB of HBM per device.

```python
import math
import jax
import jax.numpy as jnp
from jax import lax

K = 512
PATCH = 128
BLK_DEV = 64
OWNED = 1024
ROW_BLOCKS = 512
ROWS = 65536
N_SPACE = 8


def draw_patch_dest(key, part):
    subkeys = jax.random.split(key, 5)
    moved_load = jax.random.randint(subkeys[0], (N_SPACE // 2,), 0, BLK_DEV + 1).at[0].set(BLK_DEV)
    owner_loads = jnp.stack([BLK_DEV + moved_load, BLK_DEV - moved_load], axis=1).reshape(N_SPACE)
    load_ends = jnp.cumsum(owner_loads)
    starts = load_ends - owner_loads
    position = jnp.arange(N_SPACE * BLK_DEV, dtype=jnp.int32)
    virtual = jnp.sum((load_ends[None, :] <= position[:, None]).astype(jnp.int32), axis=1)
    within = position - starts[virtual]
    owner_of = jax.random.permutation(subkeys[1], N_SPACE)
    slab_of = jax.random.permutation(subkeys[2], N_SPACE)
    inner_perm = jax.vmap(lambda sub: jax.random.permutation(sub, BLK_DEV))(jax.random.split(subkeys[3], N_SPACE))
    slot_perm = jax.vmap(lambda sub: jax.random.permutation(sub, 2 * BLK_DEV))(jax.random.split(subkeys[4], N_SPACE))
    source = owner_of[virtual]
    slot_index = slot_perm[source, within]
    slab_index = slab_of[position % N_SPACE]
    block_index = slab_index * BLK_DEV + inner_perm[slab_index, position // N_SPACE]
    empty_list = jnp.full((N_SPACE * 2 * BLK_DEV,), -1, jnp.int32)
    return empty_list.at[source * (2 * BLK_DEV) + slot_index].set(block_index.astype(jnp.int32))


def draw_owned_x(key, part):
    subkeys = jax.random.split(key, 5)
    taps = 12
    noise = jax.random.truncated_normal(subkeys[0], -4.0, 4.0, (OWNED, PATCH, K + taps), jnp.float32)
    memory = jax.random.uniform(subkeys[4], (K,), jnp.float32, 0.3, 0.9)
    values = noise[:, :, taps:]
    for lag in range(1, taps + 1):
        values = values + memory ** lag * noise[:, :, taps - lag:taps - lag + K]
    col_scale = jnp.exp(jax.random.uniform(subkeys[1], (K,), jnp.float32, 0.0, math.log(4.0)))
    mixed = values * col_scale
    return jnp.clip(mixed, -600.0, 600.0).astype(jnp.bfloat16)


def level_of(own_key, extent, cuts, least, largest):
    gain, own = 1.0, jax.random.fold_in(own_key, 6)
    for dim, shards_of in cuts:
        heights = jnp.exp(jax.random.uniform(jax.random.fold_in(own, dim), (shards_of,), jnp.float32, least / len(cuts), largest / len(cuts)))
        gain = gain * jnp.repeat(heights, extent[dim] // shards_of).reshape([-1 if axis == dim else 1 for axis in range(len(extent))])
    return gain


def gaussian(rng, shape, spread, bound, shards=(), kind=jnp.bfloat16):
    loudness = level_of(rng, shape, shards, -0.22, 0.18) if shards else 1.0
    drawn = jax.random.normal(rng, shape, jnp.float32) * spread * loudness
    return jnp.minimum(jnp.maximum(drawn, -bound), bound).astype(kind)


def setup_inputs(seed: int = 0) -> dict:
    key_list = jax.random.split(jax.random.key(seed), 4)
    return {
        "owned_x": draw_owned_x(jax.random.fold_in(key_list[3], 71), 0),
        "owned_y": gaussian(key_list[1], (OWNED, PATCH, K), 1.0, 6.0, ((0, 8), (2, 4))),
        "patch_dest": draw_patch_dest(jax.random.fold_in(key_list[3], 71), 0),
    }


def place_blocks(owned, patch_dest):
    target = jnp.where(patch_dest >= 0, patch_dest, ROW_BLOCKS).astype(jnp.int32)
    empty_slab = jnp.zeros((ROW_BLOCKS, PATCH, K), owned.dtype)
    return empty_slab.at[target].set(owned, mode='drop')

def reference(owned_x, owned_y, patch_dest):
    slab_x = place_blocks(owned_x, patch_dest).reshape(ROWS, K)
    slab_y = place_blocks(owned_y, patch_dest).reshape(ROWS, K)
    gram_mean = lax.dot_general(slab_x.astype(jnp.float32), slab_x.astype(jnp.float32), (((0,), (0,)), ((), ())), preferred_element_type=jnp.float32) / ROWS
    lower = jnp.linalg.cholesky(gram_mean)
    identity = jnp.eye(K, dtype=lower.dtype)
    inverse = lax.linalg.triangular_solve(lower, identity, left_side=True, lower=True)
    basis_rows = jnp.dot(slab_x.astype(jnp.float32), inverse.T, precision=lax.Precision.HIGHEST)
    projection = lax.dot_general(basis_rows, slab_y.astype(jnp.float32), (((0,), (0,)), ((), ())), precision=lax.Precision.HIGHEST) / math.sqrt(ROWS)
    return (basis_rows.reshape(ROW_BLOCKS, PATCH, K), lower.T, projection)
```

```python
import math

import jax
import jax.numpy as jnp
from jax import lax
from jax.experimental import pallas as pl
from jax.experimental.pallas import tpu as pltpu
from jax.sharding import PartitionSpec as P

TILE = 128
GROUP = 8
CELL_TILE = 16
HIGHEST = lax.Precision.HIGHEST
SMEM = pl.BlockSpec(memory_space=pltpu.SMEM)
VMEM = pl.BlockSpec(memory_space=pltpu.VMEM)
ANY = pl.BlockSpec(memory_space=pl.ANY)
ROWS_BY_ROWS = (((0,), (0,)), ((), ()))
LANES_BY_LANES = (((1,), (1,)), ((), ()))


def plan_kernel(slabs, capacity, per_slab, dest_ref, table_ref, meta_ref, count_ref):
    def clear(i, _):
        table_ref[i] = 0
        meta_ref[i // capacity, i % capacity] = -1
        return 0

    def clear_count(i, _):
        count_ref[i] = 0
        return 0

    def place(i, _):
        block = dest_ref[i]

        @pl.when(block >= 0)
        def _():
            slab = block // per_slab
            rank = count_ref[slab]
            count_ref[slab] = rank + 1
            table_ref[slab * capacity + rank] = i
            meta_ref[slab, rank] = block - slab * per_slab

        return 0

    lax.fori_loop(0, slabs, clear_count, 0)
    lax.fori_loop(0, slabs * capacity, clear, 0)
    lax.fori_loop(0, dest_ref.shape[0], place, 0)


def plan(dest, slabs, capacity, per_slab):
    return pl.pallas_call(
        lambda *refs: plan_kernel(slabs, capacity, per_slab, *refs),
        out_shape=(
            jax.ShapeDtypeStruct((slabs * capacity,), jnp.int32),
            jax.ShapeDtypeStruct((slabs, TILE), jnp.int32),
        ),
        in_specs=[SMEM],
        out_specs=(SMEM, SMEM),
        scratch_shapes=[pltpu.SMEM((slabs,), jnp.int32)],
        name="plan",
    )(dest)


def arrival_kernel(slabs, capacity, meta_ref, table_ref):
    def clear(i, _):
        table_ref[i] = 0
        return 0

    def place(i, _):
        block = meta_ref[i // capacity, i % capacity]

        @pl.when(block >= 0)
        def _():
            table_ref[block] = i

        return 0

    lax.fori_loop(0, table_ref.shape[0], clear, 0)
    lax.fori_loop(0, slabs * capacity, place, 0)


def arrival(meta, slabs, capacity, per_slab):
    return pl.pallas_call(
        lambda *refs: arrival_kernel(slabs, capacity, *refs),
        out_shape=jax.ShapeDtypeStruct((per_slab,), jnp.int32),
        in_specs=[SMEM],
        out_specs=SMEM,
        name="arrival",
    )(meta)


def pack_kernel(part, table_ref, owned_ref, out_ref, sem):
    def send(i, _):
        pltpu.make_async_copy(owned_ref.at[table_ref[i], :, part], out_ref.at[i], sem).start()
        return 0

    lax.fori_loop(0, out_ref.shape[0], send, 0)
    pltpu.make_async_copy(out_ref, out_ref, sem).wait()


def pack(owned, table, part):
    slots, shares, _, rows, width = owned.shape
    return pl.pallas_call(
        lambda *refs: pack_kernel(part, *refs),
        out_shape=jax.ShapeDtypeStruct((slots, shares, rows, width), owned.dtype),
        in_specs=[SMEM, ANY],
        out_specs=ANY,
        scratch_shapes=[pltpu.SemaphoreType.DMA],
        cost_estimate=pl.CostEstimate(
            flops=0, bytes_accessed=2 * slots * shares * rows * width * 2, transcendentals=0
        ),
        name="pack",
    )(table, owned)


def settle_kernel(table_ref, moved_ref, out_ref, sem):
    def send(i, _):
        pltpu.make_async_copy(moved_ref.at[table_ref[i]], out_ref.at[:, i], sem).start()
        return 0

    lax.fori_loop(0, out_ref.shape[1], send, 0)
    pltpu.make_async_copy(out_ref, out_ref, sem).wait()


def settle(moved, table):
    _, shares, rows, width = moved.shape
    blocks = table.shape[0]
    return pl.pallas_call(
        settle_kernel,
        out_shape=jax.ShapeDtypeStruct((shares, blocks, rows, width), moved.dtype),
        in_specs=[SMEM, ANY],
        out_specs=ANY,
        scratch_shapes=[pltpu.SemaphoreType.DMA],
        cost_estimate=pl.CostEstimate(
            flops=0, bytes_accessed=2 * shares * blocks * rows * width * 2, transcendentals=0
        ),
        name="settle",
    )(table, moved)


def whole_rows(ref):
    shares, blocks, rows, width = ref.shape
    parts = [ref[s].reshape(blocks * rows, width) for s in range(shares)]
    return jnp.concatenate(parts, axis=1)


def gram_kernel(parts, *refs):
    out_ref = refs[parts]
    shares = refs[0].shape[0]
    step = pl.program_id(0)

    @pl.when(step == 0)
    def _():
        out_ref[...] = jnp.zeros_like(out_ref)

    for part in range(parts):
        cells = whole_rows(refs[part])
        at = 0
        for a in range(shares):
            left = cells[:, a * TILE : (a + 1) * TILE]
            product = lax.dot_general(
                left, cells[:, a * TILE :], ROWS_BY_ROWS, preferred_element_type=jnp.float32
            )
            for b in range(a, shares):
                out_ref[at] += product[:, (b - a) * TILE : (b - a + 1) * TILE]
                at += 1


def gram_blocks(cells, steps=4):
    shares, blocks, rows, width = cells[0].shape
    pairs = shares * (shares + 1) // 2
    spec = pl.BlockSpec((shares, blocks // steps, rows, width), lambda i: (0, i, 0, 0))
    return pl.pallas_call(
        lambda *refs: gram_kernel(len(cells), *refs),
        grid=(steps,),
        out_shape=jax.ShapeDtypeStruct((pairs, TILE, TILE), jnp.float32),
        in_specs=[spec] * len(cells),
        out_specs=pl.BlockSpec((pairs, TILE, TILE), lambda i: (0, 0, 0)),
        name="gram_blocks",
    )(*cells)


def cross_kernel(parts, *refs):
    out_ref = refs[2 * parts]
    step = pl.program_id(0)

    @pl.when(step == 0)
    def _():
        out_ref[...] = jnp.zeros_like(out_ref)

    for part in range(parts):
        out_ref[...] += lax.dot_general(
            whole_rows(refs[part]),
            whole_rows(refs[parts + part]),
            ROWS_BY_ROWS,
            preferred_element_type=jnp.float32,
        )


def cross_sum(x_cells, y_cells, steps=4):
    shares, blocks, rows, width = x_cells[0].shape
    spec = pl.BlockSpec((shares, blocks // steps, rows, width), lambda i: (0, i, 0, 0))
    full = shares * width
    return pl.pallas_call(
        lambda *refs: cross_kernel(len(x_cells), *refs),
        grid=(steps,),
        out_shape=jax.ShapeDtypeStruct((full, full), jnp.float32),
        in_specs=[spec] * (2 * len(x_cells)),
        out_specs=pl.BlockSpec((full, full), lambda i: (0, 0)),
        name="cross_sum",
    )(*x_cells, *y_cells)


def three_terms(value):
    high = value.astype(jnp.bfloat16).astype(jnp.float32)
    rest = value - high
    middle = rest.astype(jnp.bfloat16).astype(jnp.float32)
    return high, middle, rest - middle


def lane_of(row, lane):
    return jnp.broadcast_to(row[:, lane : lane + 1], row.shape)


def row_of(ref, row):
    return jnp.broadcast_to(ref[row : row + 1, :], (GROUP, TILE))


def factor_tile(a_ref, w_ref, u_ref, v_ref):
    panels = TILE // GROUP
    a_rows = [row_of(a_ref, i) for i in range(GROUP)]
    w_rows = [row_of(w_ref, i) for i in range(GROUP)]
    for p in range(panels):
        base = p * GROUP
        small = {
            (i, k): lane_of(a_rows[i], base + k) for i in range(GROUP) for k in range(i, GROUP)
        }
        for j in range(GROUP):
            scale = lax.rsqrt(small[j, j])
            a_rows[j] = a_rows[j] * scale
            w_rows[j] = w_rows[j] * scale
            u_ref[base + j : base + j + 1, :] = a_rows[j][:1]
            v_ref[base + j : base + j + 1, :] = w_rows[j][:1]
            below = {k: small[j, k] * scale for k in range(j + 1, GROUP)}
            for k in range(j + 1, GROUP):
                for m in range(k, GROUP):
                    small[k, m] = small[k, m] - below[k] * below[m]
            for k in range(j + 1, GROUP):
                a_rows[k] = a_rows[k] - below[k] * a_rows[j]
                w_rows[k] = w_rows[k] - below[k] * w_rows[j]
        if p + 1 == panels:
            break
        after = base + GROUP
        next_a = [row_of(a_ref, after + i) for i in range(GROUP)]
        next_w = [row_of(w_ref, after + i) for i in range(GROUP)]
        for i in range(GROUP):
            for k in range(GROUP):
                factor = lane_of(a_rows[k], after + i)
                next_a[i] = next_a[i] - factor * a_rows[k]
                next_w[i] = next_w[i] - factor * w_rows[k]
        if p + 2 < panels:
            done = after + GROUP
            u = u_ref[base:after, :]
            v = v_ref[base:after, :]
            uh, um, ul = three_terms(u)
            vh, vm, vl = three_terms(v)
            left = jnp.concatenate([uh, uh, um, uh, ul, um], axis=0).astype(jnp.bfloat16)
            right_a = jnp.concatenate([uh, um, uh, ul, uh, um], axis=0)
            right_w = jnp.concatenate([vh, vm, vh, vl, vh, vm], axis=0)
            right = jnp.concatenate([right_a, right_w], axis=1).astype(jnp.bfloat16)
            update = lax.dot_general(
                left, right, ROWS_BY_ROWS, preferred_element_type=jnp.float32
            )
            a_ref[done:, :] = a_ref[done:, :] - update[done:, :TILE]
            w_ref[done:, :] = w_ref[done:, :] - update[done:, TILE:]
        a_rows, w_rows = next_a, next_w


def factor_kernel(tiles, rows_total, g_ref, r_ref, inv_ref, hi_ref, mid_ref, lo_ref, wide, a_ref, w_ref, u_ref, v_ref):
    row = lax.broadcasted_iota(jnp.int32, (TILE, TILE), 0)
    lane = lax.broadcasted_iota(jnp.int32, (TILE, TILE), 1)
    wide[...] = jnp.zeros_like(wide)
    at = 0
    for a in range(tiles):
        for b in range(a, tiles):
            wide[a, b] = g_ref[at] / rows_total
            at += 1

    def step(b, _):
        a_ref[...] = wide[b, b]
        w_ref[...] = jnp.where(row == lane, 1.0, 0.0)
        factor_tile(a_ref, w_ref, u_ref, v_ref)
        inverse = v_ref[...]
        wide[b, b] = jnp.where(row <= lane, u_ref[...], 0.0)
        wide[b, tiles + b] = inverse
        for j in range(1, tiles):
            wide[b, b + j] = lax.dot(
                inverse, wide[b, b + j], precision=HIGHEST, preferred_element_type=jnp.float32
            )

        def trail(r, _):
            left = wide[b, r]
            for j in range(1, tiles + 1):
                wide[r, b + j] = wide[r, b + j] - lax.dot_general(
                    left,
                    wide[b, b + j],
                    ROWS_BY_ROWS,
                    precision=HIGHEST,
                    preferred_element_type=jnp.float32,
                )
            return 0

        lax.fori_loop(b + 1, tiles, trail, 0)
        return 0

    lax.fori_loop(0, tiles, step, 0)
    zero = jnp.zeros((TILE, TILE), jnp.float32)
    for a in range(tiles):
        rows = slice(a * TILE, (a + 1) * TILE)
        for b in range(tiles):
            lanes = slice(b * TILE, (b + 1) * TILE)
            r_ref[rows, lanes] = wide[a, b] if b >= a else zero
            value = wide[a, tiles + b] if b <= a else zero
            inv_ref[rows, lanes] = value
            high, middle, low = three_terms(value)
            hi_ref[rows, lanes] = high.astype(jnp.bfloat16)
            mid_ref[rows, lanes] = middle.astype(jnp.bfloat16)
            lo_ref[rows, lanes] = low.astype(jnp.bfloat16)


def factor(blocks, tiles, rows_total):
    full = tiles * TILE
    tile = pltpu.VMEM((TILE, TILE), jnp.float32)
    return pl.pallas_call(
        lambda *refs: factor_kernel(tiles, rows_total, *refs),
        out_shape=(
            jax.ShapeDtypeStruct((full, full), jnp.float32),
            jax.ShapeDtypeStruct((full, full), jnp.float32),
            jax.ShapeDtypeStruct((full, full), jnp.bfloat16),
            jax.ShapeDtypeStruct((full, full), jnp.bfloat16),
            jax.ShapeDtypeStruct((full, full), jnp.bfloat16),
        ),
        in_specs=[VMEM],
        out_specs=(VMEM,) * 5,
        scratch_shapes=[
            pltpu.VMEM((tiles, 2 * tiles, TILE, TILE), jnp.float32),
            tile,
            tile,
            tile,
            tile,
        ],
        compiler_params=pltpu.CompilerParams(vmem_limit_bytes=32 * 1024 * 1024),
        cost_estimate=pl.CostEstimate(
            flops=40 * 10**9, bytes_accessed=8 * full * full, transcendentals=full
        ),
        name="factor",
    )(blocks)


def basis_kernel(parts, *refs):
    hi_ref, mid_ref, lo_ref, out_ref = refs[parts:]
    for part in range(parts):
        cells = whole_rows(refs[part])
        total = lax.dot_general(
            cells, lo_ref[...], LANES_BY_LANES, preferred_element_type=jnp.float32
        )
        total += lax.dot_general(
            cells, mid_ref[...], LANES_BY_LANES, preferred_element_type=jnp.float32
        )
        total += lax.dot_general(
            cells, hi_ref[...], LANES_BY_LANES, preferred_element_type=jnp.float32
        )
        blocks, rows = refs[part].shape[1:3]
        out_ref[:, part] = total.reshape(blocks, rows, total.shape[-1])


def basis(cells, terms, steps=8):
    shares, blocks, rows, width = cells[0].shape
    full = shares * width
    parts = len(cells)
    spec = pl.BlockSpec((shares, blocks // steps, rows, width), lambda i: (0, i, 0, 0))
    term = pl.BlockSpec((full, full), lambda i: (0, 0))
    return pl.pallas_call(
        lambda *refs: basis_kernel(parts, *refs),
        grid=(steps,),
        out_shape=jax.ShapeDtypeStruct((blocks, parts, rows, full), jnp.float32),
        in_specs=[spec] * parts + [term] * 3,
        out_specs=pl.BlockSpec((blocks // steps, parts, rows, full), lambda i: (i, 0, 0, 0)),
        compiler_params=pltpu.CompilerParams(vmem_limit_bytes=32 * 1024 * 1024),
        name="basis",
    )(*cells, *terms)


def sum_over_devices(value, slabs, shares):
    lanes = value.shape[-1]
    pieces = lax.all_to_all(value, "space", split_axis=0, concat_axis=0, tiled=True)
    piece = jnp.sum(pieces.reshape(slabs, -1, lanes), axis=0)
    piece = jnp.sum(lax.all_gather(piece, "snap", axis=0), axis=0)
    return lax.all_gather(piece, "space", axis=0, tiled=True)


def body(owned_x, owned_y, patch_dest):
    slabs = lax.axis_size("space")
    shares = lax.axis_size("snap")
    slots, patch, width = owned_x.shape
    capacity = slots // slabs
    per_slab = slots // 2
    parts = patch // shares // CELL_TILE
    rows_total = slabs * per_slab * patch
    full = shares * width

    table, meta = plan(patch_dest, slabs, capacity, per_slab)
    meta = lax.all_to_all(
        meta.reshape(slabs, 1, TILE), "space", split_axis=0, concat_axis=0, tiled=True
    ).reshape(slabs, TILE)
    arrived = arrival(meta, slabs, capacity, per_slab)

    def exchange(owned):
        owned = owned.reshape(slots, shares, parts, CELL_TILE, width)
        cells = []
        for part in range(parts):
            sent = pack(owned, table, part)
            moved = lax.all_to_all(sent, "space", split_axis=0, concat_axis=0, tiled=True)
            settled = settle(moved, arrived)
            cells.append(
                lax.all_to_all(settled, "snap", split_axis=0, concat_axis=0, tiled=True)
            )
        return cells

    x_cells = exchange(owned_x)
    y_cells = exchange(owned_y)

    tiles = full // TILE
    pairs = tiles * (tiles + 1) // 2
    local = gram_blocks(x_cells).reshape(pairs * TILE, TILE)
    total = sum_over_devices(local, slabs, shares).reshape(pairs, TILE, TILE)
    r_factor, inverse, *terms = factor(total, tiles, rows_total)
    q_basis = basis(x_cells, terms).reshape(per_slab, patch // shares, full)

    cross = sum_over_devices(cross_sum(x_cells, y_cells), slabs, shares)
    projection = jnp.dot(inverse, cross, precision=HIGHEST) / math.sqrt(rows_total)
    return q_basis, r_factor, projection


def solution(mesh):
    in_specs = (P("space", None, "snap"), P("space", None, "snap"), P("space"))
    out_specs = (P("space", "snap", None), P(), P())
    return jax.shard_map(body, mesh=mesh, in_specs=in_specs, out_specs=out_specs, check_vma=False)
```

```python
import math

import jax
import jax.numpy as jnp
from jax import lax
from jax.experimental import pallas as pl
from jax.experimental.pallas import tpu as pltpu
from jax.sharding import PartitionSpec as P

TILE = 128
GROUP = 8
CELL_TILE = 16
VMEM_BYTES = 32 * 1024 * 1024
HIGHEST = lax.Precision.HIGHEST
SMEM = pl.BlockSpec(memory_space=pltpu.SMEM)
VMEM = pl.BlockSpec(memory_space=pltpu.VMEM)
ANY = pl.BlockSpec(memory_space=pl.ANY)
ROWS_BY_ROWS = (((0,), (0,)), ((), ()))
LANES_BY_LANES = (((1,), (1,)), ((), ()))


def pack_kernel(slabs, capacity, per_slab, parts, dest_ref, owned_ref, *refs):
    out_refs, meta_ref, count_ref = refs[:parts], refs[parts], refs[parts + 1]
    for slab in range(slabs):
        count_ref[slab] = 0

    def place(i, _):
        block = dest_ref[i]

        @pl.when(block >= 0)
        def _():
            slab = lax.div(block, per_slab)
            rank = count_ref[slab]
            count_ref[slab] = rank + 1
            meta_ref[slab, rank] = block - slab * per_slab
            at = slab * capacity + rank
            for part in range(parts):
                out_refs[part][at] = owned_ref[i, :, part]

        return 0

    lax.fori_loop(0, dest_ref.shape[0], place, 0, unroll=4)
    for slab in range(slabs):
        meta_ref[slab, capacity] = count_ref[slab]


def pack(dest, owned, slabs, per_slab):
    slots, shares, parts, rows, width = owned.shape
    sent = jax.ShapeDtypeStruct((slots, shares, rows, width), owned.dtype)
    outs = pl.pallas_call(
        lambda *refs: pack_kernel(slabs, slots // slabs, per_slab, parts, *refs),
        out_shape=(sent,) * parts + (jax.ShapeDtypeStruct((slabs, TILE), jnp.int32),),
        in_specs=[SMEM, VMEM],
        out_specs=(VMEM,) * parts + (SMEM,),
        scratch_shapes=[pltpu.SMEM((slabs,), jnp.int32)],
        compiler_params=pltpu.CompilerParams(vmem_limit_bytes=VMEM_BYTES),
        cost_estimate=pl.CostEstimate(
            flops=0, bytes_accessed=2 * owned.size * 2, transcendentals=0
        ),
        name="pack",
    )(dest, owned)
    return outs[:parts], outs[parts]


def settle_kernel(slabs, capacity, meta_ref, moved_ref, out_ref):
    for source in range(slabs):

        def place(rank, _):
            out_ref[:, meta_ref[source, rank]] = moved_ref[source * capacity + rank]
            return 0

        lax.fori_loop(0, meta_ref[source, capacity], place, 0)


def settle(meta, moved, slabs, per_slab):
    slots, shares, rows, width = moved.shape
    return pl.pallas_call(
        lambda *refs: settle_kernel(slabs, slots // slabs, *refs),
        out_shape=jax.ShapeDtypeStruct((shares, per_slab, rows, width), moved.dtype),
        in_specs=[SMEM, VMEM],
        out_specs=VMEM,
        compiler_params=pltpu.CompilerParams(vmem_limit_bytes=VMEM_BYTES),
        cost_estimate=pl.CostEstimate(
            flops=0, bytes_accessed=2 * moved.size, transcendentals=0
        ),
        name="settle",
    )(meta, moved)


def whole_rows(ref):
    shares, blocks, rows, width = ref.shape
    parts = [ref[s].reshape(blocks * rows, width) for s in range(shares)]
    return jnp.concatenate(parts, axis=1)


def gram_kernel(parts, *refs):
    out_ref = refs[parts]
    shares = refs[0].shape[0]
    step = pl.program_id(0)

    @pl.when(step == 0)
    def _():
        out_ref[...] = jnp.zeros_like(out_ref)

    for part in range(parts):
        cells = whole_rows(refs[part])
        at = 0
        for a in range(shares):
            left = cells[:, a * TILE : (a + 1) * TILE]
            product = lax.dot_general(
                left, cells[:, a * TILE :], ROWS_BY_ROWS, preferred_element_type=jnp.float32
            )
            for b in range(a, shares):
                out_ref[at] += product[:, (b - a) * TILE : (b - a + 1) * TILE]
                at += 1


def gram_blocks(cells, steps=4):
    shares, blocks, rows, width = cells[0].shape
    pairs = shares * (shares + 1) // 2
    spec = pl.BlockSpec((shares, blocks // steps, rows, width), lambda i: (0, i, 0, 0))
    return pl.pallas_call(
        lambda *refs: gram_kernel(len(cells), *refs),
        grid=(steps,),
        out_shape=jax.ShapeDtypeStruct((pairs, TILE, TILE), jnp.float32),
        in_specs=[spec] * len(cells),
        out_specs=pl.BlockSpec((pairs, TILE, TILE), lambda i: (0, 0, 0)),
        name="gram_blocks",
    )(*cells)


def cross_kernel(parts, *refs):
    out_ref = refs[2 * parts]
    step = pl.program_id(0)

    @pl.when(step == 0)
    def _():
        out_ref[...] = jnp.zeros_like(out_ref)

    for part in range(parts):
        out_ref[...] += lax.dot_general(
            whole_rows(refs[part]),
            whole_rows(refs[parts + part]),
            ROWS_BY_ROWS,
            preferred_element_type=jnp.float32,
        )


def cross_sum(x_cells, y_cells, steps=4):
    shares, blocks, rows, width = x_cells[0].shape
    spec = pl.BlockSpec((shares, blocks // steps, rows, width), lambda i: (0, i, 0, 0))
    full = shares * width
    return pl.pallas_call(
        lambda *refs: cross_kernel(len(x_cells), *refs),
        grid=(steps,),
        out_shape=jax.ShapeDtypeStruct((full, full), jnp.float32),
        in_specs=[spec] * (2 * len(x_cells)),
        out_specs=pl.BlockSpec((full, full), lambda i: (0, 0)),
        name="cross_sum",
    )(*x_cells, *y_cells)


def three_terms(value):
    high = value.astype(jnp.bfloat16).astype(jnp.float32)
    rest = value - high
    middle = rest.astype(jnp.bfloat16).astype(jnp.float32)
    return high, middle, rest - middle


def lane_of(row, lane):
    return jnp.broadcast_to(row[:, lane : lane + 1], row.shape)


def row_of(ref, row):
    return jnp.broadcast_to(ref[row : row + 1, :], (GROUP, TILE))


def factor_tile(a_ref, w_ref, u_ref, v_ref):
    panels = TILE // GROUP
    a_rows = [row_of(a_ref, i) for i in range(GROUP)]
    w_rows = [row_of(w_ref, i) for i in range(GROUP)]
    for p in range(panels):
        base = p * GROUP
        small = {
            (i, k): lane_of(a_rows[i], base + k) for i in range(GROUP) for k in range(i, GROUP)
        }
        for j in range(GROUP):
            scale = lax.rsqrt(small[j, j])
            a_rows[j] = a_rows[j] * scale
            w_rows[j] = w_rows[j] * scale
            u_ref[base + j : base + j + 1, :] = a_rows[j][:1]
            v_ref[base + j : base + j + 1, :] = w_rows[j][:1]
            below = {k: small[j, k] * scale for k in range(j + 1, GROUP)}
            for k in range(j + 1, GROUP):
                for m in range(k, GROUP):
                    small[k, m] = small[k, m] - below[k] * below[m]
            for k in range(j + 1, GROUP):
                a_rows[k] = a_rows[k] - below[k] * a_rows[j]
                w_rows[k] = w_rows[k] - below[k] * w_rows[j]
        if p + 1 == panels:
            break
        after = base + GROUP
        next_a = [row_of(a_ref, after + i) for i in range(GROUP)]
        next_w = [row_of(w_ref, after + i) for i in range(GROUP)]
        for i in range(GROUP):
            for k in range(GROUP):
                factor = lane_of(a_rows[k], after + i)
                next_a[i] = next_a[i] - factor * a_rows[k]
                next_w[i] = next_w[i] - factor * w_rows[k]
        if p + 2 < panels:
            done = after + GROUP
            u = u_ref[base:after, :]
            v = v_ref[base:after, :]
            uh, um, ul = three_terms(u)
            vh, vm, vl = three_terms(v)
            left = jnp.concatenate([uh, uh, um, uh, ul, um], axis=0).astype(jnp.bfloat16)
            right_a = jnp.concatenate([uh, um, uh, ul, uh, um], axis=0)
            right_w = jnp.concatenate([vh, vm, vh, vl, vh, vm], axis=0)
            right = jnp.concatenate([right_a, right_w], axis=1).astype(jnp.bfloat16)
            update = lax.dot_general(
                left, right, ROWS_BY_ROWS, preferred_element_type=jnp.float32
            )
            a_ref[done:, :] = a_ref[done:, :] - update[done:, :TILE]
            w_ref[done:, :] = w_ref[done:, :] - update[done:, TILE:]
        a_rows, w_rows = next_a, next_w


def factor_kernel(tiles, rows_total, g_ref, r_ref, inv_ref, hi_ref, mid_ref, lo_ref, wide, a_ref, w_ref, u_ref, v_ref):
    row = lax.broadcasted_iota(jnp.int32, (TILE, TILE), 0)
    lane = lax.broadcasted_iota(jnp.int32, (TILE, TILE), 1)
    wide[...] = jnp.zeros_like(wide)
    at = 0
    for a in range(tiles):
        for b in range(a, tiles):
            wide[a, b] = g_ref[at] / rows_total
            at += 1

    def step(b, _):
        a_ref[...] = wide[b, b]
        w_ref[...] = jnp.where(row == lane, 1.0, 0.0)
        factor_tile(a_ref, w_ref, u_ref, v_ref)
        inverse = v_ref[...]
        wide[b, b] = jnp.where(row <= lane, u_ref[...], 0.0)
        wide[b, tiles + b] = inverse
        for j in range(1, tiles):
            wide[b, b + j] = lax.dot(
                inverse, wide[b, b + j], precision=HIGHEST, preferred_element_type=jnp.float32
            )

        def trail(r, _):
            left = wide[b, r]
            for j in range(1, tiles + 1):
                wide[r, b + j] = wide[r, b + j] - lax.dot_general(
                    left,
                    wide[b, b + j],
                    ROWS_BY_ROWS,
                    precision=HIGHEST,
                    preferred_element_type=jnp.float32,
                )
            return 0

        lax.fori_loop(b + 1, tiles, trail, 0)
        return 0

    lax.fori_loop(0, tiles, step, 0)
    zero = jnp.zeros((TILE, TILE), jnp.float32)
    for a in range(tiles):
        rows = slice(a * TILE, (a + 1) * TILE)
        for b in range(tiles):
            lanes = slice(b * TILE, (b + 1) * TILE)
            r_ref[rows, lanes] = wide[a, b] if b >= a else zero
            value = wide[a, tiles + b] if b <= a else zero
            inv_ref[rows, lanes] = value
            high, middle, low = three_terms(value)
            hi_ref[rows, lanes] = high.astype(jnp.bfloat16)
            mid_ref[rows, lanes] = middle.astype(jnp.bfloat16)
            lo_ref[rows, lanes] = low.astype(jnp.bfloat16)


def factor(blocks, tiles, rows_total):
    full = tiles * TILE
    tile = pltpu.VMEM((TILE, TILE), jnp.float32)
    return pl.pallas_call(
        lambda *refs: factor_kernel(tiles, rows_total, *refs),
        out_shape=(
            jax.ShapeDtypeStruct((full, full), jnp.float32),
            jax.ShapeDtypeStruct((full, full), jnp.float32),
            jax.ShapeDtypeStruct((full, full), jnp.bfloat16),
            jax.ShapeDtypeStruct((full, full), jnp.bfloat16),
            jax.ShapeDtypeStruct((full, full), jnp.bfloat16),
        ),
        in_specs=[VMEM],
        out_specs=(VMEM,) * 5,
        scratch_shapes=[
            pltpu.VMEM((tiles, 2 * tiles, TILE, TILE), jnp.float32),
            tile,
            tile,
            tile,
            tile,
        ],
        compiler_params=pltpu.CompilerParams(vmem_limit_bytes=VMEM_BYTES),
        cost_estimate=pl.CostEstimate(
            flops=40 * 10**9, bytes_accessed=8 * full * full, transcendentals=full
        ),
        name="factor",
    )(blocks)


def basis_kernel(parts, *refs):
    hi_ref, mid_ref, lo_ref, out_ref = refs[parts:]
    for part in range(parts):
        cells = whole_rows(refs[part])
        total = lax.dot_general(
            cells, lo_ref[...], LANES_BY_LANES, preferred_element_type=jnp.float32
        )
        total += lax.dot_general(
            cells, mid_ref[...], LANES_BY_LANES, preferred_element_type=jnp.float32
        )
        total += lax.dot_general(
            cells, hi_ref[...], LANES_BY_LANES, preferred_element_type=jnp.float32
        )
        blocks, rows = refs[part].shape[1:3]
        out_ref[:, part] = total.reshape(blocks, rows, total.shape[-1])


def basis(cells, terms, steps=8):
    shares, blocks, rows, width = cells[0].shape
    full = shares * width
    parts = len(cells)
    spec = pl.BlockSpec((shares, blocks // steps, rows, width), lambda i: (0, i, 0, 0))
    term = pl.BlockSpec((full, full), lambda i: (0, 0))
    return pl.pallas_call(
        lambda *refs: basis_kernel(parts, *refs),
        grid=(steps,),
        out_shape=jax.ShapeDtypeStruct((blocks, parts, rows, full), jnp.float32),
        in_specs=[spec] * parts + [term] * 3,
        out_specs=pl.BlockSpec((blocks // steps, parts, rows, full), lambda i: (i, 0, 0, 0)),
        compiler_params=pltpu.CompilerParams(vmem_limit_bytes=VMEM_BYTES),
        name="basis",
    )(*cells, *terms)


def sum_over_devices(value, slabs, shares):
    lanes = value.shape[-1]
    pieces = lax.all_to_all(value, "space", split_axis=0, concat_axis=0, tiled=True)
    piece = jnp.sum(pieces.reshape(slabs, -1, lanes), axis=0)
    hop = 1
    while hop < shares:
        piece += lax.ppermute(piece, "snap", [(i, i ^ hop) for i in range(shares)])
        hop *= 2
    return lax.all_gather(piece, "space", axis=0, tiled=True)


def body(owned_x, owned_y, patch_dest):
    slabs = lax.axis_size("space")
    shares = lax.axis_size("snap")
    slots, patch, width = owned_x.shape
    per_slab = slots // 2
    parts = patch // shares // CELL_TILE
    rows_total = slabs * per_slab * patch
    full = shares * width

    def parted(owned):
        return owned.reshape(slots, shares, parts, CELL_TILE, width)

    def exchange(sent, meta):
        cells = []
        for part in sent:
            moved = lax.all_to_all(part, "space", split_axis=0, concat_axis=0, tiled=True)
            settled = settle(meta, moved, slabs, per_slab)
            cells.append(lax.all_to_all(settled, "snap", split_axis=0, concat_axis=0, tiled=True))
        return cells

    sent_x, meta = pack(patch_dest, parted(owned_x), slabs, per_slab)
    meta = lax.all_to_all(
        meta.reshape(slabs, 1, TILE), "space", split_axis=0, concat_axis=0, tiled=True
    ).reshape(slabs, TILE)
    sent_y, _ = pack(patch_dest, parted(owned_y), slabs, per_slab)
    x_cells = exchange(sent_x, meta)
    y_cells = exchange(sent_y, meta)

    tiles = full // TILE
    pairs = tiles * (tiles + 1) // 2
    local = gram_blocks(x_cells).reshape(pairs * TILE, TILE)
    total = sum_over_devices(local, slabs, shares).reshape(pairs, TILE, TILE)
    r_factor, inverse, *terms = factor(total, tiles, rows_total)
    q_basis = basis(x_cells, terms).reshape(per_slab, patch // shares, full)

    cross = sum_over_devices(cross_sum(x_cells, y_cells), slabs, shares)
    projection = jnp.dot(inverse, cross, precision=HIGHEST) / math.sqrt(rows_total)
    return q_basis, r_factor, projection


def solution(mesh):
    in_specs = (P("space", None, "snap"), P("space", None, "snap"), P("space"))
    out_specs = (P("space", "snap", None), P(), P())
    return jax.shard_map(body, mesh=mesh, in_specs=in_specs, out_specs=out_specs, check_vma=False)
```

```python
import math

import jax
import jax.numpy as jnp
from jax import lax
from jax.experimental import pallas as pl
from jax.experimental.pallas import tpu as pltpu
from jax.sharding import PartitionSpec as P

TILE = 128
GROUP = 8
CELL_TILE = 16
VMEM_BYTES = 32 * 1024 * 1024
HIGHEST = lax.Precision.HIGHEST
SMEM = pl.BlockSpec(memory_space=pltpu.SMEM)
VMEM = pl.BlockSpec(memory_space=pltpu.VMEM)
ANY = pl.BlockSpec(memory_space=pl.ANY)
ROWS_BY_ROWS = (((0,), (0,)), ((), ()))
LANES_BY_LANES = (((1,), (1,)), ((), ()))


def pack_kernel(slabs, capacity, per_slab, parts, dest_ref, owned_ref, *refs):
    out_refs, (buf_ref, ids_ref, count_ref) = refs[:-3], refs[-3:]
    shares = owned_ref.shape[1]
    span = capacity * shares
    me = lax.axis_index("space")
    lane = lax.broadcasted_iota(jnp.int32, (1, TILE), 1)
    ids_ref[...] = jnp.full_like(ids_ref, -1)
    for slab in range(slabs):
        count_ref[slab] = 0

    def place(i, _):
        block = dest_ref[i]

        @pl.when(block >= 0)
        def _():
            slab = lax.div(block, per_slab)
            rank = count_ref[slab]
            count_ref[slab] = rank + 1
            here = pl.ds(slab, 1)
            ids_ref[here, :] = jnp.where(lane == rank, block - slab * per_slab, ids_ref[here, :])
            at = slab * span + rank * shares
            for part in range(parts):
                buf_ref[part, pl.ds(at, shares)] = owned_ref[i, :, part]

        return 0

    lax.fori_loop(0, dest_ref.shape[0], place, 0, unroll=4)
    for part in range(parts):
        for m in range(slabs):
            out_ref = out_refs[part * slabs + m]
            slab = me ^ m
            out_ref[:span] = buf_ref[part, pl.ds(slab * span, span)]
            if out_ref.shape[0] > span:
                ids = ids_ref[pl.ds(slab, 1), :].astype(jnp.float32)
                out_ref[span] = jnp.broadcast_to(ids, out_ref.shape[1:]).astype(out_ref.dtype)


def pack(dest, owned, slabs, per_slab, after=None):
    slots, shares, parts, rows, width = owned.shape
    capacity = slots // slabs
    span = capacity * shares
    first = 0 if after is None else 1
    sent = []
    for part in range(parts):
        extra = 1 if after is None and part == 0 else 0
        sent += [jax.ShapeDtypeStruct((span + extra, rows, width), owned.dtype)] * slabs
    outs = pl.pallas_call(
        lambda *refs: pack_kernel(slabs, capacity, per_slab, parts, *refs[first:]),
        out_shape=tuple(sent),
        in_specs=[SMEM] * first + [SMEM, VMEM],
        out_specs=(VMEM,) * len(sent),
        scratch_shapes=[
            pltpu.VMEM((parts, slots * shares, rows, width), owned.dtype),
            pltpu.VMEM((slabs, TILE), jnp.int32),
            pltpu.SMEM((slabs,), jnp.int32),
        ],
        compiler_params=pltpu.CompilerParams(vmem_limit_bytes=VMEM_BYTES),
        cost_estimate=pl.CostEstimate(
            flops=0, bytes_accessed=2 * owned.size * 2, transcendentals=0
        ),
        name="pack",
    )(*([] if after is None else [after]), dest, owned)
    return [outs[part * slabs : (part + 1) * slabs] for part in range(parts)]


def settle_kernel(slabs, capacity, first, *refs):
    if first:
        moved_refs, out_refs, (ids_ref, meta_ref) = refs[:slabs], refs[slabs:-2], refs[-2:]
        meta_ref, ids_ref = ids_ref, meta_ref
        span = moved_refs[0].shape[0] - 1
        for m in range(slabs):
            tile = moved_refs[m][span].astype(jnp.float32)
            ids_ref[m : m + 1, :] = tile[:1].astype(jnp.int32)
        pltpu.sync_copy(ids_ref, meta_ref)
    else:
        meta_ref, moved_refs, out_refs = refs[0], refs[1 : 1 + slabs], refs[1 + slabs :]
    shares = len(out_refs)
    mine = lax.axis_index("snap")
    for m in range(slabs):

        def place(rank, _):
            block = meta_ref[m, rank]

            @pl.when(block >= 0)
            def _():
                for r in range(shares):
                    out_refs[r][block] = moved_refs[m][rank * shares + (mine ^ r)]

            return 0

        lax.fori_loop(0, capacity, place, 0, unroll=4)


def settle(meta, moved, capacity, per_slab, shares):
    first = meta is None
    slabs = len(moved)
    rows, width = moved[0].shape[1:]
    pieces = (jax.ShapeDtypeStruct((per_slab, rows, width), moved[0].dtype),) * shares
    ids = jax.ShapeDtypeStruct((slabs, TILE), jnp.int32)
    outs = pl.pallas_call(
        lambda *refs: settle_kernel(slabs, capacity, first, *refs),
        out_shape=pieces + ((ids,) if first else ()),
        in_specs=([] if first else [SMEM]) + [VMEM] * slabs,
        out_specs=(VMEM,) * shares + ((SMEM,) if first else ()),
        scratch_shapes=[pltpu.VMEM((slabs, TILE), jnp.int32)] if first else [],
        compiler_params=pltpu.CompilerParams(vmem_limit_bytes=VMEM_BYTES),
        cost_estimate=pl.CostEstimate(
            flops=0, bytes_accessed=2 * slabs * moved[0].size, transcendentals=0
        ),
        name="settle",
    )(*([] if first else [meta]), *moved)
    return outs[:shares], (outs[shares] if first else meta)


def whole_rows(refs):
    blocks, rows, width = refs[0].shape
    return jnp.concatenate([ref[...].reshape(blocks * rows, width) for ref in refs], axis=1)


def tile_of(row, lane, tiles):
    return row * tiles - lax.div(row * (row - 1), 2) + lane - row


def gram_kernel(parts, shares, *refs):
    out_ref, acc_ref = refs[-2:]
    step = pl.program_id(0)

    @pl.when(step == 0)
    def _():
        acc_ref[...] = jnp.zeros_like(acc_ref)

    for part in range(parts):
        cells = whole_rows(refs[part * shares : (part + 1) * shares])
        acc_ref[...] += lax.dot_general(
            cells, cells, ROWS_BY_ROWS, preferred_element_type=jnp.float32
        )

    @pl.when(step == pl.num_programs(0) - 1)
    def _():
        mine = lax.axis_index("snap")
        for a in range(shares):
            for b in range(shares):
                row, lane = mine ^ a, mine ^ b

                @pl.when(row <= lane)
                def _():
                    out_ref[tile_of(row, lane, shares)] = acc_ref[
                        a * TILE : (a + 1) * TILE, b * TILE : (b + 1) * TILE
                    ]


def gram_blocks(cells, steps=4):
    shares = len(cells[0])
    blocks, rows, width = cells[0][0].shape
    pairs = shares * (shares + 1) // 2
    full = shares * width
    spec = pl.BlockSpec((blocks // steps, rows, width), lambda i: (i, 0, 0))
    return pl.pallas_call(
        lambda *refs: gram_kernel(len(cells), shares, *refs),
        grid=(steps,),
        out_shape=jax.ShapeDtypeStruct((pairs, TILE, TILE), jnp.float32),
        in_specs=[spec] * (len(cells) * shares),
        out_specs=pl.BlockSpec((pairs, TILE, TILE), lambda i: (0, 0, 0)),
        scratch_shapes=[pltpu.VMEM((full, full), jnp.float32)],
        compiler_params=pltpu.CompilerParams(vmem_limit_bytes=VMEM_BYTES),
        cost_estimate=pl.CostEstimate(
            flops=2 * len(cells) * blocks * rows * full * full,
            bytes_accessed=2 * len(cells) * blocks * rows * full,
            transcendentals=0,
        ),
        name="gram_blocks",
    )(*[piece for part in cells for piece in part])


def cross_kernel(parts, shares, *refs):
    out_ref, acc_ref = refs[-2:]
    step = pl.program_id(0)

    @pl.when(step == 0)
    def _():
        acc_ref[...] = jnp.zeros_like(acc_ref)

    for part in range(parts):
        x_refs = refs[part * shares : (part + 1) * shares]
        y_refs = refs[(parts + part) * shares : (parts + part + 1) * shares]
        acc_ref[...] += lax.dot_general(
            whole_rows(x_refs), whole_rows(y_refs), ROWS_BY_ROWS, preferred_element_type=jnp.float32
        )

    @pl.when(step == pl.num_programs(0) - 1)
    def _():
        mine = lax.axis_index("snap")
        for a in range(shares):
            rows = pl.ds(pl.multiple_of((mine ^ a) * TILE, TILE), TILE)
            for b in range(shares):
                lanes = pl.ds(pl.multiple_of((mine ^ b) * TILE, TILE), TILE)
                out_ref[rows, lanes] = acc_ref[
                    a * TILE : (a + 1) * TILE, b * TILE : (b + 1) * TILE
                ]


def cross_sum(x_cells, y_cells, steps=4):
    parts, shares = len(x_cells), len(x_cells[0])
    blocks, rows, width = x_cells[0][0].shape
    spec = pl.BlockSpec((blocks // steps, rows, width), lambda i: (i, 0, 0))
    full = shares * width
    return pl.pallas_call(
        lambda *refs: cross_kernel(parts, shares, *refs),
        grid=(steps,),
        out_shape=jax.ShapeDtypeStruct((full, full), jnp.float32),
        in_specs=[spec] * (2 * parts * shares),
        out_specs=pl.BlockSpec((full, full), lambda i: (0, 0)),
        scratch_shapes=[pltpu.VMEM((full, full), jnp.float32)],
        compiler_params=pltpu.CompilerParams(vmem_limit_bytes=VMEM_BYTES),
        cost_estimate=pl.CostEstimate(
            flops=2 * parts * blocks * rows * full * full,
            bytes_accessed=4 * parts * blocks * rows * full,
            transcendentals=0,
        ),
        name="cross_sum",
    )(*[piece for part in list(x_cells) + list(y_cells) for piece in part])


def three_terms(value):
    high = value.astype(jnp.bfloat16).astype(jnp.float32)
    rest = value - high
    middle = rest.astype(jnp.bfloat16).astype(jnp.float32)
    return high, middle, rest - middle


def lane_of(row, lane):
    return jnp.broadcast_to(row[:, lane : lane + 1], row.shape)


def row_of(ref, row):
    return jnp.broadcast_to(ref[row : row + 1, :], (GROUP, TILE))


def factor_tile(a_ref, w_ref, u_ref, v_ref):
    panels = TILE // GROUP
    a_rows = [row_of(a_ref, i) for i in range(GROUP)]
    w_rows = [row_of(w_ref, i) for i in range(GROUP)]
    for p in range(panels):
        base = p * GROUP
        small = {
            (i, k): lane_of(a_rows[i], base + k) for i in range(GROUP) for k in range(i, GROUP)
        }
        for j in range(GROUP):
            scale = lax.rsqrt(small[j, j])
            a_rows[j] = a_rows[j] * scale
            w_rows[j] = w_rows[j] * scale
            u_ref[base + j : base + j + 1, :] = a_rows[j][:1]
            v_ref[base + j : base + j + 1, :] = w_rows[j][:1]
            below = {k: small[j, k] * scale for k in range(j + 1, GROUP)}
            for k in range(j + 1, GROUP):
                for m in range(k, GROUP):
                    small[k, m] = small[k, m] - below[k] * below[m]
            for k in range(j + 1, GROUP):
                a_rows[k] = a_rows[k] - below[k] * a_rows[j]
                w_rows[k] = w_rows[k] - below[k] * w_rows[j]
        if p + 1 == panels:
            break
        after = base + GROUP
        next_a = [row_of(a_ref, after + i) for i in range(GROUP)]
        next_w = [row_of(w_ref, after + i) for i in range(GROUP)]
        for i in range(GROUP):
            for k in range(GROUP):
                factor = lane_of(a_rows[k], after + i)
                next_a[i] = next_a[i] - factor * a_rows[k]
                next_w[i] = next_w[i] - factor * w_rows[k]
        if p + 2 < panels:
            done = after + GROUP
            u = u_ref[base:after, :]
            v = v_ref[base:after, :]
            uh, um, ul = three_terms(u)
            vh, vm, vl = three_terms(v)
            left = jnp.concatenate([uh, uh, um, uh, ul, um], axis=0).astype(jnp.bfloat16)
            right_a = jnp.concatenate([uh, um, uh, ul, uh, um], axis=0)
            right_w = jnp.concatenate([vh, vm, vh, vl, vh, vm], axis=0)
            right = jnp.concatenate([right_a, right_w], axis=1).astype(jnp.bfloat16)
            update = lax.dot_general(
                left, right, ROWS_BY_ROWS, preferred_element_type=jnp.float32
            )
            a_ref[done:, :] = a_ref[done:, :] - update[done:, :TILE]
            w_ref[done:, :] = w_ref[done:, :] - update[done:, TILE:]
        a_rows, w_rows = next_a, next_w


def factor_kernel(tiles, rows_total, g_ref, r_ref, inv_ref, hi_ref, mid_ref, lo_ref, wide, a_ref, w_ref, u_ref, v_ref):
    row = lax.broadcasted_iota(jnp.int32, (TILE, TILE), 0)
    lane = lax.broadcasted_iota(jnp.int32, (TILE, TILE), 1)
    wide[...] = jnp.zeros_like(wide)
    at = 0
    for a in range(tiles):
        for b in range(a, tiles):
            wide[a, b] = g_ref[at] / rows_total
            at += 1

    def step(b, _):
        a_ref[...] = wide[b, b]
        w_ref[...] = jnp.where(row == lane, 1.0, 0.0)
        factor_tile(a_ref, w_ref, u_ref, v_ref)
        inverse = v_ref[...]
        wide[b, b] = jnp.where(row <= lane, u_ref[...], 0.0)
        wide[b, tiles + b] = inverse
        for j in range(1, tiles):
            wide[b, b + j] = lax.dot(
                inverse, wide[b, b + j], precision=HIGHEST, preferred_element_type=jnp.float32
            )

        def trail(r, _):
            left = wide[b, r]
            for j in range(1, tiles + 1):
                wide[r, b + j] = wide[r, b + j] - lax.dot_general(
                    left,
                    wide[b, b + j],
                    ROWS_BY_ROWS,
                    precision=HIGHEST,
                    preferred_element_type=jnp.float32,
                )
            return 0

        lax.fori_loop(b + 1, tiles, trail, 0)
        return 0

    lax.fori_loop(0, tiles, step, 0)
    zero = jnp.zeros((TILE, TILE), jnp.float32)
    mine = lax.axis_index("snap")
    for a in range(tiles):
        rows = slice(a * TILE, (a + 1) * TILE)
        for b in range(tiles):
            lanes = slice(b * TILE, (b + 1) * TILE)
            r_ref[rows, lanes] = wide[a, b] if b >= a else zero
            value = wide[a, tiles + b] if b <= a else zero
            inv_ref[rows, lanes] = value
            high, middle, low = three_terms(value)
            lanes = pl.ds(pl.multiple_of((mine ^ b) * TILE, TILE), TILE)
            hi_ref[rows, lanes] = high.astype(jnp.bfloat16)
            mid_ref[rows, lanes] = middle.astype(jnp.bfloat16)
            lo_ref[rows, lanes] = low.astype(jnp.bfloat16)


def factor(blocks, tiles, rows_total):
    full = tiles * TILE
    tile = pltpu.VMEM((TILE, TILE), jnp.float32)
    return pl.pallas_call(
        lambda *refs: factor_kernel(tiles, rows_total, *refs),
        out_shape=(
            jax.ShapeDtypeStruct((full, full), jnp.float32),
            jax.ShapeDtypeStruct((full, full), jnp.float32),
            jax.ShapeDtypeStruct((full, full), jnp.bfloat16),
            jax.ShapeDtypeStruct((full, full), jnp.bfloat16),
            jax.ShapeDtypeStruct((full, full), jnp.bfloat16),
        ),
        in_specs=[VMEM],
        out_specs=(VMEM,) * 5,
        scratch_shapes=[
            pltpu.VMEM((tiles, 2 * tiles, TILE, TILE), jnp.float32),
            tile,
            tile,
            tile,
            tile,
        ],
        compiler_params=pltpu.CompilerParams(vmem_limit_bytes=VMEM_BYTES),
        cost_estimate=pl.CostEstimate(
            flops=40 * 10**9, bytes_accessed=8 * full * full, transcendentals=full
        ),
        name="factor",
    )(blocks)


def basis_kernel(parts, shares, *refs):
    hi_ref, mid_ref, lo_ref, out_ref = refs[parts * shares :]
    for part in range(parts):
        cells = whole_rows(refs[part * shares : (part + 1) * shares])
        total = lax.dot_general(
            cells, lo_ref[...], LANES_BY_LANES, preferred_element_type=jnp.float32
        )
        total += lax.dot_general(
            cells, mid_ref[...], LANES_BY_LANES, preferred_element_type=jnp.float32
        )
        total += lax.dot_general(
            cells, hi_ref[...], LANES_BY_LANES, preferred_element_type=jnp.float32
        )
        blocks, _, rows, full = out_ref.shape
        out_ref[:, part] = total.reshape(blocks, rows, full)


def basis(cells, terms, steps=8):
    parts, shares = len(cells), len(cells[0])
    blocks, rows, width = cells[0][0].shape
    full = shares * width
    spec = pl.BlockSpec((blocks // steps, rows, width), lambda i: (i, 0, 0))
    term = pl.BlockSpec((full, full), lambda i: (0, 0))
    return pl.pallas_call(
        lambda *refs: basis_kernel(parts, shares, *refs),
        grid=(steps,),
        out_shape=jax.ShapeDtypeStruct((blocks, parts, rows, full), jnp.float32),
        in_specs=[spec] * (parts * shares) + [term] * 3,
        out_specs=pl.BlockSpec((blocks // steps, parts, rows, full), lambda i: (i, 0, 0, 0)),
        compiler_params=pltpu.CompilerParams(vmem_limit_bytes=VMEM_BYTES),
        cost_estimate=pl.CostEstimate(
            flops=6 * parts * blocks * rows * full * full,
            bytes_accessed=6 * parts * blocks * rows * full,
            transcendentals=0,
        ),
        name="basis",
    )(*[piece for part in cells for piece in part], *terms)


def swap(value, axis, mask):
    return lax.ppermute(value, axis, [(i, i ^ mask) for i in range(lax.axis_size(axis))])


def sum_over_devices(value, slabs, shares):
    lanes = value.shape[-1]
    pieces = lax.all_to_all(value, "space", split_axis=0, concat_axis=0, tiled=True)
    piece = jnp.sum(pieces.reshape(slabs, -1, lanes), axis=0)
    hop = 1
    while hop < shares:
        piece += swap(piece, "snap", hop)
        hop *= 2
    return lax.all_gather(piece, "space", axis=0, tiled=True)


def body(owned_x, owned_y, patch_dest):
    slabs = lax.axis_size("space")
    shares = lax.axis_size("snap")
    slots, patch, width = owned_x.shape
    per_slab = slots // 2
    parts = patch // shares // CELL_TILE
    rows_total = slabs * per_slab * patch
    full = shares * width

    def parted(owned):
        return owned.reshape(slots, shares, parts, CELL_TILE, width)

    def exchange(sent, meta):
        cells = []
        for part in sent:
            moved = [part[0]] + [swap(part[m], "space", m) for m in range(1, slabs)]
            pieces, meta = settle(meta, moved, slots // slabs, per_slab, shares)
            cells.append([pieces[0]] + [swap(pieces[r], "snap", r) for r in range(1, shares)])
        return cells, meta

    sent_x = pack(patch_dest, parted(owned_x), slabs, per_slab)
    x_cells, meta = exchange(sent_x, None)
    sent_y = pack(patch_dest, parted(owned_y), slabs, per_slab, meta)
    y_cells, _ = exchange(sent_y, meta)

    tiles = full // TILE
    pairs = tiles * (tiles + 1) // 2
    local = gram_blocks(x_cells).reshape(pairs * TILE, TILE)
    total = sum_over_devices(local, slabs, shares).reshape(pairs, TILE, TILE)
    r_factor, inverse, *terms = factor(total, tiles, rows_total)
    q_basis = basis(x_cells, terms).reshape(per_slab, patch // shares, full)

    cross = sum_over_devices(cross_sum(x_cells, y_cells), slabs, shares)
    projection = jnp.dot(inverse, cross, precision=HIGHEST) / math.sqrt(rows_total)
    return q_basis, r_factor, projection


def solution(mesh):
    in_specs = (P("space", None, "snap"), P("space", None, "snap"), P("space"))
    out_specs = (P("space", "snap", None), P(), P())
    return jax.shard_map(body, mesh=mesh, in_specs=in_specs, out_specs=out_specs, check_vma=False)
```

```python
import math

import jax
import jax.numpy as jnp
from jax import lax
from jax.experimental import pallas as pl
from jax.experimental.pallas import tpu as pltpu
from jax.sharding import PartitionSpec as P

TILE = 128
GROUP = 8
CELL_TILE = 16
VMEM_BYTES = 32 * 1024 * 1024
HIGHEST = lax.Precision.HIGHEST
SMEM = pl.BlockSpec(memory_space=pltpu.SMEM)
VMEM = pl.BlockSpec(memory_space=pltpu.VMEM)
ANY = pl.BlockSpec(memory_space=pl.ANY)
ROWS_BY_ROWS = (((0,), (0,)), ((), ()))
LANES_BY_LANES = (((1,), (1,)), ((), ()))


def pack_kernel(slabs, capacity, per_slab, parts, dest_ref, owned_ref, *refs):
    out_refs, (ids_ref, count_ref) = refs[:parts], refs[parts:]
    shares = owned_ref.shape[1]
    used = capacity * shares
    lane = lax.broadcasted_iota(jnp.int32, (1, TILE), 1)
    ids_ref[...] = jnp.full_like(ids_ref, -1)
    for slab in range(slabs):
        count_ref[slab] = 0

    def place(i, _):
        block = dest_ref[i]

        @pl.when(block >= 0)
        def _():
            slab = lax.div(block, per_slab)
            rank = count_ref[slab]
            count_ref[slab] = rank + 1
            here = pl.ds(slab, 1)
            ids_ref[here, :] = jnp.where(lane == rank, block - slab * per_slab, ids_ref[here, :])
            for part in range(parts):
                at = slab * (out_refs[part].shape[0] // slabs) + rank * shares
                out_refs[part][pl.ds(at, shares)] = owned_ref[i, :, part]

        return 0

    lax.fori_loop(0, dest_ref.shape[0], place, 0, unroll=4)
    for part in range(parts):
        span = out_refs[part].shape[0] // slabs
        if span > used:
            for slab in range(slabs):
                ids = ids_ref[slab : slab + 1, :].astype(jnp.float32)
                tile = jnp.broadcast_to(ids, out_refs[part].shape[1:])
                out_refs[part][slab * span + used] = tile.astype(out_refs[part].dtype)


def pack(dest, owned, slabs, per_slab, with_ids, after=()):
    slots, shares, parts, rows, width = owned.shape
    capacity = slots // slabs
    sent = []
    for part in range(parts):
        extra = slabs if with_ids and part == 0 else 0
        sent.append(jax.ShapeDtypeStruct((slots * shares + extra, rows, width), owned.dtype))
    return pl.pallas_call(
        lambda *refs: pack_kernel(slabs, capacity, per_slab, parts, *refs[len(after) :]),
        out_shape=tuple(sent),
        in_specs=[ANY] * len(after) + [SMEM, VMEM],
        out_specs=(VMEM,) * len(sent),
        scratch_shapes=[
            pltpu.VMEM((slabs, TILE), jnp.int32),
            pltpu.SMEM((slabs,), jnp.int32),
        ],
        compiler_params=pltpu.CompilerParams(vmem_limit_bytes=VMEM_BYTES),
        cost_estimate=pl.CostEstimate(
            flops=0, bytes_accessed=2 * owned.size * 2, transcendentals=0
        ),
        name="pack",
    )(*after, dest, owned)


def settle_kernel(slabs, capacity, first, *refs):
    if first:
        moved_ref, out_refs, meta_ref, ids_ref = refs[0], refs[1:-2], refs[-2], refs[-1]
        span = moved_ref.shape[0] // slabs
        for source in range(slabs):
            tile = moved_ref[source * span + span - 1].astype(jnp.float32)
            ids_ref[source : source + 1, :] = tile[:1].astype(jnp.int32)
        pltpu.sync_copy(ids_ref, meta_ref)
    else:
        meta_ref, moved_ref, out_refs = refs[0], refs[1], refs[2:]
        span = moved_ref.shape[0] // slabs
    shares = len(out_refs)
    mine = lax.axis_index("snap")
    for source in range(slabs):

        def place(rank, _):
            block = meta_ref[source, rank]

            @pl.when(block >= 0)
            def _():
                for r in range(shares):
                    out_refs[r][block] = moved_ref[source * span + rank * shares + (mine ^ r)]

            return 0

        lax.fori_loop(0, capacity, place, 0, unroll=4)


def settle(meta, moved, slabs, capacity, per_slab, shares, after=()):
    first = meta is None
    rows, width = moved.shape[1:]
    pieces = (jax.ShapeDtypeStruct((per_slab, rows, width), moved.dtype),) * shares
    ids = jax.ShapeDtypeStruct((slabs, TILE), jnp.int32)
    outs = pl.pallas_call(
        lambda *refs: settle_kernel(slabs, capacity, first, *refs[len(after) :]),
        out_shape=pieces + ((ids,) if first else ()),
        in_specs=[ANY] * len(after) + ([] if first else [SMEM]) + [VMEM],
        out_specs=(VMEM,) * shares + ((SMEM,) if first else ()),
        scratch_shapes=[pltpu.VMEM((slabs, TILE), jnp.int32)] if first else [],
        compiler_params=pltpu.CompilerParams(vmem_limit_bytes=VMEM_BYTES),
        cost_estimate=pl.CostEstimate(flops=0, bytes_accessed=2 * moved.size, transcendentals=0),
        name="settle",
    )(*after, *([] if first else [meta]), moved)
    return outs[:shares], (outs[shares] if first else meta)


def whole_rows(refs):
    blocks, rows, width = refs[0].shape
    return jnp.concatenate([ref[...].reshape(blocks * rows, width) for ref in refs], axis=1)


def tile_of(row, lane, tiles):
    return row * tiles - lax.div(row * (row - 1), 2) + lane - row


def gram_kernel(parts, shares, *refs):
    out_ref, acc_ref = refs[-2:]
    step = pl.program_id(0)

    @pl.when(step == 0)
    def _():
        acc_ref[...] = jnp.zeros_like(acc_ref)

    for part in range(parts):
        cells = whole_rows(refs[part * shares : (part + 1) * shares])
        acc_ref[...] += lax.dot_general(
            cells, cells, ROWS_BY_ROWS, preferred_element_type=jnp.float32
        )

    @pl.when(step == pl.num_programs(0) - 1)
    def _():
        mine = lax.axis_index("snap")
        for a in range(shares):
            for b in range(shares):
                row, lane = mine ^ a, mine ^ b

                @pl.when(row <= lane)
                def _():
                    out_ref[tile_of(row, lane, shares)] = acc_ref[
                        a * TILE : (a + 1) * TILE, b * TILE : (b + 1) * TILE
                    ]


def gram_blocks(cells, steps=4):
    shares = len(cells[0])
    blocks, rows, width = cells[0][0].shape
    pairs = shares * (shares + 1) // 2
    full = shares * width
    spec = pl.BlockSpec((blocks // steps, rows, width), lambda i: (i, 0, 0))
    return pl.pallas_call(
        lambda *refs: gram_kernel(len(cells), shares, *refs),
        grid=(steps,),
        out_shape=jax.ShapeDtypeStruct((pairs, TILE, TILE), jnp.float32),
        in_specs=[spec] * (len(cells) * shares),
        out_specs=pl.BlockSpec((pairs, TILE, TILE), lambda i: (0, 0, 0)),
        scratch_shapes=[pltpu.VMEM((full, full), jnp.float32)],
        compiler_params=pltpu.CompilerParams(vmem_limit_bytes=VMEM_BYTES),
        cost_estimate=pl.CostEstimate(
            flops=2 * len(cells) * blocks * rows * full * full,
            bytes_accessed=2 * len(cells) * blocks * rows * full,
            transcendentals=0,
        ),
        name="gram_blocks",
    )(*[piece for part in cells for piece in part])


def cross_kernel(parts, shares, *refs):
    out_ref, acc_ref = refs[-2:]
    step = pl.program_id(0)

    @pl.when(step == 0)
    def _():
        acc_ref[...] = jnp.zeros_like(acc_ref)

    for part in range(parts):
        x_refs = refs[part * shares : (part + 1) * shares]
        y_refs = refs[(parts + part) * shares : (parts + part + 1) * shares]
        acc_ref[...] += lax.dot_general(
            whole_rows(x_refs), whole_rows(y_refs), ROWS_BY_ROWS, preferred_element_type=jnp.float32
        )

    @pl.when(step == pl.num_programs(0) - 1)
    def _():
        mine = lax.axis_index("snap")
        for a in range(shares):
            rows = pl.ds(pl.multiple_of((mine ^ a) * TILE, TILE), TILE)
            for b in range(shares):
                lanes = pl.ds(pl.multiple_of((mine ^ b) * TILE, TILE), TILE)
                out_ref[rows, lanes] = acc_ref[
                    a * TILE : (a + 1) * TILE, b * TILE : (b + 1) * TILE
                ]


def cross_sum(x_cells, y_cells, after, steps=4):
    parts, shares = len(x_cells), len(x_cells[0])
    blocks, rows, width = x_cells[0][0].shape
    spec = pl.BlockSpec((blocks // steps, rows, width), lambda i: (i, 0, 0))
    full = shares * width
    return pl.pallas_call(
        lambda *refs: cross_kernel(parts, shares, *refs[len(after) :]),
        grid=(steps,),
        out_shape=jax.ShapeDtypeStruct((full, full), jnp.float32),
        in_specs=[ANY] * len(after) + [spec] * (2 * parts * shares),
        out_specs=pl.BlockSpec((full, full), lambda i: (0, 0)),
        scratch_shapes=[pltpu.VMEM((full, full), jnp.float32)],
        compiler_params=pltpu.CompilerParams(vmem_limit_bytes=VMEM_BYTES),
        cost_estimate=pl.CostEstimate(
            flops=2 * parts * blocks * rows * full * full,
            bytes_accessed=4 * parts * blocks * rows * full,
            transcendentals=0,
        ),
        name="cross_sum",
    )(*after, *[piece for part in list(x_cells) + list(y_cells) for piece in part])


def three_terms(value):
    high = value.astype(jnp.bfloat16).astype(jnp.float32)
    rest = value - high
    middle = rest.astype(jnp.bfloat16).astype(jnp.float32)
    return high, middle, rest - middle


def lane_of(row, lane):
    return jnp.broadcast_to(row[:, lane : lane + 1], row.shape)


def row_of(ref, row):
    return jnp.broadcast_to(ref[row : row + 1, :], (GROUP, TILE))


def factor_tile(a_ref, w_ref, u_ref, v_ref):
    panels = TILE // GROUP
    a_rows = [row_of(a_ref, i) for i in range(GROUP)]
    w_rows = [row_of(w_ref, i) for i in range(GROUP)]
    for p in range(panels):
        base = p * GROUP
        small = {
            (i, k): lane_of(a_rows[i], base + k) for i in range(GROUP) for k in range(i, GROUP)
        }
        for j in range(GROUP):
            scale = lax.rsqrt(small[j, j])
            a_rows[j] = a_rows[j] * scale
            w_rows[j] = w_rows[j] * scale
            u_ref[base + j : base + j + 1, :] = a_rows[j][:1]
            v_ref[base + j : base + j + 1, :] = w_rows[j][:1]
            below = {k: small[j, k] * scale for k in range(j + 1, GROUP)}
            for k in range(j + 1, GROUP):
                for m in range(k, GROUP):
                    small[k, m] = small[k, m] - below[k] * below[m]
            for k in range(j + 1, GROUP):
                a_rows[k] = a_rows[k] - below[k] * a_rows[j]
                w_rows[k] = w_rows[k] - below[k] * w_rows[j]
        if p + 1 == panels:
            break
        after = base + GROUP
        next_a = [row_of(a_ref, after + i) for i in range(GROUP)]
        next_w = [row_of(w_ref, after + i) for i in range(GROUP)]
        for i in range(GROUP):
            for k in range(GROUP):
                factor = lane_of(a_rows[k], after + i)
                next_a[i] = next_a[i] - factor * a_rows[k]
                next_w[i] = next_w[i] - factor * w_rows[k]
        if p + 2 < panels:
            done = after + GROUP
            u = u_ref[base:after, :]
            v = v_ref[base:after, :]
            uh, um, ul = three_terms(u)
            vh, vm, vl = three_terms(v)
            left = jnp.concatenate([uh, uh, um, uh, ul, um], axis=0).astype(jnp.bfloat16)
            right_a = jnp.concatenate([uh, um, uh, ul, uh, um], axis=0)
            right_w = jnp.concatenate([vh, vm, vh, vl, vh, vm], axis=0)
            right = jnp.concatenate([right_a, right_w], axis=1).astype(jnp.bfloat16)
            update = lax.dot_general(
                left, right, ROWS_BY_ROWS, preferred_element_type=jnp.float32
            )
            a_ref[done:, :] = a_ref[done:, :] - update[done:, :TILE]
            w_ref[done:, :] = w_ref[done:, :] - update[done:, TILE:]
        a_rows, w_rows = next_a, next_w


def factor_kernel(tiles, rows_total, g_ref, r_ref, inv_ref, hi_ref, mid_ref, lo_ref, wide, a_ref, w_ref, u_ref, v_ref):
    row = lax.broadcasted_iota(jnp.int32, (TILE, TILE), 0)
    lane = lax.broadcasted_iota(jnp.int32, (TILE, TILE), 1)
    wide[...] = jnp.zeros_like(wide)
    at = 0
    for a in range(tiles):
        for b in range(a, tiles):
            wide[a, b] = g_ref[at] / rows_total
            at += 1

    def step(b, _):
        a_ref[...] = wide[b, b]
        w_ref[...] = jnp.where(row == lane, 1.0, 0.0)
        factor_tile(a_ref, w_ref, u_ref, v_ref)
        inverse = v_ref[...]
        wide[b, b] = jnp.where(row <= lane, u_ref[...], 0.0)
        wide[b, tiles + b] = inverse
        for j in range(1, tiles):
            wide[b, b + j] = lax.dot(
                inverse, wide[b, b + j], precision=HIGHEST, preferred_element_type=jnp.float32
            )

        def trail(r, _):
            left = wide[b, r]
            for j in range(1, tiles + 1):
                wide[r, b + j] = wide[r, b + j] - lax.dot_general(
                    left,
                    wide[b, b + j],
                    ROWS_BY_ROWS,
                    precision=HIGHEST,
                    preferred_element_type=jnp.float32,
                )
            return 0

        lax.fori_loop(b + 1, tiles, trail, 0)
        return 0

    lax.fori_loop(0, tiles, step, 0)
    zero = jnp.zeros((TILE, TILE), jnp.float32)
    mine = lax.axis_index("snap")
    for a in range(tiles):
        rows = slice(a * TILE, (a + 1) * TILE)
        for b in range(tiles):
            lanes = slice(b * TILE, (b + 1) * TILE)
            r_ref[rows, lanes] = wide[a, b] if b >= a else zero
            value = wide[a, tiles + b] if b <= a else zero
            inv_ref[rows, lanes] = value
            high, middle, low = three_terms(value)
            lanes = pl.ds(pl.multiple_of((mine ^ b) * TILE, TILE), TILE)
            hi_ref[rows, lanes] = high.astype(jnp.bfloat16)
            mid_ref[rows, lanes] = middle.astype(jnp.bfloat16)
            lo_ref[rows, lanes] = low.astype(jnp.bfloat16)


def factor(blocks, tiles, rows_total, after):
    full = tiles * TILE
    tile = pltpu.VMEM((TILE, TILE), jnp.float32)
    return pl.pallas_call(
        lambda *refs: factor_kernel(tiles, rows_total, *refs[len(after) :]),
        out_shape=(
            jax.ShapeDtypeStruct((full, full), jnp.float32),
            jax.ShapeDtypeStruct((full, full), jnp.float32),
            jax.ShapeDtypeStruct((full, full), jnp.bfloat16),
            jax.ShapeDtypeStruct((full, full), jnp.bfloat16),
            jax.ShapeDtypeStruct((full, full), jnp.bfloat16),
        ),
        in_specs=[ANY] * len(after) + [VMEM],
        out_specs=(VMEM,) * 5,
        scratch_shapes=[
            pltpu.VMEM((tiles, 2 * tiles, TILE, TILE), jnp.float32),
            tile,
            tile,
            tile,
            tile,
        ],
        compiler_params=pltpu.CompilerParams(vmem_limit_bytes=VMEM_BYTES),
        cost_estimate=pl.CostEstimate(
            flops=40 * 10**9, bytes_accessed=8 * full * full, transcendentals=full
        ),
        name="factor",
    )(*after, blocks)


def basis_kernel(parts, shares, *refs):
    hi_ref, mid_ref, lo_ref, out_ref = refs[parts * shares :]
    for part in range(parts):
        cells = whole_rows(refs[part * shares : (part + 1) * shares])
        total = lax.dot_general(
            cells, lo_ref[...], LANES_BY_LANES, preferred_element_type=jnp.float32
        )
        total += lax.dot_general(
            cells, mid_ref[...], LANES_BY_LANES, preferred_element_type=jnp.float32
        )
        total += lax.dot_general(
            cells, hi_ref[...], LANES_BY_LANES, preferred_element_type=jnp.float32
        )
        blocks, _, rows, full = out_ref.shape
        out_ref[:, part] = total.reshape(blocks, rows, full)


def basis(cells, terms, steps=8):
    parts, shares = len(cells), len(cells[0])
    blocks, rows, width = cells[0][0].shape
    full = shares * width
    spec = pl.BlockSpec((blocks // steps, rows, width), lambda i: (i, 0, 0))
    term = pl.BlockSpec((full, full), lambda i: (0, 0))
    return pl.pallas_call(
        lambda *refs: basis_kernel(parts, shares, *refs),
        grid=(steps,),
        out_shape=jax.ShapeDtypeStruct((blocks, parts, rows, full), jnp.float32),
        in_specs=[spec] * (parts * shares) + [term] * 3,
        out_specs=pl.BlockSpec((blocks // steps, parts, rows, full), lambda i: (i, 0, 0, 0)),
        compiler_params=pltpu.CompilerParams(vmem_limit_bytes=VMEM_BYTES),
        cost_estimate=pl.CostEstimate(
            flops=6 * parts * blocks * rows * full * full,
            bytes_accessed=6 * parts * blocks * rows * full,
            transcendentals=0,
        ),
        name="basis",
    )(*[piece for part in cells for piece in part], *terms)


def swap(value, axis, mask):
    return lax.ppermute(value, axis, [(i, i ^ mask) for i in range(lax.axis_size(axis))])


def slab_sum(value, slabs):
    return lax.psum_scatter(value, "space", scatter_dimension=0, tiled=True)


def share_sum(piece, shares):
    hop = 1
    while hop < shares:
        piece += swap(piece, "snap", hop)
        hop *= 2
    return lax.all_gather(piece, "space", axis=0, tiled=True)


def body(owned_x, owned_y, patch_dest):
    slabs = lax.axis_size("space")
    shares = lax.axis_size("snap")
    slots, patch, width = owned_x.shape
    per_slab = slots // 2
    parts = patch // shares // CELL_TILE
    rows_total = slabs * per_slab * patch
    full = shares * width
    tiles = full // TILE
    pairs = tiles * (tiles + 1) // 2

    def parted(owned):
        return owned.reshape(slots, shares, parts, CELL_TILE, width)

    def to_slabs(part):
        return lax.all_to_all(part, "space", split_axis=0, concat_axis=0, tiled=True)

    def to_rows(pieces):
        return [pieces[0]] + [swap(pieces[r], "snap", r) for r in range(1, shares)]

    def place(meta, moved, after=()):
        return settle(meta, moved, slabs, slots // slabs, per_slab, shares, after)

    sent_x = pack(patch_dest, parted(owned_x), slabs, per_slab, True)
    moved_x = [to_slabs(part) for part in sent_x]
    pieces, meta = place(None, moved_x[0])
    x_cells = [to_rows(pieces)]
    sent_y = pack(patch_dest, parted(owned_y), slabs, per_slab, False, [meta])
    for moved in moved_x[1:]:
        pieces, _ = place(meta, moved, x_cells[-1][1:] + [sent_y[0]])
        x_cells.append(to_rows(pieces))
    gram_piece = slab_sum(gram_blocks(x_cells).reshape(pairs * TILE, TILE), slabs)

    y_cells, after = [], x_cells[-1][1:]
    for part in sent_y:
        pieces, _ = place(meta, to_slabs(part), after)
        y_cells.append(to_rows(pieces))
        after = y_cells[-1][1:] + [gram_piece]

    gram = share_sum(gram_piece, shares)
    r_factor, inverse, *terms = factor(
        gram.reshape(pairs, TILE, TILE), tiles, rows_total, [y_cells[-1][0]]
    )
    q_basis = basis(x_cells, terms).reshape(per_slab, patch // shares, full)

    cross = share_sum(slab_sum(cross_sum(x_cells, y_cells, [gram]), slabs), shares)
    projection = jnp.dot(inverse, cross, precision=HIGHEST) / math.sqrt(rows_total)
    return q_basis, r_factor, projection


def solution(mesh):
    in_specs = (P("space", None, "snap"), P("space", None, "snap"), P("space"))
    out_specs = (P("space", "snap", None), P(), P())
    return jax.shard_map(body, mesh=mesh, in_specs=in_specs, out_specs=out_specs, check_vma=False)
```

```python
import math

import jax
import jax.numpy as jnp
from jax import lax
from jax.experimental import pallas as pl
from jax.experimental.pallas import tpu as pltpu
from jax.sharding import PartitionSpec as P

TILE = 128
GROUP = 8
CORES = 2
CELL_TILE = 16
VMEM_BYTES = 32 * 1024 * 1024
HIGHEST = lax.Precision.HIGHEST
SMEM = pl.BlockSpec(memory_space=pltpu.SMEM)
VMEM = pl.BlockSpec(memory_space=pltpu.VMEM)
ANY = pl.BlockSpec(memory_space=pl.ANY)
ROWS_BY_ROWS = (((0,), (0,)), ((), ()))
LANES_BY_LANES = (((1,), (1,)), ((), ()))


def pack_kernel(slabs, capacity, per_slab, parts, dest_ref, owned_ref, *refs):
    out_refs, (ids_ref, count_ref) = refs[: 2 * parts], refs[2 * parts :]
    chips = slabs // CORES
    shares = owned_ref.shape[1]
    used = capacity * shares
    me = lax.axis_index("space")
    lane = lax.broadcasted_iota(jnp.int32, (1, TILE), 1)
    ids_ref[...] = jnp.full_like(ids_ref, -1)
    for slab in range(slabs):
        count_ref[slab] = 0

    def place(i, _):
        block = dest_ref[i]

        @pl.when(block >= 0)
        def _():
            slab = lax.div(block, per_slab)
            rank = count_ref[slab]
            count_ref[slab] = rank + 1
            here = pl.ds(slab, 1)
            ids_ref[here, :] = jnp.where(lane == rank, block - slab * per_slab, ids_ref[here, :])
            away = slab ^ me
            chip = lax.shift_right_logical(away, 1)
            for core in range(CORES):

                @pl.when((away & 1) == core)
                def _():
                    for part in range(parts):
                        out_ref = out_refs[part * CORES + core]
                        at = chip * (out_ref.shape[0] // chips) + rank * shares
                        out_ref[pl.ds(at, shares)] = owned_ref[i, :, part]

        return 0

    lax.fori_loop(0, dest_ref.shape[0], place, 0, unroll=2)
    for away in range(slabs):
        for part in range(parts):
            out_ref = out_refs[part * CORES + away % CORES]
            span = out_ref.shape[0] // chips
            if span > used:
                ids = ids_ref[pl.ds(me ^ away, 1), :].astype(jnp.float32)
                tile = jnp.broadcast_to(ids, out_ref.shape[1:]).astype(out_ref.dtype)
                out_ref[away // CORES * span + used] = tile


def pack(dest, owned, slabs, per_slab, with_ids, after=()):
    slots, shares, parts, rows, width = owned.shape
    chips = slabs // CORES
    capacity = slots // slabs
    sent = []
    for part in range(parts):
        span = capacity * shares + (1 if with_ids and part == 0 else 0)
        sent += [jax.ShapeDtypeStruct((chips * span, rows, width), owned.dtype)] * CORES
    outs = pl.pallas_call(
        lambda *refs: pack_kernel(slabs, capacity, per_slab, parts, *refs[len(after) :]),
        out_shape=tuple(sent),
        in_specs=[ANY] * len(after) + [SMEM, VMEM],
        out_specs=(VMEM,) * len(sent),
        scratch_shapes=[
            pltpu.VMEM((slabs, TILE), jnp.int32),
            pltpu.SMEM((slabs,), jnp.int32),
        ],
        compiler_params=pltpu.CompilerParams(vmem_limit_bytes=VMEM_BYTES),
        cost_estimate=pl.CostEstimate(
            flops=0, bytes_accessed=2 * owned.size * 2, transcendentals=0
        ),
        name="pack",
    )(*after, dest, owned)
    return [outs[part * CORES : (part + 1) * CORES] for part in range(parts)]


def merge_kernel(same_ref, other_ref, *out_refs):
    span = same_ref.shape[0] // len(out_refs)
    for chip, out_ref in enumerate(out_refs):
        out_ref[:span] = same_ref[chip * span : (chip + 1) * span]
        out_ref[span:] = other_ref[chip * span : (chip + 1) * span]


def merge(same, other, chips):
    tiles, rows, width = same.shape
    out = jax.ShapeDtypeStruct((CORES * tiles // chips, rows, width), same.dtype)
    return pl.pallas_call(
        merge_kernel,
        out_shape=(out,) * chips,
        in_specs=[VMEM, VMEM],
        out_specs=(VMEM,) * chips,
        compiler_params=pltpu.CompilerParams(vmem_limit_bytes=VMEM_BYTES),
        cost_estimate=pl.CostEstimate(flops=0, bytes_accessed=8 * same.size, transcendentals=0),
        name="merge",
    )(same, other)


def settle_kernel(chips, capacity, first, *refs):
    if first:
        moved_refs, out_refs, meta_ref, ids_ref = refs[:chips], refs[chips:-2], refs[-2], refs[-1]
        span = moved_refs[0].shape[0] // CORES
        for source in range(chips * CORES):
            at = source % CORES * span + span - 1
            tile = moved_refs[source // CORES][at].astype(jnp.float32)
            ids_ref[source : source + 1, :] = tile[:1].astype(jnp.int32)
        pltpu.sync_copy(ids_ref, meta_ref)
    else:
        meta_ref, moved_refs, out_refs = refs[0], refs[1 : 1 + chips], refs[1 + chips :]
        span = moved_refs[0].shape[0] // CORES
    shares = len(out_refs)
    mine = lax.axis_index("snap")
    for source in range(chips * CORES):
        moved_ref = moved_refs[source // CORES]

        def place(rank, _):
            block = meta_ref[source, rank]

            @pl.when(block >= 0)
            def _():
                at = source % CORES * span + rank * shares
                for r in range(shares):
                    out_refs[r][block] = moved_ref[at + (mine ^ r)]

            return 0

        lax.fori_loop(0, capacity, place, 0, unroll=4)


def settle(meta, moved, capacity, per_slab, shares, after=()):
    first = meta is None
    chips = len(moved)
    rows, width = moved[0].shape[1:]
    pieces = (jax.ShapeDtypeStruct((per_slab, rows, width), moved[0].dtype),) * shares
    ids = jax.ShapeDtypeStruct((chips * CORES, TILE), jnp.int32)
    outs = pl.pallas_call(
        lambda *refs: settle_kernel(chips, capacity, first, *refs[len(after) :]),
        out_shape=pieces + ((ids,) if first else ()),
        in_specs=[ANY] * len(after) + ([] if first else [SMEM]) + [VMEM] * chips,
        out_specs=(VMEM,) * shares + ((SMEM,) if first else ()),
        scratch_shapes=[pltpu.VMEM((chips * CORES, TILE), jnp.int32)] if first else [],
        compiler_params=pltpu.CompilerParams(vmem_limit_bytes=VMEM_BYTES),
        cost_estimate=pl.CostEstimate(
            flops=0, bytes_accessed=2 * chips * moved[0].size, transcendentals=0
        ),
        name="settle",
    )(*after, *([] if first else [meta]), *moved)
    return outs[:shares], (outs[shares] if first else meta)


def whole_rows(refs):
    blocks, rows, width = refs[0].shape
    return jnp.concatenate([ref[...].reshape(blocks * rows, width) for ref in refs], axis=1)


def tile_of(row, lane, tiles):
    return row * tiles - lax.div(row * (row - 1), 2) + lane - row


def gram_kernel(parts, shares, *refs):
    out_ref, acc_ref = refs[-2:]
    step = pl.program_id(0)

    @pl.when(step == 0)
    def _():
        acc_ref[...] = jnp.zeros_like(acc_ref)

    for part in range(parts):
        cells = whole_rows(refs[part * shares : (part + 1) * shares])
        acc_ref[...] += lax.dot_general(
            cells, cells, ROWS_BY_ROWS, preferred_element_type=jnp.float32
        )

    @pl.when(step == pl.num_programs(0) - 1)
    def _():
        mine = lax.axis_index("snap")
        for a in range(shares):
            for b in range(shares):
                row, lane = mine ^ a, mine ^ b

                @pl.when(row <= lane)
                def _():
                    out_ref[tile_of(row, lane, shares)] = acc_ref[
                        a * TILE : (a + 1) * TILE, b * TILE : (b + 1) * TILE
                    ]


def gram_blocks(cells, steps=4):
    shares = len(cells[0])
    blocks, rows, width = cells[0][0].shape
    pairs = shares * (shares + 1) // 2
    full = shares * width
    spec = pl.BlockSpec((blocks // steps, rows, width), lambda i: (i, 0, 0))
    return pl.pallas_call(
        lambda *refs: gram_kernel(len(cells), shares, *refs),
        grid=(steps,),
        out_shape=jax.ShapeDtypeStruct((pairs, TILE, TILE), jnp.float32),
        in_specs=[spec] * (len(cells) * shares),
        out_specs=pl.BlockSpec((pairs, TILE, TILE), lambda i: (0, 0, 0)),
        scratch_shapes=[pltpu.VMEM((full, full), jnp.float32)],
        compiler_params=pltpu.CompilerParams(vmem_limit_bytes=VMEM_BYTES),
        cost_estimate=pl.CostEstimate(
            flops=2 * len(cells) * blocks * rows * full * full,
            bytes_accessed=2 * len(cells) * blocks * rows * full,
            transcendentals=0,
        ),
        name="gram_blocks",
    )(*[piece for part in cells for piece in part])


def cross_kernel(parts, shares, *refs):
    out_ref, acc_ref = refs[-2:]
    step = pl.program_id(0)

    @pl.when(step == 0)
    def _():
        acc_ref[...] = jnp.zeros_like(acc_ref)

    for part in range(parts):
        x_refs = refs[part * shares : (part + 1) * shares]
        y_refs = refs[(parts + part) * shares : (parts + part + 1) * shares]
        acc_ref[...] += lax.dot_general(
            whole_rows(x_refs), whole_rows(y_refs), ROWS_BY_ROWS, preferred_element_type=jnp.float32
        )

    @pl.when(step == pl.num_programs(0) - 1)
    def _():
        mine = lax.axis_index("snap")
        for a in range(shares):
            rows = pl.ds(pl.multiple_of((mine ^ a) * TILE, TILE), TILE)
            for b in range(shares):
                lanes = pl.ds(pl.multiple_of((mine ^ b) * TILE, TILE), TILE)
                out_ref[rows, lanes] = acc_ref[
                    a * TILE : (a + 1) * TILE, b * TILE : (b + 1) * TILE
                ]


def cross_sum(x_cells, y_cells, after, steps=4):
    parts, shares = len(x_cells), len(x_cells[0])
    blocks, rows, width = x_cells[0][0].shape
    spec = pl.BlockSpec((blocks // steps, rows, width), lambda i: (i, 0, 0))
    full = shares * width
    return pl.pallas_call(
        lambda *refs: cross_kernel(parts, shares, *refs[len(after) :]),
        grid=(steps,),
        out_shape=jax.ShapeDtypeStruct((full, full), jnp.float32),
        in_specs=[ANY] * len(after) + [spec] * (2 * parts * shares),
        out_specs=pl.BlockSpec((full, full), lambda i: (0, 0)),
        scratch_shapes=[pltpu.VMEM((full, full), jnp.float32)],
        compiler_params=pltpu.CompilerParams(vmem_limit_bytes=VMEM_BYTES),
        cost_estimate=pl.CostEstimate(
            flops=2 * parts * blocks * rows * full * full,
            bytes_accessed=4 * parts * blocks * rows * full,
            transcendentals=0,
        ),
        name="cross_sum",
    )(*after, *[piece for part in list(x_cells) + list(y_cells) for piece in part])


def three_terms(value):
    high = value.astype(jnp.bfloat16).astype(jnp.float32)
    rest = value - high
    middle = rest.astype(jnp.bfloat16).astype(jnp.float32)
    return high, middle, rest - middle


def lane_of(row, lane):
    return jnp.broadcast_to(row[:, lane : lane + 1], row.shape)


def row_of(ref, row):
    return jnp.broadcast_to(ref[row : row + 1, :], (GROUP, TILE))


def factor_tile(a_ref, w_ref, u_ref, v_ref):
    panels = TILE // GROUP
    a_rows = [row_of(a_ref, i) for i in range(GROUP)]
    w_rows = [row_of(w_ref, i) for i in range(GROUP)]
    for p in range(panels):
        base = p * GROUP
        small = {
            (i, k): lane_of(a_rows[i], base + k) for i in range(GROUP) for k in range(i, GROUP)
        }
        for j in range(GROUP):
            scale = lax.rsqrt(small[j, j])
            a_rows[j] = a_rows[j] * scale
            w_rows[j] = w_rows[j] * scale
            u_ref[base + j : base + j + 1, :] = a_rows[j][:1]
            v_ref[base + j : base + j + 1, :] = w_rows[j][:1]
            below = {k: small[j, k] * scale for k in range(j + 1, GROUP)}
            for k in range(j + 1, GROUP):
                for m in range(k, GROUP):
                    small[k, m] = small[k, m] - below[k] * below[m]
            for k in range(j + 1, GROUP):
                a_rows[k] = a_rows[k] - below[k] * a_rows[j]
                w_rows[k] = w_rows[k] - below[k] * w_rows[j]
        if p + 1 == panels:
            break
        after = base + GROUP
        next_a = [row_of(a_ref, after + i) for i in range(GROUP)]
        next_w = [row_of(w_ref, after + i) for i in range(GROUP)]
        for i in range(GROUP):
            for k in range(GROUP):
                factor = lane_of(a_rows[k], after + i)
                next_a[i] = next_a[i] - factor * a_rows[k]
                next_w[i] = next_w[i] - factor * w_rows[k]
        if p + 2 < panels:
            done = after + GROUP
            u = u_ref[base:after, :]
            v = v_ref[base:after, :]
            uh, um, ul = three_terms(u)
            vh, vm, vl = three_terms(v)
            left = jnp.concatenate([uh, uh, um, uh, ul, um], axis=0).astype(jnp.bfloat16)
            right_a = jnp.concatenate([uh, um, uh, ul, uh, um], axis=0)
            right_w = jnp.concatenate([vh, vm, vh, vl, vh, vm], axis=0)
            right = jnp.concatenate([right_a, right_w], axis=1).astype(jnp.bfloat16)
            update = lax.dot_general(
                left, right, ROWS_BY_ROWS, preferred_element_type=jnp.float32
            )
            a_ref[done:, :] = a_ref[done:, :] - update[done:, :TILE]
            w_ref[done:, :] = w_ref[done:, :] - update[done:, TILE:]
        a_rows, w_rows = next_a, next_w


def factor_step(tiles, b, wide, a_ref, w_ref, u_ref, v_ref):
    row = lax.broadcasted_iota(jnp.int32, (TILE, TILE), 0)
    lane = lax.broadcasted_iota(jnp.int32, (TILE, TILE), 1)
    a_ref[...] = wide[b, b]
    w_ref[...] = jnp.where(row == lane, 1.0, 0.0)
    factor_tile(a_ref, w_ref, u_ref, v_ref)
    inverse = v_ref[...]
    wide[b, b] = jnp.where(row <= lane, u_ref[...], 0.0)
    wide[b, tiles + b] = inverse
    for j in range(1, tiles):
        wide[b, b + j] = lax.dot(
            inverse, wide[b, b + j], precision=HIGHEST, preferred_element_type=jnp.float32
        )
    for r in range(b + 1, tiles):
        for c in list(range(r, tiles)) + list(range(tiles, tiles + b + 1)):
            update = lax.dot_general(
                wide[b, r],
                wide[b, c],
                ROWS_BY_ROWS,
                precision=HIGHEST,
                preferred_element_type=jnp.float32,
            )
            wide[r, c] = -update if c == tiles + b else wide[r, c] - update


def first_kernel(tiles, rows_total, g_ref, wide, *scratch):
    at = 0
    for a in range(tiles):
        for b in range(a, tiles):
            wide[a, b] = g_ref[at] / rows_total
            at += 1
    factor_step(tiles, 0, wide, *scratch)


def next_kernel(tiles, b, _, wide, *scratch):
    factor_step(tiles, b, wide, *scratch)


def last_kernel(tiles, wide, r_ref, inv_ref, hi_ref, mid_ref, lo_ref, *scratch):
    factor_step(tiles, tiles - 1, wide, *scratch)
    zero = jnp.zeros((TILE, TILE), jnp.float32)
    mine = lax.axis_index("snap")
    for a in range(tiles):
        rows = slice(a * TILE, (a + 1) * TILE)
        for b in range(tiles):
            lanes = slice(b * TILE, (b + 1) * TILE)
            r_ref[rows, lanes] = wide[a, b] if b >= a else zero
            value = wide[a, tiles + b] if b <= a else zero
            inv_ref[rows, lanes] = value
            high, middle, low = three_terms(value)
            lanes = pl.ds(pl.multiple_of((mine ^ b) * TILE, TILE), TILE)
            hi_ref[rows, lanes] = high.astype(jnp.bfloat16)
            mid_ref[rows, lanes] = middle.astype(jnp.bfloat16)
            lo_ref[rows, lanes] = low.astype(jnp.bfloat16)


def factor_call(kernel, out_shape, value, after, aliases, tiles):
    many = isinstance(out_shape, tuple)
    return pl.pallas_call(
        lambda *refs: kernel(*refs[len(after) :]),
        out_shape=out_shape,
        in_specs=[ANY] * len(after) + [VMEM],
        out_specs=(VMEM,) * len(out_shape) if many else VMEM,
        scratch_shapes=[pltpu.VMEM((TILE, TILE), jnp.float32)] * 4,
        input_output_aliases={len(after): 0} if aliases else {},
        compiler_params=pltpu.CompilerParams(vmem_limit_bytes=VMEM_BYTES),
        cost_estimate=pl.CostEstimate(
            flops=7 * 10**9, bytes_accessed=value.size * 4, transcendentals=TILE
        ),
        name="factor",
    )(*after, value)


def factor_steps(blocks, tiles, rows_total, after):
    state = jax.ShapeDtypeStruct((tiles, 2 * tiles, TILE, TILE), jnp.float32)
    full = jax.ShapeDtypeStruct((tiles * TILE, tiles * TILE), jnp.float32)
    term = jax.ShapeDtypeStruct(full.shape, jnp.bfloat16)
    value = factor_call(
        lambda *refs: first_kernel(tiles, rows_total, *refs), state, blocks, after, False, tiles
    )
    for b in range(1, tiles - 1):
        after = yield value
        value = factor_call(
            lambda *refs: next_kernel(tiles, b, *refs), state, value, after, True, tiles
        )
    after = yield value
    yield factor_call(
        lambda *refs: last_kernel(tiles, *refs), (full, full, term, term, term), value, after, False, tiles
    )


def basis_kernel(parts, shares, *refs):
    hi_ref, mid_ref, lo_ref, out_ref = refs[parts * shares :]
    for part in range(parts):
        cells = whole_rows(refs[part * shares : (part + 1) * shares])
        total = lax.dot_general(
            cells, lo_ref[...], LANES_BY_LANES, preferred_element_type=jnp.float32
        )
        total += lax.dot_general(
            cells, mid_ref[...], LANES_BY_LANES, preferred_element_type=jnp.float32
        )
        total += lax.dot_general(
            cells, hi_ref[...], LANES_BY_LANES, preferred_element_type=jnp.float32
        )
        blocks, _, rows, full = out_ref.shape
        out_ref[:, part] = total.reshape(blocks, rows, full)


def basis(cells, terms, steps=8):
    parts, shares = len(cells), len(cells[0])
    blocks, rows, width = cells[0][0].shape
    full = shares * width
    spec = pl.BlockSpec((blocks // steps, rows, width), lambda i: (i, 0, 0))
    term = pl.BlockSpec((full, full), lambda i: (0, 0))
    return pl.pallas_call(
        lambda *refs: basis_kernel(parts, shares, *refs),
        grid=(steps,),
        out_shape=jax.ShapeDtypeStruct((blocks, parts, rows, full), jnp.float32),
        in_specs=[spec] * (parts * shares) + [term] * 3,
        out_specs=pl.BlockSpec((blocks // steps, parts, rows, full), lambda i: (i, 0, 0, 0)),
        compiler_params=pltpu.CompilerParams(vmem_limit_bytes=VMEM_BYTES),
        cost_estimate=pl.CostEstimate(
            flops=6 * parts * blocks * rows * full * full,
            bytes_accessed=6 * parts * blocks * rows * full,
            transcendentals=0,
        ),
        name="basis",
    )(*[piece for part in cells for piece in part], *terms)


def swap(value, axis, mask):
    return lax.ppermute(value, axis, [(i, i ^ mask) for i in range(lax.axis_size(axis))])


def slab_sum(value, slabs):
    pieces = lax.all_to_all(value, "space", split_axis=0, concat_axis=0, tiled=True)
    return jnp.sum(pieces.reshape(slabs, -1, value.shape[-1]), axis=0)


def share_sum(piece, shares):
    hop = 1
    while hop < shares:
        piece += swap(piece, "snap", hop)
        hop *= 2
    return lax.all_gather(piece, "space", axis=0, tiled=True)


def body(owned_x, owned_y, patch_dest):
    slabs = lax.axis_size("space")
    shares = lax.axis_size("snap")
    slots, patch, width = owned_x.shape
    per_slab = slots // 2
    parts = patch // shares // CELL_TILE
    rows_total = slabs * per_slab * patch
    full = shares * width
    tiles = full // TILE
    pairs = tiles * (tiles + 1) // 2

    def parted(owned):
        return owned.reshape(slots, shares, parts, CELL_TILE, width)

    def merged(part):
        return merge(part[0], swap(part[1], "space", 1), slabs // CORES)

    def to_chips(joined):
        return [joined[0]] + [swap(joined[m], "space", CORES * m) for m in range(1, len(joined))]

    def to_rows(pieces):
        return [pieces[0]] + [swap(pieces[r], "snap", r) for r in range(1, shares)]

    def place(meta, moved, after=()):
        return settle(meta, moved, slots // slabs, per_slab, shares, after)

    sent_x = pack(patch_dest, parted(owned_x), slabs, per_slab, True)
    moved_x = [to_chips(merged(part)) for part in sent_x]
    pieces, meta = place(None, moved_x[0])
    x_cells = [to_rows(pieces)]
    sent_y = pack(patch_dest, parted(owned_y), slabs, per_slab, False, x_cells[0][1:2])
    joined_y = [merged(part) for part in sent_y]
    for moved in moved_x[1:]:
        pieces, _ = place(meta, moved, x_cells[-1][1:] + [joined_y[0][0]])
        x_cells.append(to_rows(pieces))
    gram_piece = slab_sum(gram_blocks(x_cells).reshape(pairs * TILE, TILE), slabs)

    y_cells, after = [], x_cells[-1][1:]
    for joined in joined_y:
        pieces, _ = place(meta, to_chips(joined), after)
        y_cells.append(to_rows(pieces))
        after = y_cells[-1][1:] + [gram_piece]

    gram = share_sum(gram_piece, shares)
    steps = factor_steps(
        gram.reshape(pairs, TILE, TILE), tiles, rows_total, [y_cells[-1][0]]
    )
    state = next(steps)
    cross_local = cross_sum(x_cells, y_cells, [state])
    state = steps.send([cross_local])
    cross_piece = slab_sum(cross_local, slabs)
    for _ in range(tiles - 2):
        state = steps.send([cross_piece])
    cross = share_sum(cross_piece, shares)
    r_factor, inverse, *terms = state
    q_basis = basis(x_cells, terms).reshape(per_slab, patch // shares, full)

    projection = jnp.dot(inverse, cross, precision=HIGHEST) / math.sqrt(rows_total)
    return q_basis, r_factor, projection


def solution(mesh):
    in_specs = (P("space", None, "snap"), P("space", None, "snap"), P("space"))
    out_specs = (P("space", "snap", None), P(), P())
    return jax.shard_map(body, mesh=mesh, in_specs=in_specs, out_specs=out_specs, check_vma=False)
```

```python
import math

import jax
import jax.numpy as jnp
from jax import lax
from jax.experimental import pallas as pl
from jax.experimental.pallas import tpu as pltpu
from jax.sharding import PartitionSpec as P

TILE = 128
GROUP = 8
CORES = 2
CELL_TILE = 16
VMEM_BYTES = 32 * 1024 * 1024
HIGHEST = lax.Precision.HIGHEST
SMEM = pl.BlockSpec(memory_space=pltpu.SMEM)
VMEM = pl.BlockSpec(memory_space=pltpu.VMEM)
ANY = pl.BlockSpec(memory_space=pl.ANY)
ROWS_BY_ROWS = (((0,), (0,)), ((), ()))
LANES_BY_LANES = (((1,), (1,)), ((), ()))


def cost(flops, bytes_accessed, transcendentals):
    return pl.CostEstimate(
        flops=flops,
        bytes_accessed=bytes_accessed,
        transcendentals=transcendentals,
    )


def pack_kernel(slabs, capacity, per_slab, parts, dest_ref, owned_ref, *refs):
    out_refs, (ids_ref, count_ref) = refs[: 2 * parts], refs[2 * parts :]
    chips = slabs // CORES
    shares = owned_ref.shape[1]
    used = capacity * shares
    me = lax.axis_index("space")
    lane = lax.broadcasted_iota(jnp.int32, (1, TILE), 1)
    ids_ref[...] = jnp.full_like(ids_ref, -1)
    for slab in range(slabs):
        count_ref[slab] = 0

    def place(i, _):
        block = dest_ref[i]

        @pl.when(block >= 0)
        def _():
            slab = lax.div(block, per_slab)
            rank = count_ref[slab]
            count_ref[slab] = rank + 1
            here = pl.ds(slab, 1)
            ids_ref[here, :] = jnp.where(lane == rank, block - slab * per_slab, ids_ref[here, :])
            away = slab ^ me
            chip = lax.shift_right_logical(away, 1)
            for core in range(CORES):

                @pl.when((away & 1) == core)
                def _():
                    for part in range(parts):
                        out_ref = out_refs[part * CORES + core]
                        at = chip * (out_ref.shape[0] // chips) + rank * shares
                        out_ref[pl.ds(at, shares)] = owned_ref[i, :, part]

        return 0

    lax.fori_loop(0, dest_ref.shape[0], place, 0, unroll=2)
    for away in range(slabs):
        for part in range(parts):
            out_ref = out_refs[part * CORES + away % CORES]
            span = out_ref.shape[0] // chips
            if span > used:
                ids = ids_ref[pl.ds(me ^ away, 1), :].astype(jnp.float32)
                tile = jnp.broadcast_to(ids, out_ref.shape[1:]).astype(out_ref.dtype)
                out_ref[away // CORES * span + used] = tile


def pack(dest, owned, slabs, per_slab, with_ids, after=()):
    slots, shares, parts, rows, width = owned.shape
    chips = slabs // CORES
    capacity = slots // slabs
    sent = []
    for part in range(parts):
        span = capacity * shares + (1 if with_ids and part == 0 else 0)
        sent += [jax.ShapeDtypeStruct((chips * span, rows, width), owned.dtype)] * CORES
    outs = pl.pallas_call(
        lambda *refs: pack_kernel(slabs, capacity, per_slab, parts, *refs[len(after) :]),
        out_shape=tuple(sent),
        in_specs=[ANY] * len(after) + [SMEM, VMEM],
        out_specs=(VMEM,) * len(sent),
        scratch_shapes=[
            pltpu.VMEM((slabs, TILE), jnp.int32),
            pltpu.SMEM((slabs,), jnp.int32),
        ],
        compiler_params=pltpu.CompilerParams(vmem_limit_bytes=VMEM_BYTES),
        cost_estimate=cost(
            flops=0, bytes_accessed=2 * owned.size * 2, transcendentals=0
        ),
        name="pack",
    )(*after, dest, owned)
    return [outs[part * CORES : (part + 1) * CORES] for part in range(parts)]


def merge_kernel(same_ref, other_ref, *out_refs):
    span = same_ref.shape[0] // len(out_refs)
    for chip, out_ref in enumerate(out_refs):
        out_ref[:span] = same_ref[chip * span : (chip + 1) * span]
        out_ref[span:] = other_ref[chip * span : (chip + 1) * span]


def merge(same, other, chips):
    tiles, rows, width = same.shape
    out = jax.ShapeDtypeStruct((CORES * tiles // chips, rows, width), same.dtype)
    return pl.pallas_call(
        merge_kernel,
        out_shape=(out,) * chips,
        in_specs=[VMEM, VMEM],
        out_specs=(VMEM,) * chips,
        compiler_params=pltpu.CompilerParams(vmem_limit_bytes=VMEM_BYTES),
        cost_estimate=cost(flops=0, bytes_accessed=8 * same.size, transcendentals=0),
        name="merge",
    )(same, other)


def settle_kernel(chips, capacity, first, *refs):
    if first:
        moved_refs, out_refs, meta_ref, ids_ref = refs[:chips], refs[chips:-2], refs[-2], refs[-1]
        span = moved_refs[0].shape[0] // CORES
        for source in range(chips * CORES):
            at = source % CORES * span + span - 1
            tile = moved_refs[source // CORES][at].astype(jnp.float32)
            ids_ref[source : source + 1, :] = tile[:1].astype(jnp.int32)
        pltpu.sync_copy(ids_ref, meta_ref)
    else:
        meta_ref, moved_refs, out_refs = refs[0], refs[1 : 1 + chips], refs[1 + chips :]
        span = moved_refs[0].shape[0] // CORES
    shares = len(out_refs)
    mine = lax.axis_index("snap")
    for source in range(chips * CORES):
        moved_ref = moved_refs[source // CORES]

        def place(rank, _):
            block = meta_ref[source, rank]

            @pl.when(block >= 0)
            def _():
                at = source % CORES * span + rank * shares
                for r in range(shares):
                    out_refs[r][block] = moved_ref[at + (mine ^ r)]

            return 0

        lax.fori_loop(0, capacity, place, 0, unroll=4)


def settle(meta, moved, capacity, per_slab, shares, after=()):
    first = meta is None
    chips = len(moved)
    rows, width = moved[0].shape[1:]
    pieces = (jax.ShapeDtypeStruct((per_slab, rows, width), moved[0].dtype),) * shares
    ids = jax.ShapeDtypeStruct((chips * CORES, TILE), jnp.int32)
    outs = pl.pallas_call(
        lambda *refs: settle_kernel(chips, capacity, first, *refs[len(after) :]),
        out_shape=pieces + ((ids,) if first else ()),
        in_specs=[ANY] * len(after) + ([] if first else [SMEM]) + [VMEM] * chips,
        out_specs=(VMEM,) * shares + ((SMEM,) if first else ()),
        scratch_shapes=[pltpu.VMEM((chips * CORES, TILE), jnp.int32)] if first else [],
        compiler_params=pltpu.CompilerParams(vmem_limit_bytes=VMEM_BYTES),
        cost_estimate=cost(
            flops=0, bytes_accessed=2 * chips * moved[0].size, transcendentals=0
        ),
        name="settle",
    )(*after, *([] if first else [meta]), *moved)
    return outs[:shares], (outs[shares] if first else meta)


def whole_rows(refs):
    blocks, rows, width = refs[0].shape
    return jnp.concatenate([ref[...].reshape(blocks * rows, width) for ref in refs], axis=1)


def tile_of(row, lane, tiles):
    return row * tiles - lax.div(row * (row - 1), 2) + lane - row


def gram_kernel(parts, shares, *refs):
    out_ref, acc_ref = refs[-2:]
    step = pl.program_id(0)

    @pl.when(step == 0)
    def _():
        acc_ref[...] = jnp.zeros_like(acc_ref)

    for part in range(parts):
        cells = whole_rows(refs[part * shares : (part + 1) * shares])
        acc_ref[...] += lax.dot_general(
            cells, cells, ROWS_BY_ROWS, preferred_element_type=jnp.float32
        )

    @pl.when(step == pl.num_programs(0) - 1)
    def _():
        mine = lax.axis_index("snap")
        for a in range(shares):
            for b in range(shares):
                row, lane = mine ^ a, mine ^ b

                @pl.when(row <= lane)
                def _():
                    out_ref[tile_of(row, lane, shares)] = acc_ref[
                        a * TILE : (a + 1) * TILE, b * TILE : (b + 1) * TILE
                    ]


def gram_blocks(cells, after, steps=4):
    shares = len(cells[0])
    blocks, rows, width = cells[0][0].shape
    pairs = shares * (shares + 1) // 2
    full = shares * width
    spec = pl.BlockSpec((blocks // steps, rows, width), lambda i: (i, 0, 0))
    return pl.pallas_call(
        lambda *refs: gram_kernel(len(cells), shares, *refs[len(after) :]),
        grid=(steps,),
        out_shape=jax.ShapeDtypeStruct((pairs, TILE, TILE), jnp.float32),
        in_specs=[ANY] * len(after) + [spec] * (len(cells) * shares),
        out_specs=pl.BlockSpec((pairs, TILE, TILE), lambda i: (0, 0, 0)),
        scratch_shapes=[pltpu.VMEM((full, full), jnp.float32)],
        compiler_params=pltpu.CompilerParams(vmem_limit_bytes=VMEM_BYTES),
        cost_estimate=cost(
            flops=2 * len(cells) * blocks * rows * full * full,
            bytes_accessed=2 * len(cells) * blocks * rows * full,
            transcendentals=0,
        ),
        name="gram_blocks",
    )(*after, *[piece for part in cells for piece in part])


def cross_kernel(parts, shares, *refs):
    out_ref, acc_ref = refs[-2:]
    step = pl.program_id(0)

    @pl.when(step == 0)
    def _():
        acc_ref[...] = jnp.zeros_like(acc_ref)

    for part in range(parts):
        x_refs = refs[part * shares : (part + 1) * shares]
        y_refs = refs[(parts + part) * shares : (parts + part + 1) * shares]
        acc_ref[...] += lax.dot_general(
            whole_rows(x_refs), whole_rows(y_refs), ROWS_BY_ROWS, preferred_element_type=jnp.float32
        )

    @pl.when(step == pl.num_programs(0) - 1)
    def _():
        mine = lax.axis_index("snap")
        for a in range(shares):
            rows = pl.ds(pl.multiple_of((mine ^ a) * TILE, TILE), TILE)
            for b in range(shares):
                lanes = pl.ds(pl.multiple_of((mine ^ b) * TILE, TILE), TILE)
                out_ref[rows, lanes] = acc_ref[
                    a * TILE : (a + 1) * TILE, b * TILE : (b + 1) * TILE
                ]


def cross_sum(x_cells, y_cells, after, steps=4):
    parts, shares = len(x_cells), len(x_cells[0])
    blocks, rows, width = x_cells[0][0].shape
    spec = pl.BlockSpec((blocks // steps, rows, width), lambda i: (i, 0, 0))
    full = shares * width
    return pl.pallas_call(
        lambda *refs: cross_kernel(parts, shares, *refs[len(after) :]),
        grid=(steps,),
        out_shape=jax.ShapeDtypeStruct((full, full), jnp.float32),
        in_specs=[ANY] * len(after) + [spec] * (2 * parts * shares),
        out_specs=pl.BlockSpec((full, full), lambda i: (0, 0)),
        scratch_shapes=[pltpu.VMEM((full, full), jnp.float32)],
        compiler_params=pltpu.CompilerParams(vmem_limit_bytes=VMEM_BYTES),
        cost_estimate=cost(
            flops=2 * parts * blocks * rows * full * full,
            bytes_accessed=4 * parts * blocks * rows * full,
            transcendentals=0,
        ),
        name="cross_sum",
    )(*after, *[piece for part in list(x_cells) + list(y_cells) for piece in part])


def three_terms(value):
    high = value.astype(jnp.bfloat16).astype(jnp.float32)
    rest = value - high
    middle = rest.astype(jnp.bfloat16).astype(jnp.float32)
    return high, middle, rest - middle


def lane_of(row, lane):
    return jnp.broadcast_to(row[:, lane : lane + 1], row.shape)


def row_of(ref, row):
    return jnp.broadcast_to(ref[row : row + 1, :], (GROUP, TILE))


def factor_tile(a_ref, w_ref, u_ref, v_ref):
    panels = TILE // GROUP
    a_rows = [row_of(a_ref, i) for i in range(GROUP)]
    w_rows = [row_of(w_ref, i) for i in range(GROUP)]
    for p in range(panels):
        base = p * GROUP
        small = {
            (i, k): lane_of(a_rows[i], base + k) for i in range(GROUP) for k in range(i, GROUP)
        }
        for j in range(GROUP):
            scale = lax.rsqrt(small[j, j])
            a_rows[j] = a_rows[j] * scale
            w_rows[j] = w_rows[j] * scale
            u_ref[base + j : base + j + 1, :] = a_rows[j][:1]
            v_ref[base + j : base + j + 1, :] = w_rows[j][:1]
            below = {k: small[j, k] * scale for k in range(j + 1, GROUP)}
            for k in range(j + 1, GROUP):
                for m in range(k, GROUP):
                    small[k, m] = small[k, m] - below[k] * below[m]
            for k in range(j + 1, GROUP):
                a_rows[k] = a_rows[k] - below[k] * a_rows[j]
                w_rows[k] = w_rows[k] - below[k] * w_rows[j]
        if p + 1 == panels:
            break
        after = base + GROUP
        next_a = [row_of(a_ref, after + i) for i in range(GROUP)]
        next_w = [row_of(w_ref, after + i) for i in range(GROUP)]
        for i in range(GROUP):
            for k in range(GROUP):
                factor = lane_of(a_rows[k], after + i)
                next_a[i] = next_a[i] - factor * a_rows[k]
                next_w[i] = next_w[i] - factor * w_rows[k]
        if p + 2 < panels:
            done = after + GROUP
            u = u_ref[base:after, :]
            v = v_ref[base:after, :]
            uh, um, ul = three_terms(u)
            vh, vm, vl = three_terms(v)
            left = jnp.concatenate([uh, uh, um, uh, ul, um], axis=0).astype(jnp.bfloat16)
            right_a = jnp.concatenate([uh, um, uh, ul, uh, um], axis=0)
            right_w = jnp.concatenate([vh, vm, vh, vl, vh, vm], axis=0)
            right = jnp.concatenate([right_a, right_w], axis=1).astype(jnp.bfloat16)
            update = lax.dot_general(
                left, right, ROWS_BY_ROWS, preferred_element_type=jnp.float32
            )
            a_ref[done:, :] = a_ref[done:, :] - update[done:, :TILE]
            w_ref[done:, :] = w_ref[done:, :] - update[done:, TILE:]
        a_rows, w_rows = next_a, next_w


def factor_step(tiles, b, wide, a_ref, w_ref, u_ref, v_ref):
    row = lax.broadcasted_iota(jnp.int32, (TILE, TILE), 0)
    lane = lax.broadcasted_iota(jnp.int32, (TILE, TILE), 1)
    a_ref[...] = wide[b, b]
    w_ref[...] = jnp.where(row == lane, 1.0, 0.0)
    factor_tile(a_ref, w_ref, u_ref, v_ref)
    inverse = v_ref[...]
    wide[b, b] = jnp.where(row <= lane, u_ref[...], 0.0)
    wide[b, tiles + b] = inverse
    for j in range(1, tiles):
        wide[b, b + j] = lax.dot(
            inverse, wide[b, b + j], precision=HIGHEST, preferred_element_type=jnp.float32
        )
    for r in range(b + 1, tiles):
        for c in list(range(r, tiles)) + list(range(tiles, tiles + b + 1)):
            update = lax.dot_general(
                wide[b, r],
                wide[b, c],
                ROWS_BY_ROWS,
                precision=HIGHEST,
                preferred_element_type=jnp.float32,
            )
            wide[r, c] = -update if c == tiles + b else wide[r, c] - update


def first_kernel(tiles, rows_total, g_ref, wide, *scratch):
    at = 0
    for a in range(tiles):
        for b in range(a, tiles):
            wide[a, b] = g_ref[at] / rows_total
            at += 1
    factor_step(tiles, 0, wide, *scratch)


def next_kernel(tiles, b, _, wide, *scratch):
    factor_step(tiles, b, wide, *scratch)


def last_kernel(tiles, wide, r_ref, inv_ref, hi_ref, mid_ref, lo_ref, *scratch):
    factor_step(tiles, tiles - 1, wide, *scratch)
    zero = jnp.zeros((TILE, TILE), jnp.float32)
    mine = lax.axis_index("snap")
    for a in range(tiles):
        rows = slice(a * TILE, (a + 1) * TILE)
        for b in range(tiles):
            lanes = slice(b * TILE, (b + 1) * TILE)
            r_ref[rows, lanes] = wide[a, b] if b >= a else zero
            value = wide[a, tiles + b] if b <= a else zero
            inv_ref[rows, lanes] = value
            high, middle, low = three_terms(value)
            lanes = pl.ds(pl.multiple_of((mine ^ b) * TILE, TILE), TILE)
            hi_ref[rows, lanes] = high.astype(jnp.bfloat16)
            mid_ref[rows, lanes] = middle.astype(jnp.bfloat16)
            lo_ref[rows, lanes] = low.astype(jnp.bfloat16)


def factor_call(kernel, out_shape, value, after, aliases, tiles):
    many = isinstance(out_shape, tuple)
    return pl.pallas_call(
        lambda *refs: kernel(*refs[len(after) :]),
        out_shape=out_shape,
        in_specs=[ANY] * len(after) + [VMEM],
        out_specs=(VMEM,) * len(out_shape) if many else VMEM,
        scratch_shapes=[pltpu.VMEM((TILE, TILE), jnp.float32)] * 4,
        input_output_aliases={len(after): 0} if aliases else {},
        compiler_params=pltpu.CompilerParams(vmem_limit_bytes=VMEM_BYTES),
        cost_estimate=cost(
            flops=7 * 10**9, bytes_accessed=value.size * 4, transcendentals=TILE
        ),
        name="factor",
    )(*after, value)


def factor_steps(blocks, tiles, rows_total, after):
    state = jax.ShapeDtypeStruct((tiles, 2 * tiles, TILE, TILE), jnp.float32)
    full = jax.ShapeDtypeStruct((tiles * TILE, tiles * TILE), jnp.float32)
    term = jax.ShapeDtypeStruct(full.shape, jnp.bfloat16)
    value = factor_call(
        lambda *refs: first_kernel(tiles, rows_total, *refs), state, blocks, after, False, tiles
    )
    for b in range(1, tiles - 1):
        after = yield value
        value = factor_call(
            lambda *refs: next_kernel(tiles, b, *refs), state, value, after, True, tiles
        )
    after = yield value
    yield factor_call(
        lambda *refs: last_kernel(tiles, *refs), (full, full, term, term, term), value, after, False, tiles
    )


def basis_kernel(*refs):
    hi_ref, mid_ref, lo_ref, out_ref = refs[-4:]
    cells = whole_rows(refs[:-4])
    total = lax.dot_general(
        cells, lo_ref[...], LANES_BY_LANES, preferred_element_type=jnp.float32
    )
    total += lax.dot_general(
        cells, mid_ref[...], LANES_BY_LANES, preferred_element_type=jnp.float32
    )
    total += lax.dot_general(
        cells, hi_ref[...], LANES_BY_LANES, preferred_element_type=jnp.float32
    )
    out_ref[:, 0] = total.reshape(out_ref.shape[0], *out_ref.shape[2:])


def basis(cells, terms, part, parts, filled, after, steps=4):
    shares = len(cells)
    blocks, rows, width = cells[0].shape
    full = shares * width
    spec = pl.BlockSpec((blocks // steps, rows, width), lambda i: (i, 0, 0))
    term = pl.BlockSpec((full, full), lambda i: (0, 0))
    unread = ([] if filled is None else [filled]) + list(after)
    return pl.pallas_call(
        lambda *refs: basis_kernel(*refs[len(unread) :]),
        grid=(steps,),
        out_shape=jax.ShapeDtypeStruct((blocks, parts, rows, full), jnp.float32),
        in_specs=[ANY] * len(unread) + [spec] * shares + [term] * 3,
        out_specs=pl.BlockSpec((blocks // steps, 1, rows, full), lambda i: (i, part, 0, 0)),
        input_output_aliases={} if filled is None else {0: 0},
        compiler_params=pltpu.CompilerParams(vmem_limit_bytes=VMEM_BYTES),
        cost_estimate=cost(
            flops=6 * blocks * rows * full * full,
            bytes_accessed=6 * blocks * rows * full,
            transcendentals=0,
        ),
        name="basis",
    )(*unread, *cells, *terms)


def sum_kernel(count, value_ref, out_ref):
    rows = out_ref.shape[0]
    total = value_ref[:rows]
    for i in range(1, count):
        total += value_ref[i * rows : (i + 1) * rows]
    out_ref[...] = total


def sum_pieces(value, count, after):
    rows, lanes = value.shape
    return pl.pallas_call(
        lambda *refs: sum_kernel(count, *refs[len(after) :]),
        out_shape=jax.ShapeDtypeStruct((rows // count, lanes), value.dtype),
        in_specs=[ANY] * len(after) + [VMEM],
        out_specs=VMEM,
        cost_estimate=cost(flops=value.size, bytes_accessed=4 * value.size, transcendentals=0),
        name="sum_pieces",
    )(*after, value)


def add_kernel(one_ref, two_ref, out_ref):
    out_ref[...] = one_ref[...] + two_ref[...]


def add(one, two, after):
    return pl.pallas_call(
        lambda *refs: add_kernel(*refs[len(after) :]),
        out_shape=jax.ShapeDtypeStruct(one.shape, one.dtype),
        in_specs=[ANY] * len(after) + [VMEM, VMEM],
        out_specs=VMEM,
        cost_estimate=cost(flops=one.size, bytes_accessed=12 * one.size, transcendentals=0),
        name="add",
    )(*after, one, two)


def swap(value, axis, mask):
    return lax.ppermute(value, axis, [(i, i ^ mask) for i in range(lax.axis_size(axis))])


def body(owned_x, owned_y, patch_dest):
    slabs = lax.axis_size("space")
    shares = lax.axis_size("snap")
    slots, patch, width = owned_x.shape
    per_slab = slots // 2
    parts = patch // shares // CELL_TILE
    rows_total = slabs * per_slab * patch
    full = shares * width
    tiles = full // TILE
    pairs = tiles * (tiles + 1) // 2

    def parted(owned):
        return owned.reshape(slots, shares, parts, CELL_TILE, width)

    def merged(part):
        return merge(part[0], swap(part[1], "space", 1), slabs // CORES)

    def to_chips(joined):
        return [joined[0]] + [swap(joined[m], "space", CORES * m) for m in range(1, len(joined))]

    def to_rows(pieces):
        return [pieces[0]] + [swap(pieces[r], "snap", r) for r in range(1, shares)]

    def place(meta, moved, after):
        return settle(meta, moved, slots // slabs, per_slab, shares, after)

    def to_pieces(value):
        return lax.all_to_all(value, "space", split_axis=0, concat_axis=0, tiled=True)

    def hops():
        hop = 1
        while hop < shares:
            yield hop
            hop *= 2

    sent_x = pack(patch_dest, parted(owned_x), slabs, per_slab, True)
    joined_x = [merged(part) for part in sent_x]
    moved_x = [to_chips(joined) for joined in joined_x]
    sent_y = pack(patch_dest, parted(owned_y), slabs, per_slab, False)
    joined_y = [merged(part) for part in sent_y]
    moved_y = [to_chips(joined) for joined in joined_y]

    pieces, meta = place(None, moved_x[0], [joined[0] for joined in joined_x[1:]] + [sent_y[0][0]])
    x_cells = [to_rows(pieces)]
    for moved in moved_x[1:]:
        pieces, _ = place(meta, moved, x_cells[-1][1:] + moved_y[0][1:2])
        x_cells.append(to_rows(pieces))
    gram_local = gram_blocks(x_cells, [joined[0] for joined in joined_y[1:]])
    gram = to_pieces(gram_local.reshape(pairs * TILE, TILE))
    pieces, _ = place(meta, moved_y[0], x_cells[-1][1:])
    y_cells = [to_rows(pieces)]
    gram = sum_pieces(gram, slabs, pieces[:1])
    for hop in hops():
        gram = add(gram, swap(gram, "snap", hop), y_cells[0][1:2] if hop == 1 else y_cells[0][2:] + moved_y[1][1:])
    gram = lax.all_gather(gram, "space", axis=0, tiled=True)
    for moved in moved_y[1:]:
        pieces, _ = place(meta, moved, y_cells[-1][1:])
        y_cells.append(to_rows(pieces))

    steps = factor_steps(gram.reshape(pairs, TILE, TILE), tiles, rows_total, pieces[:1])
    state = next(steps)
    for _ in range(tiles - 2):
        state = steps.send([])
    cross_local = cross_sum(x_cells, y_cells, [state])
    cross = to_pieces(cross_local)
    r_factor, inverse, *terms = steps.send([cross_local])

    q_basis = basis(x_cells[0], terms, 0, parts, None, [])
    cross = sum_pieces(cross, slabs, [q_basis])
    for part in range(1, parts):
        q_basis = basis(x_cells[part], terms, part, parts, q_basis, [cross])
    for hop in hops():
        cross = add(cross, swap(cross, "snap", hop), [q_basis] if hop == 1 else [])
    cross = lax.all_gather(cross, "space", axis=0, tiled=True)
    projection = jnp.dot(inverse, cross, precision=HIGHEST) / math.sqrt(rows_total)
    return q_basis.reshape(per_slab, patch // shares, full), r_factor, projection


def solution(mesh):
    in_specs = (P("space", None, "snap"), P("space", None, "snap"), P("space"))
    out_specs = (P("space", "snap", None), P(), P())
    return jax.shard_map(body, mesh=mesh, in_specs=in_specs, out_specs=out_specs, check_vma=False)
```

```python
import math

import jax
import jax.numpy as jnp
from jax import lax
from jax.experimental import pallas as pl
from jax.experimental.pallas import tpu as pltpu
from jax.sharding import PartitionSpec as P

TILE = 128
GROUP = 8
CORES = 2
CELL_TILE = 16
VMEM_BYTES = 32 * 1024 * 1024
HIGHEST = lax.Precision.HIGHEST
SMEM = pl.BlockSpec(memory_space=pltpu.SMEM)
VMEM = pl.BlockSpec(memory_space=pltpu.VMEM)
ANY = pl.BlockSpec(memory_space=pl.ANY)
ROWS_BY_ROWS = (((0,), (0,)), ((), ()))
LANES_BY_LANES = (((1,), (1,)), ((), ()))


def cost(flops, bytes_accessed, transcendentals):
    return pl.CostEstimate(
        flops=flops,
        bytes_accessed=bytes_accessed,
        transcendentals=transcendentals,
    )


def pack_kernel(slabs, capacity, per_slab, parts, dest_ref, owned_ref, *refs):
    out_refs, (ids_ref, count_ref) = refs[: 2 * parts], refs[2 * parts :]
    chips = slabs // CORES
    shares = owned_ref.shape[1]
    used = capacity * shares
    me = lax.axis_index("space")
    lane = lax.broadcasted_iota(jnp.int32, (1, TILE), 1)
    ids_ref[...] = jnp.full_like(ids_ref, -1)
    for slab in range(slabs):
        count_ref[slab] = 0

    def place(i, _):
        block = dest_ref[i]

        @pl.when(block >= 0)
        def _():
            slab = lax.div(block, per_slab)
            rank = count_ref[slab]
            count_ref[slab] = rank + 1
            here = pl.ds(slab, 1)
            ids_ref[here, :] = jnp.where(lane == rank, block - slab * per_slab, ids_ref[here, :])
            away = slab ^ me
            chip = lax.shift_right_logical(away, 1)
            for core in range(CORES):

                @pl.when((away & 1) == core)
                def _():
                    for part in range(parts):
                        out_ref = out_refs[part * CORES + core]
                        at = chip * (out_ref.shape[0] // chips) + rank * shares
                        out_ref[pl.ds(at, shares)] = owned_ref[i, :, part]

        return 0

    lax.fori_loop(0, dest_ref.shape[0], place, 0, unroll=2)
    for away in range(slabs):
        for part in range(parts):
            out_ref = out_refs[part * CORES + away % CORES]
            span = out_ref.shape[0] // chips
            if span > used:
                ids = ids_ref[pl.ds(me ^ away, 1), :].astype(jnp.float32)
                tile = jnp.broadcast_to(ids, out_ref.shape[1:]).astype(out_ref.dtype)
                out_ref[away // CORES * span + used] = tile


def pack(dest, owned, slabs, per_slab, with_ids, after=()):
    slots, shares, parts, rows, width = owned.shape
    chips = slabs // CORES
    capacity = slots // slabs
    sent = []
    for part in range(parts):
        span = capacity * shares + (1 if with_ids and part == 0 else 0)
        sent += [jax.ShapeDtypeStruct((chips * span, rows, width), owned.dtype)] * CORES
    outs = pl.pallas_call(
        lambda *refs: pack_kernel(slabs, capacity, per_slab, parts, *refs[len(after) :]),
        out_shape=tuple(sent),
        in_specs=[ANY] * len(after) + [SMEM, VMEM],
        out_specs=(VMEM,) * len(sent),
        scratch_shapes=[
            pltpu.VMEM((slabs, TILE), jnp.int32),
            pltpu.SMEM((slabs,), jnp.int32),
        ],
        compiler_params=pltpu.CompilerParams(vmem_limit_bytes=VMEM_BYTES),
        cost_estimate=cost(
            flops=0, bytes_accessed=2 * owned.size * 2, transcendentals=0
        ),
        name="pack",
    )(*after, dest, owned)
    return [outs[part * CORES : (part + 1) * CORES] for part in range(parts)]


def merge_kernel(same_ref, other_ref, *out_refs):
    span = same_ref.shape[0] // len(out_refs)
    for chip, out_ref in enumerate(out_refs):
        out_ref[:span] = same_ref[chip * span : (chip + 1) * span]
        out_ref[span:] = other_ref[chip * span : (chip + 1) * span]


def merge(same, other, chips):
    tiles, rows, width = same.shape
    out = jax.ShapeDtypeStruct((CORES * tiles // chips, rows, width), same.dtype)
    return pl.pallas_call(
        merge_kernel,
        out_shape=(out,) * chips,
        in_specs=[VMEM, VMEM],
        out_specs=(VMEM,) * chips,
        compiler_params=pltpu.CompilerParams(vmem_limit_bytes=VMEM_BYTES),
        cost_estimate=cost(flops=0, bytes_accessed=8 * same.size, transcendentals=0),
        name="merge",
    )(same, other)


def settle_kernel(chips, capacity, first, joint, *refs):
    if first:
        moved_refs, out_refs, meta_ref, ids_ref = refs[:chips], refs[chips:-2], refs[-2], refs[-1]
        span = moved_refs[0].shape[0] // CORES
        for source in range(chips * CORES):
            at = source % CORES * span + span - 1
            tile = moved_refs[source // CORES][at].astype(jnp.float32)
            ids_ref[source : source + 1, :] = tile[:1].astype(jnp.int32)
        pltpu.sync_copy(ids_ref, meta_ref)
    else:
        meta_ref, moved_refs, out_refs = refs[0], refs[1 : 1 + chips], refs[1 + chips :]
        span = moved_refs[0].shape[0] // CORES
    shares = out_refs[0].shape[0] if joint else len(out_refs)
    mine = lax.axis_index("snap")
    for source in range(chips * CORES):
        moved_ref = moved_refs[source // CORES]

        def place(rank, _):
            block = meta_ref[source, rank]

            @pl.when(block >= 0)
            def _():
                at = source % CORES * span + rank * shares
                if joint:
                    out_refs[0][:, block] = moved_ref[pl.ds(at, shares)]
                else:
                    for r in range(shares):
                        out_refs[r][block] = moved_ref[at + (mine ^ r)]

            return 0

        lax.fori_loop(0, capacity, place, 0, unroll=4)


def settle(meta, moved, capacity, per_slab, shares, joint, after=()):
    first = meta is None
    chips = len(moved)
    rows, width = moved[0].shape[1:]
    if joint:
        pieces = (jax.ShapeDtypeStruct((shares, per_slab, rows, width), moved[0].dtype),)
    else:
        pieces = (jax.ShapeDtypeStruct((per_slab, rows, width), moved[0].dtype),) * shares
    ids = jax.ShapeDtypeStruct((chips * CORES, TILE), jnp.int32)
    outs = pl.pallas_call(
        lambda *refs: settle_kernel(chips, capacity, first, joint, *refs[len(after) :]),
        out_shape=pieces + ((ids,) if first else ()),
        in_specs=[ANY] * len(after) + ([] if first else [SMEM]) + [VMEM] * chips,
        out_specs=(VMEM,) * len(pieces) + ((SMEM,) if first else ()),
        scratch_shapes=[pltpu.VMEM((chips * CORES, TILE), jnp.int32)] if first else [],
        compiler_params=pltpu.CompilerParams(vmem_limit_bytes=VMEM_BYTES),
        cost_estimate=cost(
            flops=0, bytes_accessed=2 * chips * moved[0].size, transcendentals=0
        ),
        name="settle",
    )(*after, *([] if first else [meta]), *moved)
    return outs[: len(pieces)], (outs[-1] if first else meta)


def whole_rows(refs):
    blocks, rows, width = refs[0].shape
    return jnp.concatenate([ref[...].reshape(blocks * rows, width) for ref in refs], axis=1)


def joint_rows(ref):
    return whole_rows([ref.at[share] for share in range(ref.shape[0])])


def gram_kernel(parts, *refs):
    out_ref = refs[-1]
    shares = refs[0].shape[0]

    @pl.when(pl.program_id(0) == 0)
    def _():
        out_ref[...] = jnp.zeros_like(out_ref)

    for part in range(parts):
        cells = joint_rows(refs[part])
        at = 0
        for a in range(shares):
            product = lax.dot_general(
                cells[:, a * TILE : (a + 1) * TILE],
                cells[:, a * TILE :],
                ROWS_BY_ROWS,
                preferred_element_type=jnp.float32,
            )
            for b in range(a, shares):
                out_ref[at] += product[:, (b - a) * TILE : (b - a + 1) * TILE]
                at += 1


def gram_blocks(cells, after, steps=4):
    shares, blocks, rows, width = cells[0].shape
    pairs = shares * (shares + 1) // 2
    full = shares * width
    spec = pl.BlockSpec((shares, blocks // steps, rows, width), lambda i: (0, i, 0, 0))
    return pl.pallas_call(
        lambda *refs: gram_kernel(len(cells), *refs[len(after) :]),
        grid=(steps,),
        out_shape=jax.ShapeDtypeStruct((pairs, TILE, TILE), jnp.float32),
        in_specs=[ANY] * len(after) + [spec] * len(cells),
        out_specs=pl.BlockSpec((pairs, TILE, TILE), lambda i: (0, 0, 0)),
        compiler_params=pltpu.CompilerParams(vmem_limit_bytes=VMEM_BYTES),
        cost_estimate=cost(
            flops=2 * len(cells) * blocks * rows * full * full,
            bytes_accessed=2 * len(cells) * blocks * rows * full,
            transcendentals=0,
        ),
        name="gram_blocks",
    )(*after, *cells)


def cross_kernel(parts, shares, *refs):
    out_ref, acc_ref = refs[-2:]
    step = pl.program_id(0)

    @pl.when(step == 0)
    def _():
        acc_ref[...] = jnp.zeros_like(acc_ref)

    for part in range(parts):
        y_refs = refs[parts + part * shares : parts + (part + 1) * shares]
        acc_ref[...] += lax.dot_general(
            joint_rows(refs[part]),
            whole_rows(y_refs),
            ROWS_BY_ROWS,
            preferred_element_type=jnp.float32,
        )

    @pl.when(step == pl.num_programs(0) - 1)
    def _():
        mine = lax.axis_index("snap")
        for b in range(shares):
            lanes = pl.ds(pl.multiple_of((mine ^ b) * TILE, TILE), TILE)
            out_ref[:, lanes] = acc_ref[:, b * TILE : (b + 1) * TILE]


def cross_sum(x_cells, y_cells, after, steps=4):
    parts = len(x_cells)
    shares, blocks, rows, width = x_cells[0].shape
    spec = pl.BlockSpec((blocks // steps, rows, width), lambda i: (i, 0, 0))
    joint = pl.BlockSpec((shares, blocks // steps, rows, width), lambda i: (0, i, 0, 0))
    full = shares * width
    return pl.pallas_call(
        lambda *refs: cross_kernel(parts, shares, *refs[len(after) :]),
        grid=(steps,),
        out_shape=jax.ShapeDtypeStruct((full, full), jnp.float32),
        in_specs=[ANY] * len(after) + [joint] * parts + [spec] * (parts * shares),
        out_specs=pl.BlockSpec((full, full), lambda i: (0, 0)),
        scratch_shapes=[pltpu.VMEM((full, full), jnp.float32)],
        compiler_params=pltpu.CompilerParams(vmem_limit_bytes=VMEM_BYTES),
        cost_estimate=cost(
            flops=2 * parts * blocks * rows * full * full,
            bytes_accessed=4 * parts * blocks * rows * full,
            transcendentals=0,
        ),
        name="cross_sum",
    )(*after, *x_cells, *[piece for part in y_cells for piece in part])


def three_terms(value):
    high = value.astype(jnp.bfloat16).astype(jnp.float32)
    rest = value - high
    middle = rest.astype(jnp.bfloat16).astype(jnp.float32)
    return high, middle, rest - middle


def lane_of(row, lane):
    return jnp.broadcast_to(row[:, lane : lane + 1], row.shape)


def row_of(ref, row):
    return jnp.broadcast_to(ref[row : row + 1, :], (GROUP, TILE))


def factor_tile(a_ref, w_ref, u_ref, v_ref):
    panels = TILE // GROUP
    a_rows = [row_of(a_ref, i) for i in range(GROUP)]
    w_rows = [row_of(w_ref, i) for i in range(GROUP)]
    for p in range(panels):
        base = p * GROUP
        small = {
            (i, k): lane_of(a_rows[i], base + k) for i in range(GROUP) for k in range(i, GROUP)
        }
        for j in range(GROUP):
            scale = lax.rsqrt(small[j, j])
            a_rows[j] = a_rows[j] * scale
            w_rows[j] = w_rows[j] * scale
            u_ref[base + j : base + j + 1, :] = a_rows[j][:1]
            v_ref[base + j : base + j + 1, :] = w_rows[j][:1]
            below = {k: small[j, k] * scale for k in range(j + 1, GROUP)}
            for k in range(j + 1, GROUP):
                for m in range(k, GROUP):
                    small[k, m] = small[k, m] - below[k] * below[m]
            for k in range(j + 1, GROUP):
                a_rows[k] = a_rows[k] - below[k] * a_rows[j]
                w_rows[k] = w_rows[k] - below[k] * w_rows[j]
        if p + 1 == panels:
            break
        after = base + GROUP
        next_a = [row_of(a_ref, after + i) for i in range(GROUP)]
        next_w = [row_of(w_ref, after + i) for i in range(GROUP)]
        for i in range(GROUP):
            for k in range(GROUP):
                factor = lane_of(a_rows[k], after + i)
                next_a[i] = next_a[i] - factor * a_rows[k]
                next_w[i] = next_w[i] - factor * w_rows[k]
        if p + 2 < panels:
            done = after + GROUP
            u = u_ref[base:after, :]
            v = v_ref[base:after, :]
            uh, um, ul = three_terms(u)
            vh, vm, vl = three_terms(v)
            left = jnp.concatenate([uh, uh, um, uh, ul, um], axis=0).astype(jnp.bfloat16)
            right_a = jnp.concatenate([uh, um, uh, ul, uh, um], axis=0)
            right_w = jnp.concatenate([vh, vm, vh, vl, vh, vm], axis=0)
            right = jnp.concatenate([right_a, right_w], axis=1).astype(jnp.bfloat16)
            update = lax.dot_general(
                left, right, ROWS_BY_ROWS, preferred_element_type=jnp.float32
            )
            a_ref[done:, :] = a_ref[done:, :] - update[done:, :TILE]
            w_ref[done:, :] = w_ref[done:, :] - update[done:, TILE:]
        a_rows, w_rows = next_a, next_w


def factor_step(tiles, b, wide, a_ref, w_ref, u_ref, v_ref):
    row = lax.broadcasted_iota(jnp.int32, (TILE, TILE), 0)
    lane = lax.broadcasted_iota(jnp.int32, (TILE, TILE), 1)
    a_ref[...] = wide[b, b]
    w_ref[...] = jnp.where(row == lane, 1.0, 0.0)
    factor_tile(a_ref, w_ref, u_ref, v_ref)
    inverse = v_ref[...]
    wide[b, b] = jnp.where(row <= lane, u_ref[...], 0.0)
    wide[b, tiles + b] = inverse
    for j in range(1, tiles):
        wide[b, b + j] = lax.dot(
            inverse, wide[b, b + j], precision=HIGHEST, preferred_element_type=jnp.float32
        )
    for r in range(b + 1, tiles):
        for c in list(range(r, tiles)) + list(range(tiles, tiles + b + 1)):
            update = lax.dot_general(
                wide[b, r],
                wide[b, c],
                ROWS_BY_ROWS,
                precision=HIGHEST,
                preferred_element_type=jnp.float32,
            )
            wide[r, c] = -update if c == tiles + b else wide[r, c] - update


def first_kernel(tiles, rows_total, g_ref, wide, *scratch):
    at = 0
    for a in range(tiles):
        for b in range(a, tiles):
            wide[a, b] = g_ref[at] / rows_total
            at += 1
    factor_step(tiles, 0, wide, *scratch)


def next_kernel(tiles, b, _, wide, *scratch):
    factor_step(tiles, b, wide, *scratch)


def last_kernel(tiles, wide, r_ref, inv_ref, hi_ref, mid_ref, lo_ref, *scratch):
    factor_step(tiles, tiles - 1, wide, *scratch)
    zero = jnp.zeros((TILE, TILE), jnp.float32)
    for a in range(tiles):
        rows = slice(a * TILE, (a + 1) * TILE)
        for b in range(tiles):
            lanes = slice(b * TILE, (b + 1) * TILE)
            r_ref[rows, lanes] = wide[a, b] if b >= a else zero
            value = wide[a, tiles + b] if b <= a else zero
            inv_ref[rows, lanes] = value
            high, middle, low = three_terms(value)
            hi_ref[rows, lanes] = high.astype(jnp.bfloat16)
            mid_ref[rows, lanes] = middle.astype(jnp.bfloat16)
            lo_ref[rows, lanes] = low.astype(jnp.bfloat16)


def factor_call(kernel, out_shape, value, after, aliases, tiles):
    many = isinstance(out_shape, tuple)
    return pl.pallas_call(
        lambda *refs: kernel(*refs[len(after) :]),
        out_shape=out_shape,
        in_specs=[ANY] * len(after) + [VMEM],
        out_specs=(VMEM,) * len(out_shape) if many else VMEM,
        scratch_shapes=[pltpu.VMEM((TILE, TILE), jnp.float32)] * 4,
        input_output_aliases={len(after): 0} if aliases else {},
        compiler_params=pltpu.CompilerParams(vmem_limit_bytes=VMEM_BYTES),
        cost_estimate=cost(
            flops=7 * 10**9, bytes_accessed=value.size * 4, transcendentals=TILE
        ),
        name="factor",
    )(*after, value)


def factor_steps(blocks, tiles, rows_total, after):
    state = jax.ShapeDtypeStruct((tiles, 2 * tiles, TILE, TILE), jnp.float32)
    full = jax.ShapeDtypeStruct((tiles * TILE, tiles * TILE), jnp.float32)
    term = jax.ShapeDtypeStruct(full.shape, jnp.bfloat16)
    value = factor_call(
        lambda *refs: first_kernel(tiles, rows_total, *refs), state, blocks, after, False, tiles
    )
    for b in range(1, tiles - 1):
        after = yield value
        value = factor_call(
            lambda *refs: next_kernel(tiles, b, *refs), state, value, after, True, tiles
        )
    after = yield value
    yield factor_call(
        lambda *refs: last_kernel(tiles, *refs), (full, full, term, term, term), value, after, False, tiles
    )


def basis_kernel(*refs):
    hi_ref, mid_ref, lo_ref, out_ref = refs[-4:]
    cells = joint_rows(refs[0])
    total = lax.dot_general(
        cells, lo_ref[...], LANES_BY_LANES, preferred_element_type=jnp.float32
    )
    total += lax.dot_general(
        cells, mid_ref[...], LANES_BY_LANES, preferred_element_type=jnp.float32
    )
    total += lax.dot_general(
        cells, hi_ref[...], LANES_BY_LANES, preferred_element_type=jnp.float32
    )
    out_ref[:, 0] = total.reshape(out_ref.shape[0], *out_ref.shape[2:])


def basis(cells, terms, part, parts, filled, after, steps=4):
    shares, blocks, rows, width = cells.shape
    full = shares * width
    spec = pl.BlockSpec((shares, blocks // steps, rows, width), lambda i: (0, i, 0, 0))
    term = pl.BlockSpec((full, full), lambda i: (0, 0))
    unread = ([] if filled is None else [filled]) + list(after)
    return pl.pallas_call(
        lambda *refs: basis_kernel(*refs[len(unread) :]),
        grid=(steps,),
        out_shape=jax.ShapeDtypeStruct((blocks, parts, rows, full), jnp.float32),
        in_specs=[ANY] * len(unread) + [spec] + [term] * 3,
        out_specs=pl.BlockSpec((blocks // steps, 1, rows, full), lambda i: (i, part, 0, 0)),
        input_output_aliases={} if filled is None else {0: 0},
        compiler_params=pltpu.CompilerParams(vmem_limit_bytes=VMEM_BYTES),
        cost_estimate=cost(
            flops=6 * blocks * rows * full * full,
            bytes_accessed=6 * blocks * rows * full,
            transcendentals=0,
        ),
        name="basis",
    )(*unread, cells, *terms)


def sum_kernel(count, value_ref, out_ref):
    rows = out_ref.shape[0]
    total = value_ref[:rows]
    for i in range(1, count):
        total += value_ref[i * rows : (i + 1) * rows]
    out_ref[...] = total


def sum_pieces(value, count, after):
    rows, lanes = value.shape
    return pl.pallas_call(
        lambda *refs: sum_kernel(count, *refs[len(after) :]),
        out_shape=jax.ShapeDtypeStruct((rows // count, lanes), value.dtype),
        in_specs=[ANY] * len(after) + [VMEM],
        out_specs=VMEM,
        cost_estimate=cost(flops=value.size, bytes_accessed=4 * value.size, transcendentals=0),
        name="sum_pieces",
    )(*after, value)


def add_kernel(one_ref, two_ref, out_ref):
    out_ref[...] = one_ref[...] + two_ref[...]


def add(one, two, after):
    return pl.pallas_call(
        lambda *refs: add_kernel(*refs[len(after) :]),
        out_shape=jax.ShapeDtypeStruct(one.shape, one.dtype),
        in_specs=[ANY] * len(after) + [VMEM, VMEM],
        out_specs=VMEM,
        cost_estimate=cost(flops=one.size, bytes_accessed=12 * one.size, transcendentals=0),
        name="add",
    )(*after, one, two)


def join_kernel(*refs):
    rows = refs[0].shape[0]
    for i, ref in enumerate(refs[:-1]):
        refs[-1][i * rows : (i + 1) * rows] = ref[...]


def join(values):
    rows, lanes = values[0].shape
    return pl.pallas_call(
        join_kernel,
        out_shape=jax.ShapeDtypeStruct((len(values) * rows, lanes), values[0].dtype),
        in_specs=[VMEM] * len(values),
        out_specs=VMEM,
        name="join",
    )(*values)


def projection_kernel(slabs, divisor, inverse_ref, same_ref, other_ref, out_ref, cross_ref):
    me = lax.axis_index("space")
    rows = cross_ref.shape[0] // slabs
    for away in range(slabs):
        at = pl.ds(pl.multiple_of((me ^ away) * rows, rows), rows)
        chip = slice(away // CORES * rows, (away // CORES + 1) * rows)
        cross_ref[at, :] = (other_ref if away % CORES else same_ref)[chip]
    out_ref[...] = (
        lax.dot(
            inverse_ref[...],
            cross_ref[...],
            precision=HIGHEST,
            preferred_element_type=jnp.float32,
        )
        / divisor
    )


def project(inverse, same, other, slabs, divisor):
    return pl.pallas_call(
        lambda *refs: projection_kernel(slabs, divisor, *refs),
        out_shape=jax.ShapeDtypeStruct(inverse.shape, jnp.float32),
        in_specs=[VMEM] * 3,
        out_specs=VMEM,
        scratch_shapes=[pltpu.VMEM(inverse.shape, jnp.float32)],
        compiler_params=pltpu.CompilerParams(vmem_limit_bytes=VMEM_BYTES),
        name="project",
    )(inverse, same, other)


def swap(value, axis, mask):
    return lax.ppermute(value, axis, [(i, i ^ mask) for i in range(lax.axis_size(axis))])


def body(owned_x, owned_y, patch_dest):
    slabs = lax.axis_size("space")
    shares = lax.axis_size("snap")
    slots, patch, width = owned_x.shape
    per_slab = slots // 2
    parts = patch // shares // CELL_TILE
    rows_total = slabs * per_slab * patch
    full = shares * width
    tiles = full // TILE
    pairs = tiles * (tiles + 1) // 2

    def parted(owned):
        return owned.reshape(slots, shares, parts, CELL_TILE, width)

    def merged(part):
        return merge(part[0], swap(part[1], "space", 1), slabs // CORES)

    def to_chips(joined):
        return [joined[0]] + [swap(joined[m], "space", CORES * m) for m in range(1, len(joined))]

    def to_rows(pieces):
        return [pieces[0]] + [swap(pieces[r], "snap", r) for r in range(1, shares)]

    def place(meta, moved, joint, after):
        return settle(meta, moved, slots // slabs, per_slab, shares, joint, after)

    def to_pieces(value):
        return lax.all_to_all(value, "space", split_axis=0, concat_axis=0, tiled=True)

    def hops():
        hop = 1
        while hop < shares:
            yield hop
            hop *= 2

    sent_x = pack(patch_dest, parted(owned_x), slabs, per_slab, True)
    joined_x = [merged(part) for part in sent_x]
    moved_x = [to_chips(joined) for joined in joined_x]
    sent_y = pack(patch_dest, parted(owned_y), slabs, per_slab, False)
    joined_y = [merged(part) for part in sent_y]
    moved_y = [to_chips(joined) for joined in joined_y]

    def to_joint_rows(pieces):
        return lax.all_to_all(pieces[0], "snap", split_axis=0, concat_axis=0, tiled=True)

    after = [joined[0] for joined in joined_x[1:]] + [sent_y[0][0]]
    pieces, meta = place(None, moved_x[0], True, after)
    x_cells = [to_joint_rows(pieces)]
    for moved in moved_x[1:]:
        pieces, _ = place(meta, moved, True, joined_y[0][:1])
        x_cells.append(to_joint_rows(pieces))
    gram_local = gram_blocks(x_cells, [joined[0] for joined in joined_y[1:]])
    gram = to_pieces(gram_local.reshape(pairs * TILE, TILE))
    pieces, _ = place(meta, moved_y[0], False, [])
    y_cells = [to_rows(pieces)]
    gram = sum_pieces(gram, slabs, pieces[:1])
    for hop in hops():
        gram = add(gram, swap(gram, "snap", hop), [])
    gram = lax.all_gather(gram, "space", axis=0, tiled=True)
    for moved in moved_y[1:]:
        pieces, _ = place(meta, moved, False, y_cells[-1][1:])
        y_cells.append(to_rows(pieces))

    steps = factor_steps(gram.reshape(pairs, TILE, TILE), tiles, rows_total, pieces[:1])
    state = next(steps)
    for _ in range(tiles - 2):
        state = steps.send([])
    cross_local = cross_sum(x_cells, y_cells, [state])
    cross = to_pieces(cross_local)
    r_factor, inverse, *terms = steps.send([cross_local])

    q_basis = basis(x_cells[0], terms, 0, parts, None, [])
    cross = sum_pieces(cross, slabs, [q_basis])
    for part in range(1, parts):
        q_basis = basis(x_cells[part], terms, part, parts, q_basis, [cross])
    for hop in hops():
        cross = add(cross, swap(cross, "snap", hop), [q_basis] if hop == 1 else [])
    same = join([cross] + [swap(cross, "space", m) for m in range(CORES, slabs, CORES)])
    projection = project(inverse, same, swap(same, "space", 1), slabs, math.sqrt(rows_total))
    return q_basis.reshape(per_slab, patch // shares, full), r_factor, projection


def solution(mesh):
    in_specs = (P("space", None, "snap"), P("space", None, "snap"), P("space"))
    out_specs = (P("space", "snap", None), P(), P())
    return jax.shard_map(body, mesh=mesh, in_specs=in_specs, out_specs=out_specs, check_vma=False)
```

```python
import math

import jax
import jax.numpy as jnp
from jax import lax
from jax.experimental import pallas as pl
from jax.experimental.pallas import tpu as pltpu
from jax.sharding import PartitionSpec as P

TILE = 128
GROUP = 8
CORES = 2
CELL_TILE = 16
VMEM_BYTES = 32 * 1024 * 1024
HIGHEST = lax.Precision.HIGHEST
SMEM = pl.BlockSpec(memory_space=pltpu.SMEM)
VMEM = pl.BlockSpec(memory_space=pltpu.VMEM)
ANY = pl.BlockSpec(memory_space=pl.ANY)
ROWS_BY_ROWS = (((0,), (0,)), ((), ()))
LANES_BY_LANES = (((1,), (1,)), ((), ()))


def cost(flops, bytes_accessed, transcendentals):
    return pl.CostEstimate(
        flops=flops,
        bytes_accessed=bytes_accessed,
        transcendentals=transcendentals,
    )


def pack_kernel(slabs, capacity, per_slab, dest_ref, owned_ref, *refs):
    out_refs, (ids_ref, count_ref) = refs[:CORES], refs[CORES:]
    chips = slabs // CORES
    tiles = owned_ref.shape[1]
    used = capacity * tiles
    span = out_refs[0].shape[0] // chips
    me = lax.axis_index("space")
    lane = lax.broadcasted_iota(jnp.int32, (1, TILE), 1)
    ids_ref[...] = jnp.full_like(ids_ref, -1)
    for slab in range(slabs):
        count_ref[slab] = 0

    def place(i, _):
        block = dest_ref[i]

        @pl.when(block >= 0)
        def _():
            slab = lax.div(block, per_slab)
            rank = count_ref[slab]
            count_ref[slab] = rank + 1
            here = pl.ds(slab, 1)
            ids_ref[here, :] = jnp.where(lane == rank, block - slab * per_slab, ids_ref[here, :])
            away = slab ^ me
            at = pl.ds(lax.shift_right_logical(away, 1) * span + rank * tiles, tiles)
            for core in range(CORES):

                @pl.when((away & 1) == core)
                def _():
                    out_refs[core][at] = owned_ref[i]

        return 0

    lax.fori_loop(0, dest_ref.shape[0], place, 0, unroll=2)
    if span > used:
        for away in range(slabs):
            out_ref = out_refs[away % CORES]
            ids = ids_ref[pl.ds(me ^ away, 1), :].astype(jnp.float32)
            tile = jnp.broadcast_to(ids, out_ref.shape[1:]).astype(out_ref.dtype)
            out_ref[away // CORES * span + used] = tile


def pack(dest, owned, slabs, per_slab, with_ids):
    slots, tiles, rows, width = owned.shape
    chips = slabs // CORES
    capacity = slots // slabs
    span = capacity * tiles + (1 if with_ids else 0)
    sent = jax.ShapeDtypeStruct((chips * span, rows, width), owned.dtype)
    return pl.pallas_call(
        lambda *refs: pack_kernel(slabs, capacity, per_slab, *refs),
        out_shape=(sent,) * CORES,
        in_specs=[SMEM, VMEM],
        out_specs=(VMEM,) * CORES,
        scratch_shapes=[
            pltpu.VMEM((slabs, TILE), jnp.int32),
            pltpu.SMEM((slabs,), jnp.int32),
        ],
        compiler_params=pltpu.CompilerParams(vmem_limit_bytes=VMEM_BYTES),
        cost_estimate=cost(flops=0, bytes_accessed=2 * owned.size * 2, transcendentals=0),
        name="pack",
    )(dest, owned)


def merge_kernel(same_ref, other_ref, *out_refs):
    span = same_ref.shape[0] // len(out_refs)
    for chip, out_ref in enumerate(out_refs):
        out_ref[:span] = same_ref[chip * span : (chip + 1) * span]
        out_ref[span:] = other_ref[chip * span : (chip + 1) * span]


def merge(same, other, chips, after):
    tiles, rows, width = same.shape
    out = jax.ShapeDtypeStruct((CORES * tiles // chips, rows, width), same.dtype)
    return pl.pallas_call(
        lambda *refs: merge_kernel(*refs[len(after) :]),
        out_shape=(out,) * chips,
        in_specs=[ANY] * len(after) + [VMEM, VMEM],
        out_specs=(VMEM,) * chips,
        compiler_params=pltpu.CompilerParams(vmem_limit_bytes=VMEM_BYTES),
        cost_estimate=cost(flops=0, bytes_accessed=8 * same.size, transcendentals=0),
        name="merge",
    )(*after, same, other)


def settle_kernel(chips, capacity, parts, part, *refs):
    first = part is None
    if first:
        moved_refs, (out_ref, meta_ref, ids_ref) = refs[:chips], refs[chips:]
        span = moved_refs[0].shape[0] // CORES
        for source in range(chips * CORES):
            at = source % CORES * span + span - 1
            tile = moved_refs[source // CORES][at].astype(jnp.float32)
            ids_ref[source : source + 1, :] = tile[:1].astype(jnp.int32)
        pltpu.sync_copy(ids_ref, meta_ref)
        shares = out_ref.shape[0]
    else:
        meta_ref, moved_refs, out_refs = refs[0], refs[1 : 1 + chips], refs[1 + chips :]
        span = moved_refs[0].shape[0] // CORES
        shares = len(out_refs)
    tiles = shares * parts
    rows = moved_refs[0].shape[1]
    mine = lax.axis_index("snap")
    for source in range(chips * CORES):
        moved_ref = moved_refs[source // CORES]

        def place(rank, _):
            block = meta_ref[source, rank]

            @pl.when(block >= 0)
            def _():
                at = source % CORES * span + rank * tiles
                for share in range(shares):
                    if first:
                        for k in range(parts):
                            cells = slice(k * rows, (k + 1) * rows)
                            out_ref[share, block, cells] = moved_ref[at + share * parts + k]
                    else:
                        cells = moved_ref[at + (mine ^ share) * parts + part]
                        out_refs[share][block] = cells

            return 0

        lax.fori_loop(0, capacity, place, 0, unroll=4)


def settle(meta, moved, capacity, per_slab, shares, parts, part, after):
    first = part is None
    chips = len(moved)
    rows, width = moved[0].shape[1:]
    if first:
        pieces = (
            jax.ShapeDtypeStruct((shares, per_slab, parts * rows, width), moved[0].dtype),
            jax.ShapeDtypeStruct((chips * CORES, TILE), jnp.int32),
        )
    else:
        pieces = (jax.ShapeDtypeStruct((per_slab, rows, width), moved[0].dtype),) * shares
    return pl.pallas_call(
        lambda *refs: settle_kernel(chips, capacity, parts, part, *refs[len(after) :]),
        out_shape=pieces,
        in_specs=[ANY] * len(after) + ([] if first else [SMEM]) + [VMEM] * chips,
        out_specs=(VMEM, SMEM) if first else (VMEM,) * shares,
        scratch_shapes=[pltpu.VMEM((chips * CORES, TILE), jnp.int32)] if first else [],
        compiler_params=pltpu.CompilerParams(vmem_limit_bytes=VMEM_BYTES),
        cost_estimate=cost(
            flops=0, bytes_accessed=2 * chips * moved[0].size, transcendentals=0
        ),
        name="settle",
    )(*after, *([] if first else [meta]), *moved)


def whole_rows(refs):
    blocks, rows, width = refs[0].shape
    return jnp.concatenate([ref[...].reshape(blocks * rows, width) for ref in refs], axis=1)


def joint_rows(ref):
    return whole_rows([ref.at[share] for share in range(ref.shape[0])])


def gram_kernel(x_ref, out_ref):
    shares = x_ref.shape[0]

    @pl.when(pl.program_id(0) == 0)
    def _():
        out_ref[...] = jnp.zeros_like(out_ref)

    cells = joint_rows(x_ref)
    at = 0
    for a in range(shares):
        product = lax.dot_general(
            cells[:, a * TILE : (a + 1) * TILE],
            cells[:, a * TILE :],
            ROWS_BY_ROWS,
            preferred_element_type=jnp.float32,
        )
        for b in range(a, shares):
            out_ref[at] += product[:, (b - a) * TILE : (b - a + 1) * TILE]
            at += 1


def gram_blocks(cells, after, steps=4):
    shares, blocks, rows, width = cells.shape
    pairs = shares * (shares + 1) // 2
    full = shares * width
    spec = pl.BlockSpec((shares, blocks // steps, rows, width), lambda i: (0, i, 0, 0))
    return pl.pallas_call(
        lambda *refs: gram_kernel(*refs[len(after) :]),
        grid=(steps,),
        out_shape=jax.ShapeDtypeStruct((pairs, TILE, TILE), jnp.float32),
        in_specs=[ANY] * len(after) + [spec],
        out_specs=pl.BlockSpec((pairs, TILE, TILE), lambda i: (0, 0, 0)),
        compiler_params=pltpu.CompilerParams(vmem_limit_bytes=VMEM_BYTES),
        cost_estimate=cost(
            flops=2 * blocks * rows * full * full,
            bytes_accessed=2 * blocks * rows * full,
            transcendentals=0,
        ),
        name="gram_blocks",
    )(*after, cells)


def cross_kernel(parts, shares, *refs):
    x_ref, (out_ref, acc_ref) = refs[0], refs[-2:]
    step = pl.program_id(0)

    @pl.when(step == 0)
    def _():
        acc_ref[...] = jnp.zeros_like(acc_ref)

    rows = x_ref.shape[2] // parts
    for part in range(parts):
        cells = slice(part * rows, (part + 1) * rows)
        acc_ref[...] += lax.dot_general(
            whole_rows([x_ref.at[share, :, cells] for share in range(shares)]),
            whole_rows(refs[1 + part * shares : 1 + (part + 1) * shares]),
            ROWS_BY_ROWS,
            preferred_element_type=jnp.float32,
        )

    @pl.when(step == pl.num_programs(0) - 1)
    def _():
        mine = lax.axis_index("snap")
        for b in range(shares):
            lanes = pl.ds(pl.multiple_of((mine ^ b) * TILE, TILE), TILE)
            out_ref[:, lanes] = acc_ref[:, b * TILE : (b + 1) * TILE]


def cross_sum(x_cells, y_cells, after, steps=4):
    parts = len(y_cells)
    shares, blocks, cells, width = x_cells.shape
    spec = pl.BlockSpec((blocks // steps, cells // parts, width), lambda i: (i, 0, 0))
    joint = pl.BlockSpec((shares, blocks // steps, cells, width), lambda i: (0, i, 0, 0))
    full = shares * width
    return pl.pallas_call(
        lambda *refs: cross_kernel(parts, shares, *refs[len(after) :]),
        grid=(steps,),
        out_shape=jax.ShapeDtypeStruct((full, full), jnp.float32),
        in_specs=[ANY] * len(after) + [joint] + [spec] * (parts * shares),
        out_specs=pl.BlockSpec((full, full), lambda i: (0, 0)),
        scratch_shapes=[pltpu.VMEM((full, full), jnp.float32)],
        compiler_params=pltpu.CompilerParams(vmem_limit_bytes=VMEM_BYTES),
        cost_estimate=cost(
            flops=2 * blocks * cells * full * full,
            bytes_accessed=4 * blocks * cells * full,
            transcendentals=0,
        ),
        name="cross_sum",
    )(*after, x_cells, *[piece for part in y_cells for piece in part])


def three_terms(value):
    high = value.astype(jnp.bfloat16).astype(jnp.float32)
    rest = value - high
    middle = rest.astype(jnp.bfloat16).astype(jnp.float32)
    return high, middle, rest - middle


def lane_of(row, lane):
    return jnp.broadcast_to(row[:, lane : lane + 1], row.shape)


def row_of(ref, row):
    return jnp.broadcast_to(ref[row : row + 1, :], (GROUP, TILE))


def factor_tile(a_ref, w_ref, u_ref, v_ref):
    panels = TILE // GROUP
    a_rows = [row_of(a_ref, i) for i in range(GROUP)]
    w_rows = [row_of(w_ref, i) for i in range(GROUP)]
    for p in range(panels):
        base = p * GROUP
        small = {
            (i, k): lane_of(a_rows[i], base + k) for i in range(GROUP) for k in range(i, GROUP)
        }
        for j in range(GROUP):
            scale = lax.rsqrt(small[j, j])
            a_rows[j] = a_rows[j] * scale
            w_rows[j] = w_rows[j] * scale
            u_ref[base + j : base + j + 1, :] = a_rows[j][:1]
            v_ref[base + j : base + j + 1, :] = w_rows[j][:1]
            below = {k: small[j, k] * scale for k in range(j + 1, GROUP)}
            for k in range(j + 1, GROUP):
                for m in range(k, GROUP):
                    small[k, m] = small[k, m] - below[k] * below[m]
            for k in range(j + 1, GROUP):
                a_rows[k] = a_rows[k] - below[k] * a_rows[j]
                w_rows[k] = w_rows[k] - below[k] * w_rows[j]
        if p + 1 == panels:
            break
        after = base + GROUP
        next_a = [row_of(a_ref, after + i) for i in range(GROUP)]
        next_w = [row_of(w_ref, after + i) for i in range(GROUP)]
        for i in range(GROUP):
            for k in range(GROUP):
                factor = lane_of(a_rows[k], after + i)
                next_a[i] = next_a[i] - factor * a_rows[k]
                next_w[i] = next_w[i] - factor * w_rows[k]
        if p + 2 < panels:
            done = after + GROUP
            u = u_ref[base:after, :]
            v = v_ref[base:after, :]
            uh, um, ul = three_terms(u)
            vh, vm, vl = three_terms(v)
            left = jnp.concatenate([uh, uh, um, uh, ul, um], axis=0).astype(jnp.bfloat16)
            right_a = jnp.concatenate([uh, um, uh, ul, uh, um], axis=0)
            right_w = jnp.concatenate([vh, vm, vh, vl, vh, vm], axis=0)
            right = jnp.concatenate([right_a, right_w], axis=1).astype(jnp.bfloat16)
            update = lax.dot_general(
                left, right, ROWS_BY_ROWS, preferred_element_type=jnp.float32
            )
            a_ref[done:, :] = a_ref[done:, :] - update[done:, :TILE]
            w_ref[done:, :] = w_ref[done:, :] - update[done:, TILE:]
        a_rows, w_rows = next_a, next_w


def factor_step(tiles, b, wide, a_ref, w_ref, u_ref, v_ref):
    row = lax.broadcasted_iota(jnp.int32, (TILE, TILE), 0)
    lane = lax.broadcasted_iota(jnp.int32, (TILE, TILE), 1)
    a_ref[...] = wide[b, b]
    w_ref[...] = jnp.where(row == lane, 1.0, 0.0)
    factor_tile(a_ref, w_ref, u_ref, v_ref)
    inverse = v_ref[...]
    wide[b, b] = jnp.where(row <= lane, u_ref[...], 0.0)
    wide[b, tiles + b] = inverse
    for j in range(1, tiles):
        wide[b, b + j] = lax.dot(
            inverse, wide[b, b + j], precision=HIGHEST, preferred_element_type=jnp.float32
        )
    for r in range(b + 1, tiles):
        for c in list(range(r, tiles)) + list(range(tiles, tiles + b + 1)):
            update = lax.dot_general(
                wide[b, r],
                wide[b, c],
                ROWS_BY_ROWS,
                precision=HIGHEST,
                preferred_element_type=jnp.float32,
            )
            wide[r, c] = -update if c == tiles + b else wide[r, c] - update


def first_kernel(tiles, rows_total, g_ref, wide, *scratch):
    at = 0
    for a in range(tiles):
        for b in range(a, tiles):
            wide[a, b] = g_ref[at] / rows_total
            at += 1
    factor_step(tiles, 0, wide, *scratch)


def next_kernel(tiles, b, _, wide, *scratch):
    factor_step(tiles, b, wide, *scratch)


def last_kernel(tiles, wide, r_ref, inv_ref, hi_ref, mid_ref, lo_ref, *scratch):
    factor_step(tiles, tiles - 1, wide, *scratch)
    zero = jnp.zeros((TILE, TILE), jnp.float32)
    for a in range(tiles):
        rows = slice(a * TILE, (a + 1) * TILE)
        for b in range(tiles):
            lanes = slice(b * TILE, (b + 1) * TILE)
            r_ref[rows, lanes] = wide[a, b] if b >= a else zero
            value = wide[a, tiles + b] if b <= a else zero
            inv_ref[rows, lanes] = value
            high, middle, low = three_terms(value)
            hi_ref[rows, lanes] = high.astype(jnp.bfloat16)
            mid_ref[rows, lanes] = middle.astype(jnp.bfloat16)
            lo_ref[rows, lanes] = low.astype(jnp.bfloat16)


def factor_call(kernel, out_shape, value, after, aliases, tiles):
    many = isinstance(out_shape, tuple)
    return pl.pallas_call(
        lambda *refs: kernel(*refs[len(after) :]),
        out_shape=out_shape,
        in_specs=[ANY] * len(after) + [VMEM],
        out_specs=(VMEM,) * len(out_shape) if many else VMEM,
        scratch_shapes=[pltpu.VMEM((TILE, TILE), jnp.float32)] * 4,
        input_output_aliases={len(after): 0} if aliases else {},
        compiler_params=pltpu.CompilerParams(vmem_limit_bytes=VMEM_BYTES),
        cost_estimate=cost(
            flops=7 * 10**9, bytes_accessed=value.size * 4, transcendentals=TILE
        ),
        name="factor",
    )(*after, value)


def factor_steps(blocks, tiles, rows_total, after):
    state = jax.ShapeDtypeStruct((tiles, 2 * tiles, TILE, TILE), jnp.float32)
    full = jax.ShapeDtypeStruct((tiles * TILE, tiles * TILE), jnp.float32)
    term = jax.ShapeDtypeStruct(full.shape, jnp.bfloat16)
    value = factor_call(
        lambda *refs: first_kernel(tiles, rows_total, *refs), state, blocks, after, False, tiles
    )
    for b in range(1, tiles - 1):
        after = yield value
        value = factor_call(
            lambda *refs: next_kernel(tiles, b, *refs), state, value, after, True, tiles
        )
    after = yield value
    yield factor_call(
        lambda *refs: last_kernel(tiles, *refs), (full, full, term, term, term), value, after, False, tiles
    )


def basis_kernel(*refs):
    hi_ref, mid_ref, lo_ref, out_ref = refs[-4:]
    cells = joint_rows(refs[0])
    total = lax.dot_general(
        cells, lo_ref[...], LANES_BY_LANES, preferred_element_type=jnp.float32
    )
    total += lax.dot_general(
        cells, mid_ref[...], LANES_BY_LANES, preferred_element_type=jnp.float32
    )
    total += lax.dot_general(
        cells, hi_ref[...], LANES_BY_LANES, preferred_element_type=jnp.float32
    )
    out_ref[...] = total.reshape(out_ref.shape)


def basis(cells, terms, call, calls, filled, after, steps=4):
    shares, blocks, rows, width = cells.shape
    full = shares * width
    size = blocks // calls // steps
    first = call * steps
    spec = pl.BlockSpec((shares, size, rows, width), lambda i: (0, first + i, 0, 0))
    term = pl.BlockSpec((full, full), lambda i: (0, 0))
    unread = ([] if filled is None else [filled]) + list(after)
    return pl.pallas_call(
        lambda *refs: basis_kernel(*refs[len(unread) :]),
        grid=(steps,),
        out_shape=jax.ShapeDtypeStruct((blocks, rows, full), jnp.float32),
        in_specs=[ANY] * len(unread) + [spec] + [term] * 3,
        out_specs=pl.BlockSpec((size, rows, full), lambda i: (first + i, 0, 0)),
        input_output_aliases={} if filled is None else {0: 0},
        compiler_params=pltpu.CompilerParams(vmem_limit_bytes=VMEM_BYTES),
        cost_estimate=cost(
            flops=6 * blocks * rows * full * full // calls,
            bytes_accessed=6 * blocks * rows * full // calls,
            transcendentals=0,
        ),
        name="basis",
    )(*unread, cells, *terms)


def sum_kernel(count, value_ref, out_ref):
    rows = out_ref.shape[0]
    total = value_ref[:rows]
    for i in range(1, count):
        total += value_ref[i * rows : (i + 1) * rows]
    out_ref[...] = total


def sum_pieces(value, count, after):
    rows, lanes = value.shape
    return pl.pallas_call(
        lambda *refs: sum_kernel(count, *refs[len(after) :]),
        out_shape=jax.ShapeDtypeStruct((rows // count, lanes), value.dtype),
        in_specs=[ANY] * len(after) + [VMEM],
        out_specs=VMEM,
        cost_estimate=cost(flops=value.size, bytes_accessed=4 * value.size, transcendentals=0),
        name="sum_pieces",
    )(*after, value)


def add_kernel(one_ref, two_ref, out_ref):
    out_ref[...] = one_ref[...] + two_ref[...]


def add(one, two, after):
    return pl.pallas_call(
        lambda *refs: add_kernel(*refs[len(after) :]),
        out_shape=jax.ShapeDtypeStruct(one.shape, one.dtype),
        in_specs=[ANY] * len(after) + [VMEM, VMEM],
        out_specs=VMEM,
        cost_estimate=cost(flops=one.size, bytes_accessed=12 * one.size, transcendentals=0),
        name="add",
    )(*after, one, two)


def join_kernel(*refs):
    rows = refs[0].shape[0]
    for i, ref in enumerate(refs[:-1]):
        refs[-1][i * rows : (i + 1) * rows] = ref[...]


def join(values):
    rows, lanes = values[0].shape
    return pl.pallas_call(
        join_kernel,
        out_shape=jax.ShapeDtypeStruct((len(values) * rows, lanes), values[0].dtype),
        in_specs=[VMEM] * len(values),
        out_specs=VMEM,
        name="join",
    )(*values)


def projection_kernel(slabs, divisor, inverse_ref, same_ref, other_ref, out_ref, cross_ref):
    me = lax.axis_index("space")
    rows = cross_ref.shape[0] // slabs
    for away in range(slabs):
        at = pl.ds(pl.multiple_of((me ^ away) * rows, rows), rows)
        chip = slice(away // CORES * rows, (away // CORES + 1) * rows)
        cross_ref[at, :] = (other_ref if away % CORES else same_ref)[chip]
    out_ref[...] = (
        lax.dot(
            inverse_ref[...],
            cross_ref[...],
            precision=HIGHEST,
            preferred_element_type=jnp.float32,
        )
        / divisor
    )


def project(inverse, same, other, slabs, divisor):
    return pl.pallas_call(
        lambda *refs: projection_kernel(slabs, divisor, *refs),
        out_shape=jax.ShapeDtypeStruct(inverse.shape, jnp.float32),
        in_specs=[VMEM] * 3,
        out_specs=VMEM,
        scratch_shapes=[pltpu.VMEM(inverse.shape, jnp.float32)],
        compiler_params=pltpu.CompilerParams(vmem_limit_bytes=VMEM_BYTES),
        name="project",
    )(inverse, same, other)


def swap(value, axis, mask):
    return lax.ppermute(value, axis, [(i, i ^ mask) for i in range(lax.axis_size(axis))])


def body(owned_x, owned_y, patch_dest):
    slabs = lax.axis_size("space")
    shares = lax.axis_size("snap")
    slots, patch, width = owned_x.shape
    per_slab = slots // 2
    parts = patch // shares // CELL_TILE
    rows_total = slabs * per_slab * patch
    full = shares * width
    tiles = full // TILE
    pairs = tiles * (tiles + 1) // 2

    def packed(owned, with_ids):
        tiles = owned.reshape(slots, patch // CELL_TILE, CELL_TILE, width)
        return pack(patch_dest, tiles, slabs, per_slab, with_ids)

    def merged(sent, after):
        return merge(sent[0], swap(sent[1], "space", 1), slabs // CORES, after)

    def to_chips(joined):
        return [joined[0]] + [swap(joined[m], "space", CORES * m) for m in range(1, len(joined))]

    def to_rows(pieces):
        return [pieces[0]] + [swap(pieces[r], "snap", r) for r in range(1, shares)]

    def place(meta, moved, part, after):
        return settle(meta, moved, slots // slabs, per_slab, shares, parts, part, after)

    def to_pieces(value):
        return lax.all_to_all(value, "space", split_axis=0, concat_axis=0, tiled=True)

    def hops():
        hop = 1
        while hop < shares:
            yield hop
            hop *= 2

    moved_x = to_chips(merged(packed(owned_x, True), []))
    moved_y = to_chips(merged(packed(owned_y, False), moved_x[1:3]))
    pieces, meta = place(None, moved_x, None, [])
    x_cells = lax.all_to_all(pieces, "snap", split_axis=0, concat_axis=0, tiled=True)

    gram_local = gram_blocks(x_cells, moved_y[1:2])
    gram = to_pieces(gram_local.reshape(pairs * TILE, TILE))
    pieces = place(meta, moved_y, 0, [gram_local])
    y_cells = [to_rows(pieces)]
    gram = sum_pieces(gram, slabs, pieces[:1])
    for hop in hops():
        gram = add(gram, swap(gram, "snap", hop), y_cells[0][hop : hop + 1])
    gram = lax.all_gather(gram, "space", axis=0, tiled=True)
    for part in range(1, parts):
        pieces = place(meta, moved_y, part, y_cells[-1][1:3])
        y_cells.append(to_rows(pieces))

    steps = factor_steps(gram.reshape(pairs, TILE, TILE), tiles, rows_total, pieces[:1])
    state = next(steps)
    for _ in range(tiles - 2):
        state = steps.send([])
    cross_local = cross_sum(x_cells, y_cells, [state])
    cross = to_pieces(cross_local)
    r_factor, inverse, *terms = steps.send([cross_local])

    q_basis = basis(x_cells, terms, 0, 2, None, [])
    cross = sum_pieces(cross, slabs, [q_basis])
    q_basis = basis(x_cells, terms, 1, 2, q_basis, [cross])
    for hop in hops():
        cross = add(cross, swap(cross, "snap", hop), [q_basis] if hop == 1 else [])
    same = join([cross] + [swap(cross, "space", m) for m in range(CORES, slabs, CORES)])
    projection = project(inverse, same, swap(same, "space", 1), slabs, math.sqrt(rows_total))
    return q_basis, r_factor, projection


def solution(mesh):
    in_specs = (P("space", None, "snap"), P("space", None, "snap"), P("space"))
    out_specs = (P("space", "snap", None), P(), P())
    return jax.shard_map(body, mesh=mesh, in_specs=in_specs, out_specs=out_specs, check_vma=False)
```

```python
import math

import jax
import jax.numpy as jnp
from jax import lax
from jax.experimental import pallas as pl
from jax.experimental.pallas import tpu as pltpu
from jax.sharding import PartitionSpec as P

TILE = 128
GROUP = 8
CORES = 2
VMEM_BYTES = 32 * 1024 * 1024
HIGHEST = lax.Precision.HIGHEST
SMEM = pl.BlockSpec(memory_space=pltpu.SMEM)
VMEM = pl.BlockSpec(memory_space=pltpu.VMEM)
ANY = pl.BlockSpec(memory_space=pl.ANY)
LIGHT = pl.CostEstimate(flops=1, bytes_accessed=1, transcendentals=0)
ROWS_BY_ROWS = (((0,), (0,)), ((), ()))
LANES_BY_LANES = (((1,), (1,)), ((), ()))


def pack_kernel(slabs, capacity, per_slab, shares_of, dest_ref, owned_ref, *refs):
    out_refs, (ids_ref, count_ref) = refs[:-2], refs[-2:]
    chips = slabs // CORES
    me = lax.axis_index("space")
    mine = lax.axis_index("snap")
    lane = lax.broadcasted_iota(jnp.int32, (1, TILE), 1)
    ids_ref[...] = jnp.full_like(ids_ref, -1)
    for slab in range(slabs):
        count_ref[slab] = 0

    def place(i, _):
        block = dest_ref[i]

        @pl.when(block >= 0)
        def _():
            slab = lax.div(block, per_slab)
            rank = count_ref[slab]
            count_ref[slab] = rank + 1
            here = pl.ds(slab, 1)
            ids_ref[here, :] = jnp.where(lane == rank, block - slab * per_slab, ids_ref[here, :])
            away = slab ^ me
            chip = lax.shift_right_logical(away, 1)
            for core in range(CORES):

                @pl.when((away & 1) == core)
                def _():
                    for group, shares in enumerate(shares_of):
                        out_ref = out_refs[group * CORES + core]
                        at = chip * (out_ref.shape[0] // chips) + rank * len(shares)
                        for k, share in enumerate(shares):
                            out_ref[at + k] = owned_ref[i, mine ^ share]

        return 0

    lax.fori_loop(0, dest_ref.shape[0], place, 0, unroll=2)
    for group, shares in enumerate(shares_of):
        used = capacity * len(shares)
        for away in range(slabs):
            out_ref = out_refs[group * CORES + away % CORES]
            span = out_ref.shape[0] // chips
            if span > used:
                ids = ids_ref[pl.ds(me ^ away, 1), :].astype(jnp.float32)
                tile = jnp.broadcast_to(ids, out_ref.shape[1:]).astype(out_ref.dtype)
                out_ref[away // CORES * span + used] = tile


def pack(dest, owned, slabs, per_slab, shares_of, with_ids, after):
    slots, _, rows, width = owned.shape
    chips = slabs // CORES
    capacity = slots // slabs
    sent = []
    for group, shares in enumerate(shares_of):
        span = capacity * len(shares) + (1 if with_ids and group == 0 else 0)
        sent += [jax.ShapeDtypeStruct((chips * span, rows, width), owned.dtype)] * CORES
    outs = pl.pallas_call(
        lambda *refs: pack_kernel(slabs, capacity, per_slab, shares_of, *refs[len(after) :]),
        out_shape=tuple(sent),
        in_specs=[ANY] * len(after) + [SMEM, VMEM],
        out_specs=(VMEM,) * len(sent),
        scratch_shapes=[
            pltpu.VMEM((slabs, TILE), jnp.int32),
            pltpu.SMEM((slabs,), jnp.int32),
        ],
        compiler_params=pltpu.CompilerParams(vmem_limit_bytes=VMEM_BYTES),
        cost_estimate=LIGHT,
        name="pack",
    )(*after, dest, owned)
    return [outs[at : at + CORES] for at in range(0, len(outs), CORES)]


def merge_kernel(same_ref, other_ref, *out_refs):
    span = same_ref.shape[0] // len(out_refs)
    for chip, out_ref in enumerate(out_refs):
        out_ref[:span] = same_ref[chip * span : (chip + 1) * span]
        out_ref[span:] = other_ref[chip * span : (chip + 1) * span]


def pick_kernel(picked, same_ref, other_ref, *out_refs):
    for chip, out_ref in enumerate(out_refs):
        for owner, ref in enumerate((same_ref, other_ref)):
            out_ref[owner] = ref[chip, :, picked]


def merge(same, other, chips, after, picked=None, of=1):
    tiles, rows, width = same.shape
    if picked is None:
        kernel = merge_kernel
        shape = (CORES * tiles // chips, rows, width)
    else:
        kernel = lambda *refs: pick_kernel(picked, *refs)
        ranks = tiles // chips // of
        shape = (CORES, ranks, picked.stop - picked.start, rows, width)
        same, other = (value.reshape(chips, ranks, of, rows, width) for value in (same, other))
    outs = pl.pallas_call(
        lambda *refs: kernel(*refs[len(after) :]),
        out_shape=(jax.ShapeDtypeStruct(shape, same.dtype),) * chips,
        in_specs=[ANY] * len(after) + [VMEM, VMEM],
        out_specs=(VMEM,) * chips,
        compiler_params=pltpu.CompilerParams(vmem_limit_bytes=VMEM_BYTES),
        cost_estimate=LIGHT,
        name="merge",
    )(*after, same, other)
    return [out.reshape(-1, rows, width) for out in outs]


def settle_kernel(chips, capacity, with_ids, far, *refs):
    if with_ids:
        moved_refs, out_refs, meta_ref, ids_ref = refs[:chips], refs[chips:-2], refs[-2], refs[-1]
        span = moved_refs[0].shape[0] // CORES
        for source in range(chips * CORES):
            at = source % CORES * span + span - 1
            tile = moved_refs[source // CORES][at].astype(jnp.float32)
            ids_ref[source : source + 1, :] = tile[:1].astype(jnp.int32)
        pltpu.sync_copy(ids_ref, meta_ref)
    else:
        meta_ref, moved_refs, out_refs = refs[0], refs[1 : 1 + chips], refs[1 + chips :]
        span = moved_refs[0].shape[0] // CORES
    mine = lax.axis_index("snap")
    count = len(far) or len(out_refs)
    for source in range(chips * CORES):
        moved_ref = moved_refs[source // CORES]

        def place(rank, _):
            block = meta_ref[source, rank]

            @pl.when(block >= 0)
            def _():
                at = source % CORES * span + rank * count
                for k in range(count):
                    if far:
                        out_refs[0][mine ^ far[k], block] = moved_ref[at + k]
                    else:
                        out_refs[k][block] = moved_ref[at + k]

            return 0

        lax.fori_loop(0, capacity, place, 0, unroll=4)


def settle(meta, moved, capacity, per_slab, shares, far, after):
    with_ids = meta is None
    chips = len(moved)
    rows, width = moved[0].shape[1:]
    if far:
        pieces = (jax.ShapeDtypeStruct((shares, per_slab, rows, width), moved[0].dtype),)
    else:
        pieces = (jax.ShapeDtypeStruct((per_slab, rows, width), moved[0].dtype),) * (shares // 2)
    ids = jax.ShapeDtypeStruct((chips * CORES, TILE), jnp.int32)
    outs = pl.pallas_call(
        lambda *refs: settle_kernel(chips, capacity, with_ids, far, *refs[len(after) :]),
        out_shape=pieces + ((ids,) if with_ids else ()),
        in_specs=[ANY] * len(after) + ([] if with_ids else [SMEM]) + [VMEM] * chips,
        out_specs=(VMEM,) * len(pieces) + ((SMEM,) if with_ids else ()),
        scratch_shapes=[pltpu.VMEM((chips * CORES, TILE), jnp.int32)] if with_ids else [],
        compiler_params=pltpu.CompilerParams(vmem_limit_bytes=VMEM_BYTES),
        cost_estimate=LIGHT,
        name="settle",
    )(*after, *([] if with_ids else [meta]), *moved)
    return list(outs[: len(pieces)]), (outs[-1] if with_ids else meta)


def by_distance(refs):
    near = len(refs) - 1
    mine = lax.axis_index("snap")
    return list(refs[:near]) + [refs[near].at[mine ^ share] for share in range(near, 2 * near)]


def cell_specs(shares, size, rows, width, first):
    near = pl.BlockSpec((size, rows, width), lambda i: (first + i, 0, 0))
    far = pl.BlockSpec((shares, size, rows, width), lambda i: (0, first + i, 0, 0))
    return [near] * (shares // 2) + [far]


def whole_rows(refs):
    blocks, rows, width = refs[0].shape
    return jnp.concatenate([ref[...].reshape(blocks * rows, width) for ref in refs], axis=1)


def tile_of(row, lane, tiles):
    return row * tiles - lax.div(row * (row - 1), 2) + lane - row


def gram_kernel(shares, *refs):
    out_ref, acc_ref = refs[-2:]
    step = pl.program_id(0)

    @pl.when(step == 0)
    def _():
        acc_ref[...] = jnp.zeros_like(acc_ref)

    cells = whole_rows(by_distance(refs[:-2]))
    acc_ref[...] += lax.dot_general(
        cells, cells, ROWS_BY_ROWS, preferred_element_type=jnp.float32
    )

    @pl.when(step == pl.num_programs(0) - 1)
    def _():
        mine = lax.axis_index("snap")
        for a in range(shares):
            for b in range(shares):
                row, lane = mine ^ a, mine ^ b

                @pl.when(row <= lane)
                def _():
                    out_ref[tile_of(row, lane, shares)] = acc_ref[
                        a * TILE : (a + 1) * TILE, b * TILE : (b + 1) * TILE
                    ]


def gram_blocks(cells, after, steps=4):
    shares, blocks, rows, width = cells[-1].shape
    pairs = shares * (shares + 1) // 2
    full = shares * width
    return pl.pallas_call(
        lambda *refs: gram_kernel(shares, *refs[len(after) :]),
        grid=(steps,),
        out_shape=jax.ShapeDtypeStruct((pairs, TILE, TILE), jnp.float32),
        in_specs=[ANY] * len(after) + cell_specs(shares, blocks // steps, rows, width, 0),
        out_specs=pl.BlockSpec((pairs, TILE, TILE), lambda i: (0, 0, 0)),
        scratch_shapes=[pltpu.VMEM((full, full), jnp.float32)],
        compiler_params=pltpu.CompilerParams(vmem_limit_bytes=VMEM_BYTES),
        cost_estimate=LIGHT,
        name="gram_blocks",
    )(*after, *cells)


def cross_kernel(shares, *refs):
    out_ref, acc_ref = refs[-2:]
    step = pl.program_id(0)

    @pl.when(step == 0)
    def _():
        acc_ref[...] = jnp.zeros_like(acc_ref)

    count = len(refs) // 2 - 1
    acc_ref[...] += lax.dot_general(
        whole_rows(by_distance(refs[:count])),
        whole_rows(by_distance(refs[count : 2 * count])),
        ROWS_BY_ROWS,
        preferred_element_type=jnp.float32,
    )

    @pl.when(step == pl.num_programs(0) - 1)
    def _():
        mine = lax.axis_index("snap")
        for a in range(shares):
            rows = pl.ds(pl.multiple_of((mine ^ a) * TILE, TILE), TILE)
            for b in range(shares):
                lanes = pl.ds(pl.multiple_of((mine ^ b) * TILE, TILE), TILE)
                out_ref[rows, lanes] = acc_ref[
                    a * TILE : (a + 1) * TILE, b * TILE : (b + 1) * TILE
                ]


def cross_sum(x_cells, y_cells, after, steps=4):
    shares, blocks, rows, width = x_cells[-1].shape
    full = shares * width
    specs = cell_specs(shares, blocks // steps, rows, width, 0)
    return pl.pallas_call(
        lambda *refs: cross_kernel(shares, *refs[len(after) :]),
        grid=(steps,),
        out_shape=jax.ShapeDtypeStruct((full, full), jnp.float32),
        in_specs=[ANY] * len(after) + specs * 2,
        out_specs=pl.BlockSpec((full, full), lambda i: (0, 0)),
        scratch_shapes=[pltpu.VMEM((full, full), jnp.float32)],
        compiler_params=pltpu.CompilerParams(vmem_limit_bytes=VMEM_BYTES),
        cost_estimate=LIGHT,
        name="cross_sum",
    )(*after, *x_cells, *y_cells)


def three_terms(value):
    high = value.astype(jnp.bfloat16).astype(jnp.float32)
    rest = value - high
    middle = rest.astype(jnp.bfloat16).astype(jnp.float32)
    return high, middle, rest - middle


def lane_of(row, lane):
    return jnp.broadcast_to(row[:, lane : lane + 1], row.shape)


def row_of(ref, row):
    return jnp.broadcast_to(ref[row : row + 1, :], (GROUP, TILE))


def factor_tile(a_ref, w_ref, u_ref, v_ref):
    panels = TILE // GROUP
    a_rows = [row_of(a_ref, i) for i in range(GROUP)]
    w_rows = [row_of(w_ref, i) for i in range(GROUP)]
    for p in range(panels):
        base = p * GROUP
        small = {
            (i, k): lane_of(a_rows[i], base + k) for i in range(GROUP) for k in range(i, GROUP)
        }
        for j in range(GROUP):
            scale = lax.rsqrt(small[j, j])
            a_rows[j] = a_rows[j] * scale
            w_rows[j] = w_rows[j] * scale
            u_ref[base + j : base + j + 1, :] = a_rows[j][:1]
            v_ref[base + j : base + j + 1, :] = w_rows[j][:1]
            below = {k: small[j, k] * scale for k in range(j + 1, GROUP)}
            for k in range(j + 1, GROUP):
                for m in range(k, GROUP):
                    small[k, m] = small[k, m] - below[k] * below[m]
            for k in range(j + 1, GROUP):
                a_rows[k] = a_rows[k] - below[k] * a_rows[j]
                w_rows[k] = w_rows[k] - below[k] * w_rows[j]
        if p + 1 == panels:
            break
        after = base + GROUP
        next_a = [row_of(a_ref, after + i) for i in range(GROUP)]
        next_w = [row_of(w_ref, after + i) for i in range(GROUP)]
        for i in range(GROUP):
            for k in range(GROUP):
                factor = lane_of(a_rows[k], after + i)
                next_a[i] = next_a[i] - factor * a_rows[k]
                next_w[i] = next_w[i] - factor * w_rows[k]
        if p + 2 < panels:
            done = after + GROUP
            u = u_ref[base:after, :]
            v = v_ref[base:after, :]
            uh, um, ul = three_terms(u)
            vh, vm, vl = three_terms(v)
            left = jnp.concatenate([uh, uh, um, uh, ul, um], axis=0).astype(jnp.bfloat16)
            right_a = jnp.concatenate([uh, um, uh, ul, uh, um], axis=0)
            right_w = jnp.concatenate([vh, vm, vh, vl, vh, vm], axis=0)
            right = jnp.concatenate([right_a, right_w], axis=1).astype(jnp.bfloat16)
            update = lax.dot_general(
                left, right, ROWS_BY_ROWS, preferred_element_type=jnp.float32
            )
            a_ref[done:, :] = a_ref[done:, :] - update[done:, :TILE]
            w_ref[done:, :] = w_ref[done:, :] - update[done:, TILE:]
        a_rows, w_rows = next_a, next_w


def factor_step(tiles, b, wide, a_ref, w_ref, u_ref, v_ref):
    row = lax.broadcasted_iota(jnp.int32, (TILE, TILE), 0)
    lane = lax.broadcasted_iota(jnp.int32, (TILE, TILE), 1)
    a_ref[...] = wide[b, b]
    w_ref[...] = jnp.where(row == lane, 1.0, 0.0)
    factor_tile(a_ref, w_ref, u_ref, v_ref)
    inverse = v_ref[...]
    wide[b, b] = jnp.where(row <= lane, u_ref[...], 0.0)
    wide[b, tiles + b] = inverse
    for j in range(1, tiles):
        wide[b, b + j] = lax.dot(
            inverse, wide[b, b + j], precision=HIGHEST, preferred_element_type=jnp.float32
        )
    for r in range(b + 1, tiles):
        for c in list(range(r, tiles)) + list(range(tiles, tiles + b + 1)):
            update = lax.dot_general(
                wide[b, r],
                wide[b, c],
                ROWS_BY_ROWS,
                precision=HIGHEST,
                preferred_element_type=jnp.float32,
            )
            wide[r, c] = -update if c == tiles + b else wide[r, c] - update


def first_kernel(tiles, rows_total, g_ref, wide, *scratch):
    at = 0
    for a in range(tiles):
        for b in range(a, tiles):
            wide[a, b] = g_ref[at] / rows_total
            at += 1
    factor_step(tiles, 0, wide, *scratch)


def next_kernel(tiles, b, _, wide, *scratch):
    factor_step(tiles, b, wide, *scratch)


def last_kernel(tiles, wide, r_ref, inv_ref, hi_ref, mid_ref, lo_ref, *scratch):
    factor_step(tiles, tiles - 1, wide, *scratch)
    zero = jnp.zeros((TILE, TILE), jnp.float32)
    mine = lax.axis_index("snap")
    for a in range(tiles):
        rows = slice(a * TILE, (a + 1) * TILE)
        for b in range(tiles):
            lanes = slice(b * TILE, (b + 1) * TILE)
            r_ref[rows, lanes] = wide[a, b] if b >= a else zero
            value = wide[a, tiles + b] if b <= a else zero
            inv_ref[rows, lanes] = value
            high, middle, low = three_terms(value)
            lanes = pl.ds(pl.multiple_of((mine ^ b) * TILE, TILE), TILE)
            hi_ref[rows, lanes] = high.astype(jnp.bfloat16)
            mid_ref[rows, lanes] = middle.astype(jnp.bfloat16)
            lo_ref[rows, lanes] = low.astype(jnp.bfloat16)


def factor_call(kernel, out_shape, value, after, aliases, tiles):
    many = isinstance(out_shape, tuple)
    return pl.pallas_call(
        lambda *refs: kernel(*refs[len(after) :]),
        out_shape=out_shape,
        in_specs=[ANY] * len(after) + [VMEM],
        out_specs=(VMEM,) * len(out_shape) if many else VMEM,
        scratch_shapes=[pltpu.VMEM((TILE, TILE), jnp.float32)] * 4,
        input_output_aliases={len(after): 0} if aliases else {},
        compiler_params=pltpu.CompilerParams(vmem_limit_bytes=VMEM_BYTES),
        cost_estimate=LIGHT,
        name="factor",
    )(*after, value)


def factor_steps(blocks, tiles, rows_total, after):
    state = jax.ShapeDtypeStruct((tiles, 2 * tiles, TILE, TILE), jnp.float32)
    full = jax.ShapeDtypeStruct((tiles * TILE, tiles * TILE), jnp.float32)
    term = jax.ShapeDtypeStruct(full.shape, jnp.bfloat16)
    value = factor_call(
        lambda *refs: first_kernel(tiles, rows_total, *refs), state, blocks, after, False, tiles
    )
    for b in range(1, tiles - 1):
        after = yield value
        value = factor_call(
            lambda *refs: next_kernel(tiles, b, *refs), state, value, after, True, tiles
        )
    after = yield value
    yield factor_call(
        lambda *refs: last_kernel(tiles, *refs), (full, full, term, term, term), value, after, False, tiles
    )


def basis_kernel(*refs):
    hi_ref, mid_ref, lo_ref, out_ref = refs[-4:]
    cells = whole_rows(by_distance(refs[:-4]))
    total = lax.dot_general(
        cells, lo_ref[...], LANES_BY_LANES, preferred_element_type=jnp.float32
    )
    total += lax.dot_general(
        cells, mid_ref[...], LANES_BY_LANES, preferred_element_type=jnp.float32
    )
    total += lax.dot_general(
        cells, hi_ref[...], LANES_BY_LANES, preferred_element_type=jnp.float32
    )
    out_ref[...] = total.reshape(out_ref.shape)


def basis(cells, terms, call, calls, filled, after, steps=4):
    shares, blocks, rows, width = cells[-1].shape
    full = shares * width
    size = blocks // calls // steps
    first = call * steps
    term = pl.BlockSpec((full, full), lambda i: (0, 0))
    unread = ([] if filled is None else [filled]) + list(after)
    return pl.pallas_call(
        lambda *refs: basis_kernel(*refs[len(unread) :]),
        grid=(steps,),
        out_shape=jax.ShapeDtypeStruct((blocks, rows, full), jnp.float32),
        in_specs=[ANY] * len(unread) + cell_specs(shares, size, rows, width, first) + [term] * 3,
        out_specs=pl.BlockSpec((size, rows, full), lambda i: (first + i, 0, 0)),
        input_output_aliases={} if filled is None else {0: 0},
        compiler_params=pltpu.CompilerParams(vmem_limit_bytes=VMEM_BYTES),
        cost_estimate=LIGHT,
        name="basis",
    )(*unread, *cells, *terms)


def sum_kernel(count, copies, value_ref, out_ref):
    rows = value_ref.shape[0] // count
    total = value_ref[:rows]
    for i in range(1, count):
        total += value_ref[i * rows : (i + 1) * rows]
    for i in range(copies):
        out_ref[i * rows : (i + 1) * rows] = total


def sum_pieces(value, count, after, copies=1):
    rows, lanes = value.shape
    return pl.pallas_call(
        lambda *refs: sum_kernel(count, copies, *refs[len(after) :]),
        out_shape=jax.ShapeDtypeStruct((rows // count * copies, lanes), value.dtype),
        in_specs=[ANY] * len(after) + [VMEM],
        out_specs=VMEM,
        cost_estimate=LIGHT,
        name="sum_pieces",
    )(*after, value)


def add_kernel(one_ref, two_ref, out_ref):
    out_ref[...] = one_ref[...] + two_ref[...]


def add(one, two, after):
    return pl.pallas_call(
        lambda *refs: add_kernel(*refs[len(after) :]),
        out_shape=jax.ShapeDtypeStruct(one.shape, one.dtype),
        in_specs=[ANY] * len(after) + [VMEM, VMEM],
        out_specs=VMEM,
        cost_estimate=LIGHT,
        name="add",
    )(*after, one, two)


def join_kernel(*refs):
    rows = refs[0].shape[0]
    for i, ref in enumerate(refs[:-1]):
        refs[-1][i * rows : (i + 1) * rows] = ref[...]


def join(values):
    rows, lanes = values[0].shape
    return pl.pallas_call(
        join_kernel,
        out_shape=jax.ShapeDtypeStruct((len(values) * rows, lanes), values[0].dtype),
        in_specs=[VMEM] * len(values),
        out_specs=VMEM,
        name="join",
    )(*values)


def projection_kernel(slabs, divisor, inverse_ref, same_ref, other_ref, out_ref, cross_ref):
    me = lax.axis_index("space")
    rows = cross_ref.shape[0] // slabs
    for away in range(slabs):
        at = pl.ds(pl.multiple_of((me ^ away) * rows, rows), rows)
        chip = slice(away // CORES * rows, (away // CORES + 1) * rows)
        cross_ref[at, :] = (other_ref if away % CORES else same_ref)[chip]
    out_ref[...] = (
        lax.dot(
            inverse_ref[...],
            cross_ref[...],
            precision=HIGHEST,
            preferred_element_type=jnp.float32,
        )
        / divisor
    )


def project(inverse, same, other, slabs, divisor):
    return pl.pallas_call(
        lambda *refs: projection_kernel(slabs, divisor, *refs),
        out_shape=jax.ShapeDtypeStruct(inverse.shape, jnp.float32),
        in_specs=[VMEM] * 3,
        out_specs=VMEM,
        scratch_shapes=[pltpu.VMEM(inverse.shape, jnp.float32)],
        compiler_params=pltpu.CompilerParams(vmem_limit_bytes=VMEM_BYTES),
        name="project",
    )(inverse, same, other)


def swap(value, axis, mask):
    return lax.ppermute(value, axis, [(i, i ^ mask) for i in range(lax.axis_size(axis))])


def body(owned_x, owned_y, patch_dest):
    slabs = lax.axis_size("space")
    shares = lax.axis_size("snap")
    slots, patch, width = owned_x.shape
    per_slab = slots // 2
    rows_total = slabs * per_slab * patch
    full = shares * width
    tiles = full // TILE
    pairs = tiles * (tiles + 1) // 2
    half = shares // 2
    shares_of = (tuple(range(half, shares)), tuple(range(half)))

    def packed(owned, groups, with_ids, after):
        cells = owned.reshape(slots, shares, patch // shares, width)
        return pack(patch_dest, cells, slabs, per_slab, groups, with_ids, after)

    def merged(sent, after):
        return merge(sent[0], swap(sent[1], "space", 1), slabs // CORES, after)

    def to_chips(joined):
        return [joined[0]] + [swap(joined[m], "space", CORES * m) for m in range(1, len(joined))]

    def to_pieces(value, axis="space"):
        return lax.all_to_all(value, axis, split_axis=0, concat_axis=0, tiled=True)

    def place_far(meta, moved, after):
        pieces, meta = settle(
            meta, moved, slots // slabs, per_slab, shares, shares_of[0], after
        )
        return pieces[0], to_pieces(pieces[0], "snap"), meta

    def place_near(meta, moved, after):
        pieces, _ = settle(meta, moved, slots // slabs, per_slab, shares, (), after)
        return [
            swap(piece, "snap", share) if share else piece
            for share, piece in zip(shares_of[1], pieces)
        ]

    def hops():
        hop = 1
        while hop < shares:
            yield hop
            hop *= 2

    chips = slabs // CORES
    sent_x = packed(owned_x, shares_of, True, [])
    ((same_y, other_y),) = packed(owned_y, (shares_of[0] + shares_of[1],), False, [])
    other_y = swap(other_y, "space", 1)
    joined_near = merged(sent_x[1], [])
    far = to_chips(merged(sent_x[0], []))
    settled, x_far, meta = place_far(None, far, [other_y, joined_near[0]])
    near = to_chips(joined_near)
    y_far = to_chips(merge(same_y, other_y, chips, near[1:3], slice(0, half), shares))
    y_near = to_chips(merge(same_y, other_y, chips, y_far[1:3], slice(half, shares), shares))
    x_cells = place_near(meta, near, []) + [x_far]

    gram_local = gram_blocks(x_cells, y_far[1:3])
    gram = to_pieces(gram_local.reshape(pairs * TILE, TILE))
    gram = sum_pieces(gram, slabs, [])
    settled, y_cells, _ = place_far(meta, y_far, [gram])
    for hop in hops():
        gram = add(gram, swap(gram, "snap", hop), [settled] if hop == 1 else y_near[1:3])
    y_cells = place_near(meta, y_near, [gram]) + [y_cells]
    gram = lax.all_gather(gram, "space", axis=0, tiled=True)

    steps = factor_steps(gram.reshape(pairs, TILE, TILE), tiles, rows_total, y_cells[:1])
    state = next(steps)
    for _ in range(tiles - 2):
        state = steps.send([])
    cross_local = cross_sum(x_cells, y_cells, [state])
    cross = to_pieces(cross_local)
    r_factor, inverse, *terms = steps.send([cross_local])

    q_basis = basis(x_cells, terms, 0, 2, None, [])
    cross = sum_pieces(cross, slabs, [q_basis])
    q_basis = basis(x_cells, terms, 1, 2, q_basis, [cross])
    for hop in hops():
        cross = add(cross, swap(cross, "snap", hop), [q_basis] if hop == 1 else [])
    same = join([cross] + [swap(cross, "space", m) for m in range(CORES, slabs, CORES)])
    projection = project(inverse, same, swap(same, "space", 1), slabs, math.sqrt(rows_total))
    return q_basis, r_factor, projection


def solution(mesh):
    in_specs = (P("space", None, "snap"), P("space", None, "snap"), P("space"))
    out_specs = (P("space", "snap", None), P(), P())
    return jax.shard_map(body, mesh=mesh, in_specs=in_specs, out_specs=out_specs, check_vma=False)
```

```python
import math

import jax
import jax.numpy as jnp
from jax import lax
from jax.experimental import pallas as pl
from jax.experimental.pallas import tpu as pltpu
from jax.sharding import PartitionSpec as P

TILE = 128
GROUP = 8
CORES = 2
VMEM_BYTES = 32 * 1024 * 1024
HIGHEST = lax.Precision.HIGHEST
SMEM = pl.BlockSpec(memory_space=pltpu.SMEM)
VMEM = pl.BlockSpec(memory_space=pltpu.VMEM)
ANY = pl.BlockSpec(memory_space=pl.ANY)
LIGHT = pl.CostEstimate(flops=1, bytes_accessed=1, transcendentals=0)
ROWS_BY_ROWS = (((0,), (0,)), ((), ()))
LANES_BY_LANES = (((1,), (1,)), ((), ()))


def pack_kernel(slabs, capacity, per_slab, shares_of, dest_ref, owned_ref, *refs):
    out_refs, (ids_ref, count_ref) = refs[:-2], refs[-2:]
    chips = slabs // CORES
    me = lax.axis_index("space")
    mine = lax.axis_index("snap")
    lane = lax.broadcasted_iota(jnp.int32, (1, TILE), 1)
    ids_ref[...] = jnp.full_like(ids_ref, -1)
    for slab in range(slabs):
        count_ref[slab] = 0

    def place(i, _):
        block = dest_ref[i]

        @pl.when(block >= 0)
        def _():
            slab = lax.div(block, per_slab)
            rank = count_ref[slab]
            count_ref[slab] = rank + 1
            here = pl.ds(slab, 1)
            ids_ref[here, :] = jnp.where(lane == rank, block - slab * per_slab, ids_ref[here, :])
            away = slab ^ me
            chip = lax.shift_right_logical(away, 1)
            for core in range(CORES):

                @pl.when((away & 1) == core)
                def _():
                    for group, shares in enumerate(shares_of):
                        out_ref = out_refs[group * CORES + core]
                        at = chip * (out_ref.shape[0] // chips) + rank * len(shares)
                        for k, share in enumerate(shares):
                            out_ref[at + k] = owned_ref[i, mine ^ share]

        return 0

    lax.fori_loop(0, dest_ref.shape[0], place, 0, unroll=2)
    for group, shares in enumerate(shares_of):
        used = capacity * len(shares)
        for away in range(slabs):
            out_ref = out_refs[group * CORES + away % CORES]
            span = out_ref.shape[0] // chips
            if span > used:
                ids = ids_ref[pl.ds(me ^ away, 1), :].astype(jnp.float32)
                tile = jnp.broadcast_to(ids, out_ref.shape[1:]).astype(out_ref.dtype)
                out_ref[away // CORES * span + used] = tile


def pack(dest, owned, slabs, per_slab, shares_of, with_ids, after):
    slots, _, rows, width = owned.shape
    chips = slabs // CORES
    capacity = slots // slabs
    sent = []
    for group, shares in enumerate(shares_of):
        span = capacity * len(shares) + (1 if with_ids and group == 0 else 0)
        sent += [jax.ShapeDtypeStruct((chips * span, rows, width), owned.dtype)] * CORES
    outs = pl.pallas_call(
        lambda *refs: pack_kernel(slabs, capacity, per_slab, shares_of, *refs[len(after) :]),
        out_shape=tuple(sent),
        in_specs=[ANY] * len(after) + [SMEM, VMEM],
        out_specs=(VMEM,) * len(sent),
        scratch_shapes=[
            pltpu.VMEM((slabs, TILE), jnp.int32),
            pltpu.SMEM((slabs,), jnp.int32),
        ],
        compiler_params=pltpu.CompilerParams(vmem_limit_bytes=VMEM_BYTES),
        cost_estimate=LIGHT,
        name="pack",
    )(*after, dest, owned)
    return [outs[at : at + CORES] for at in range(0, len(outs), CORES)]


def merge_kernel(same_ref, other_ref, *out_refs):
    span = same_ref.shape[0] // len(out_refs)
    for chip, out_ref in enumerate(out_refs):
        out_ref[:span] = same_ref[chip * span : (chip + 1) * span]
        out_ref[span:] = other_ref[chip * span : (chip + 1) * span]


def pick_kernel(picked, same_ref, other_ref, *out_refs):
    for chip, out_ref in enumerate(out_refs):
        for owner, ref in enumerate((same_ref, other_ref)):
            out_ref[owner] = ref[chip, :, picked]


def merge(same, other, chips, after, picked=None, of=1):
    tiles, rows, width = same.shape
    if picked is None:
        kernel = merge_kernel
        shape = (CORES * tiles // chips, rows, width)
    else:
        kernel = lambda *refs: pick_kernel(picked, *refs)
        ranks = tiles // chips // of
        shape = (CORES, ranks, picked.stop - picked.start, rows, width)
        same, other = (value.reshape(chips, ranks, of, rows, width) for value in (same, other))
    outs = pl.pallas_call(
        lambda *refs: kernel(*refs[len(after) :]),
        out_shape=(jax.ShapeDtypeStruct(shape, same.dtype),) * chips,
        in_specs=[ANY] * len(after) + [VMEM, VMEM],
        out_specs=(VMEM,) * chips,
        compiler_params=pltpu.CompilerParams(vmem_limit_bytes=VMEM_BYTES),
        cost_estimate=LIGHT,
        name="merge",
    )(*after, same, other)
    return [out.reshape(-1, rows, width) for out in outs]


def settle_kernel(chips, capacity, with_ids, far, cuts, *refs):
    if with_ids:
        moved_refs, out_refs, meta_ref, ids_ref = refs[:chips], refs[chips:-2], refs[-2], refs[-1]
        span = moved_refs[0].shape[0] // CORES
        for source in range(chips * CORES):
            at = source % CORES * span + span - 1
            tile = moved_refs[source // CORES][at].astype(jnp.float32)
            ids_ref[source : source + 1, :] = tile[:1].astype(jnp.int32)
        pltpu.sync_copy(ids_ref, meta_ref)
    else:
        meta_ref, moved_refs, out_refs = refs[0], refs[1 : 1 + chips], refs[1 + chips :]
        span = moved_refs[0].shape[0] // CORES
    mine = lax.axis_index("snap")
    count = len(far) or len(out_refs) // cuts
    for source in range(chips * CORES):
        moved_ref = moved_refs[source // CORES]

        def place(rank, _):
            block = meta_ref[source, rank]

            @pl.when(block >= 0)
            def _():
                at = source % CORES * span + rank * count
                if far:
                    for k in range(count):
                        out_refs[0][mine ^ far[k], block] = moved_ref[at + k]
                else:
                    for k, out_ref in enumerate(out_refs):
                        rows = out_ref.shape[1]
                        cells = slice(k % cuts * rows, (k % cuts + 1) * rows)
                        out_ref[block] = moved_ref[at + k // cuts, cells]

            return 0

        lax.fori_loop(0, capacity, place, 0, unroll=4)


def settle(meta, moved, capacity, per_slab, shares, far, cuts, after):
    with_ids = meta is None
    chips = len(moved)
    rows, width = moved[0].shape[1:]
    if far:
        pieces = (jax.ShapeDtypeStruct((shares, per_slab, rows, width), moved[0].dtype),)
    else:
        piece = jax.ShapeDtypeStruct((per_slab, rows // cuts, width), moved[0].dtype)
        pieces = (piece,) * (shares // 2 * cuts)
    ids = jax.ShapeDtypeStruct((chips * CORES, TILE), jnp.int32)
    outs = pl.pallas_call(
        lambda *refs: settle_kernel(chips, capacity, with_ids, far, cuts, *refs[len(after) :]),
        out_shape=pieces + ((ids,) if with_ids else ()),
        in_specs=[ANY] * len(after) + ([] if with_ids else [SMEM]) + [VMEM] * chips,
        out_specs=(VMEM,) * len(pieces) + ((SMEM,) if with_ids else ()),
        scratch_shapes=[pltpu.VMEM((chips * CORES, TILE), jnp.int32)] if with_ids else [],
        compiler_params=pltpu.CompilerParams(vmem_limit_bytes=VMEM_BYTES),
        cost_estimate=LIGHT,
        name="settle",
    )(*after, *([] if with_ids else [meta]), *moved)
    return list(outs[: len(pieces)]), (outs[-1] if with_ids else meta)


def by_distance(refs):
    near = len(refs) - 1
    mine = lax.axis_index("snap")
    return list(refs[:near]) + [refs[near].at[mine ^ share] for share in range(near, 2 * near)]


def cell_specs(shares, size, rows, width, first):
    near = pl.BlockSpec((size, rows, width), lambda i: (first + i, 0, 0))
    far = pl.BlockSpec((shares, size, rows, width), lambda i: (0, first + i, 0, 0))
    return [near] * (shares // 2) + [far]


def whole_rows(refs):
    blocks, rows, width = refs[0].shape
    return jnp.concatenate([ref[...].reshape(blocks * rows, width) for ref in refs], axis=1)


def tile_of(row, lane, tiles):
    return row * tiles - lax.div(row * (row - 1), 2) + lane - row


def gram_kernel(shares, *refs):
    out_ref, acc_ref = refs[-2:]
    step = pl.program_id(0)

    @pl.when(step == 0)
    def _():
        acc_ref[...] = jnp.zeros_like(acc_ref)

    cells = whole_rows(by_distance(refs[:-2]))
    acc_ref[...] += lax.dot_general(
        cells, cells, ROWS_BY_ROWS, preferred_element_type=jnp.float32
    )

    @pl.when(step == pl.num_programs(0) - 1)
    def _():
        mine = lax.axis_index("snap")
        for a in range(shares):
            for b in range(shares):
                row, lane = mine ^ a, mine ^ b

                @pl.when(row <= lane)
                def _():
                    out_ref[tile_of(row, lane, shares)] = acc_ref[
                        a * TILE : (a + 1) * TILE, b * TILE : (b + 1) * TILE
                    ]


def gram_blocks(cells, after, steps=4):
    shares, blocks, rows, width = cells[-1].shape
    pairs = shares * (shares + 1) // 2
    full = shares * width
    return pl.pallas_call(
        lambda *refs: gram_kernel(shares, *refs[len(after) :]),
        grid=(steps,),
        out_shape=jax.ShapeDtypeStruct((pairs, TILE, TILE), jnp.float32),
        in_specs=[ANY] * len(after) + cell_specs(shares, blocks // steps, rows, width, 0),
        out_specs=pl.BlockSpec((pairs, TILE, TILE), lambda i: (0, 0, 0)),
        scratch_shapes=[pltpu.VMEM((full, full), jnp.float32)],
        compiler_params=pltpu.CompilerParams(vmem_limit_bytes=VMEM_BYTES),
        cost_estimate=LIGHT,
        name="gram_blocks",
    )(*after, *cells)


def cross_kernel(shares, *refs):
    out_ref, acc_ref = refs[-2:]
    step = pl.program_id(0)

    @pl.when(step == 0)
    def _():
        acc_ref[...] = jnp.zeros_like(acc_ref)

    count = shares // 2 + 1
    rows = refs[0].shape[1]
    y_refs, y_shares = refs[count:-2], []
    while y_refs:
        cuts = rows // y_refs[0].shape[1]
        y_shares.append(jnp.concatenate([ref[...] for ref in y_refs[:cuts]], axis=1))
        y_refs = y_refs[cuts:]
    acc_ref[...] += lax.dot_general(
        whole_rows(by_distance(refs[:count])),
        whole_rows(y_shares),
        ROWS_BY_ROWS,
        preferred_element_type=jnp.float32,
    )

    @pl.when(step == pl.num_programs(0) - 1)
    def _():
        mine = lax.axis_index("snap")
        for a in range(shares):
            rows = pl.ds(pl.multiple_of((mine ^ a) * TILE, TILE), TILE)
            for b in range(shares):
                lanes = pl.ds(pl.multiple_of((mine ^ b) * TILE, TILE), TILE)
                out_ref[rows, lanes] = acc_ref[
                    a * TILE : (a + 1) * TILE, b * TILE : (b + 1) * TILE
                ]


def cross_sum(x_cells, y_cells, after, steps=4):
    shares, blocks, rows, width = x_cells[-1].shape
    full = shares * width
    specs = cell_specs(shares, blocks // steps, rows, width, 0)
    for piece in y_cells:
        specs.append(pl.BlockSpec((blocks // steps, piece.shape[1], width), lambda i: (i, 0, 0)))
    return pl.pallas_call(
        lambda *refs: cross_kernel(shares, *refs[len(after) :]),
        grid=(steps,),
        out_shape=jax.ShapeDtypeStruct((full, full), jnp.float32),
        in_specs=[ANY] * len(after) + specs,
        out_specs=pl.BlockSpec((full, full), lambda i: (0, 0)),
        scratch_shapes=[pltpu.VMEM((full, full), jnp.float32)],
        compiler_params=pltpu.CompilerParams(vmem_limit_bytes=VMEM_BYTES),
        cost_estimate=LIGHT,
        name="cross_sum",
    )(*after, *x_cells, *y_cells)


def three_terms(value):
    high = value.astype(jnp.bfloat16).astype(jnp.float32)
    rest = value - high
    middle = rest.astype(jnp.bfloat16).astype(jnp.float32)
    return high, middle, rest - middle


def lane_of(row, lane):
    return jnp.broadcast_to(row[:, lane : lane + 1], row.shape)


def row_of(ref, row):
    return jnp.broadcast_to(ref[row : row + 1, :], (GROUP, TILE))


def factor_tile(a_ref, w_ref, u_ref, v_ref):
    panels = TILE // GROUP
    a_rows = [row_of(a_ref, i) for i in range(GROUP)]
    w_rows = [row_of(w_ref, i) for i in range(GROUP)]
    for p in range(panels):
        base = p * GROUP
        small = {
            (i, k): lane_of(a_rows[i], base + k) for i in range(GROUP) for k in range(i, GROUP)
        }
        for j in range(GROUP):
            scale = lax.rsqrt(small[j, j])
            a_rows[j] = a_rows[j] * scale
            w_rows[j] = w_rows[j] * scale
            u_ref[base + j : base + j + 1, :] = a_rows[j][:1]
            v_ref[base + j : base + j + 1, :] = w_rows[j][:1]
            below = {k: small[j, k] * scale for k in range(j + 1, GROUP)}
            for k in range(j + 1, GROUP):
                for m in range(k, GROUP):
                    small[k, m] = small[k, m] - below[k] * below[m]
            for k in range(j + 1, GROUP):
                a_rows[k] = a_rows[k] - below[k] * a_rows[j]
                w_rows[k] = w_rows[k] - below[k] * w_rows[j]
        if p + 1 == panels:
            break
        after = base + GROUP
        next_a = [row_of(a_ref, after + i) for i in range(GROUP)]
        next_w = [row_of(w_ref, after + i) for i in range(GROUP)]
        for i in range(GROUP):
            for k in range(GROUP):
                factor = lane_of(a_rows[k], after + i)
                next_a[i] = next_a[i] - factor * a_rows[k]
                next_w[i] = next_w[i] - factor * w_rows[k]
        if p + 2 < panels:
            done = after + GROUP
            u = u_ref[base:after, :]
            v = v_ref[base:after, :]
            uh, um, ul = three_terms(u)
            vh, vm, vl = three_terms(v)
            left = jnp.concatenate([uh, uh, um, uh, ul, um], axis=0).astype(jnp.bfloat16)
            right_a = jnp.concatenate([uh, um, uh, ul, uh, um], axis=0)
            right_w = jnp.concatenate([vh, vm, vh, vl, vh, vm], axis=0)
            right = jnp.concatenate([right_a, right_w], axis=1).astype(jnp.bfloat16)
            update = lax.dot_general(
                left, right, ROWS_BY_ROWS, preferred_element_type=jnp.float32
            )
            a_ref[done:, :] = a_ref[done:, :] - update[done:, :TILE]
            w_ref[done:, :] = w_ref[done:, :] - update[done:, TILE:]
        a_rows, w_rows = next_a, next_w


def factor_step(tiles, b, wide, a_ref, w_ref, u_ref, v_ref):
    row = lax.broadcasted_iota(jnp.int32, (TILE, TILE), 0)
    lane = lax.broadcasted_iota(jnp.int32, (TILE, TILE), 1)
    a_ref[...] = wide[b, b]
    w_ref[...] = jnp.where(row == lane, 1.0, 0.0)
    factor_tile(a_ref, w_ref, u_ref, v_ref)
    inverse = v_ref[...]
    wide[b, b] = jnp.where(row <= lane, u_ref[...], 0.0)
    wide[b, tiles + b] = inverse
    for j in range(1, tiles):
        wide[b, b + j] = lax.dot(
            inverse, wide[b, b + j], precision=HIGHEST, preferred_element_type=jnp.float32
        )
    for r in range(b + 1, tiles):
        for c in list(range(r, tiles)) + list(range(tiles, tiles + b + 1)):
            update = lax.dot_general(
                wide[b, r],
                wide[b, c],
                ROWS_BY_ROWS,
                precision=HIGHEST,
                preferred_element_type=jnp.float32,
            )
            wide[r, c] = -update if c == tiles + b else wide[r, c] - update


def first_kernel(tiles, rows_total, g_ref, wide, *scratch):
    at = 0
    for a in range(tiles):
        for b in range(a, tiles):
            wide[a, b] = g_ref[at] / rows_total
            at += 1
    factor_step(tiles, 0, wide, *scratch)


def next_kernel(tiles, b, _, wide, *scratch):
    factor_step(tiles, b, wide, *scratch)


def last_kernel(tiles, wide, r_ref, inv_ref, hi_ref, mid_ref, lo_ref, *scratch):
    factor_step(tiles, tiles - 1, wide, *scratch)
    zero = jnp.zeros((TILE, TILE), jnp.float32)
    mine = lax.axis_index("snap")
    for a in range(tiles):
        rows = slice(a * TILE, (a + 1) * TILE)
        for b in range(tiles):
            lanes = slice(b * TILE, (b + 1) * TILE)
            r_ref[rows, lanes] = wide[a, b] if b >= a else zero
            value = wide[a, tiles + b] if b <= a else zero
            inv_ref[rows, lanes] = value
            high, middle, low = three_terms(value)
            lanes = pl.ds(pl.multiple_of((mine ^ b) * TILE, TILE), TILE)
            hi_ref[rows, lanes] = high.astype(jnp.bfloat16)
            mid_ref[rows, lanes] = middle.astype(jnp.bfloat16)
            lo_ref[rows, lanes] = low.astype(jnp.bfloat16)


def factor_call(kernel, out_shape, value, after, aliases, tiles):
    many = isinstance(out_shape, tuple)
    return pl.pallas_call(
        lambda *refs: kernel(*refs[len(after) :]),
        out_shape=out_shape,
        in_specs=[ANY] * len(after) + [VMEM],
        out_specs=(VMEM,) * len(out_shape) if many else VMEM,
        scratch_shapes=[pltpu.VMEM((TILE, TILE), jnp.float32)] * 4,
        input_output_aliases={len(after): 0} if aliases else {},
        compiler_params=pltpu.CompilerParams(vmem_limit_bytes=VMEM_BYTES),
        cost_estimate=LIGHT,
        name="factor",
    )(*after, value)


def factor_steps(blocks, tiles, rows_total, after):
    state = jax.ShapeDtypeStruct((tiles, 2 * tiles, TILE, TILE), jnp.float32)
    full = jax.ShapeDtypeStruct((tiles * TILE, tiles * TILE), jnp.float32)
    term = jax.ShapeDtypeStruct(full.shape, jnp.bfloat16)
    value = factor_call(
        lambda *refs: first_kernel(tiles, rows_total, *refs), state, blocks, after, False, tiles
    )
    for b in range(1, tiles - 1):
        after = yield value
        value = factor_call(
            lambda *refs: next_kernel(tiles, b, *refs), state, value, after, True, tiles
        )
    after = yield value
    yield factor_call(
        lambda *refs: last_kernel(tiles, *refs), (full, full, term, term, term), value, after, False, tiles
    )


def basis_kernel(*refs):
    hi_ref, mid_ref, lo_ref, out_ref = refs[-4:]
    cells = whole_rows(by_distance(refs[:-4]))
    total = lax.dot_general(
        cells, lo_ref[...], LANES_BY_LANES, preferred_element_type=jnp.float32
    )
    total += lax.dot_general(
        cells, mid_ref[...], LANES_BY_LANES, preferred_element_type=jnp.float32
    )
    total += lax.dot_general(
        cells, hi_ref[...], LANES_BY_LANES, preferred_element_type=jnp.float32
    )
    out_ref[...] = total.reshape(out_ref.shape)


def basis(cells, terms, call, calls, filled, after, steps=4):
    shares, blocks, rows, width = cells[-1].shape
    full = shares * width
    size = blocks // calls // steps
    first = call * steps
    term = pl.BlockSpec((full, full), lambda i: (0, 0))
    unread = ([] if filled is None else [filled]) + list(after)
    return pl.pallas_call(
        lambda *refs: basis_kernel(*refs[len(unread) :]),
        grid=(steps,),
        out_shape=jax.ShapeDtypeStruct((blocks, rows, full), jnp.float32),
        in_specs=[ANY] * len(unread) + cell_specs(shares, size, rows, width, first) + [term] * 3,
        out_specs=pl.BlockSpec((size, rows, full), lambda i: (first + i, 0, 0)),
        input_output_aliases={} if filled is None else {0: 0},
        compiler_params=pltpu.CompilerParams(vmem_limit_bytes=VMEM_BYTES),
        cost_estimate=LIGHT,
        name="basis",
    )(*unread, *cells, *terms)


def sum_kernel(count, copies, value_ref, out_ref):
    rows = value_ref.shape[0] // count
    total = value_ref[:rows]
    for i in range(1, count):
        total += value_ref[i * rows : (i + 1) * rows]
    for i in range(copies):
        out_ref[i * rows : (i + 1) * rows] = total


def sum_pieces(value, count, after, copies=1):
    rows, lanes = value.shape
    return pl.pallas_call(
        lambda *refs: sum_kernel(count, copies, *refs[len(after) :]),
        out_shape=jax.ShapeDtypeStruct((rows // count * copies, lanes), value.dtype),
        in_specs=[ANY] * len(after) + [VMEM],
        out_specs=VMEM,
        cost_estimate=LIGHT,
        name="sum_pieces",
    )(*after, value)


def add_kernel(one_ref, two_ref, out_ref):
    out_ref[...] = one_ref[...] + two_ref[...]


def add(one, two, after):
    return pl.pallas_call(
        lambda *refs: add_kernel(*refs[len(after) :]),
        out_shape=jax.ShapeDtypeStruct(one.shape, one.dtype),
        in_specs=[ANY] * len(after) + [VMEM, VMEM],
        out_specs=VMEM,
        cost_estimate=LIGHT,
        name="add",
    )(*after, one, two)


def join_kernel(*refs):
    rows = refs[0].shape[0]
    for i, ref in enumerate(refs[:-1]):
        refs[-1][i * rows : (i + 1) * rows] = ref[...]


def join(values, after):
    rows, lanes = values[0].shape
    return pl.pallas_call(
        lambda *refs: join_kernel(*refs[len(after) :]),
        out_shape=jax.ShapeDtypeStruct((len(values) * rows, lanes), values[0].dtype),
        in_specs=[ANY] * len(after) + [VMEM] * len(values),
        out_specs=VMEM,
        cost_estimate=LIGHT,
        name="join",
    )(*after, *values)


def projection_kernel(slabs, divisor, inverse_ref, same_ref, other_ref, out_ref, cross_ref):
    me = lax.axis_index("space")
    rows = cross_ref.shape[0] // slabs
    for away in range(slabs):
        at = pl.ds(pl.multiple_of((me ^ away) * rows, rows), rows)
        chip = slice(away // CORES * rows, (away // CORES + 1) * rows)
        cross_ref[at, :] = (other_ref if away % CORES else same_ref)[chip]
    out_ref[...] = (
        lax.dot(
            inverse_ref[...],
            cross_ref[...],
            precision=HIGHEST,
            preferred_element_type=jnp.float32,
        )
        / divisor
    )


def project(inverse, same, other, slabs, divisor):
    return pl.pallas_call(
        lambda *refs: projection_kernel(slabs, divisor, *refs),
        out_shape=jax.ShapeDtypeStruct(inverse.shape, jnp.float32),
        in_specs=[VMEM] * 3,
        out_specs=VMEM,
        scratch_shapes=[pltpu.VMEM(inverse.shape, jnp.float32)],
        compiler_params=pltpu.CompilerParams(vmem_limit_bytes=VMEM_BYTES),
        name="project",
    )(inverse, same, other)


def swap(value, axis, mask):
    return lax.ppermute(value, axis, [(i, i ^ mask) for i in range(lax.axis_size(axis))])


def body(owned_x, owned_y, patch_dest):
    slabs = lax.axis_size("space")
    shares = lax.axis_size("snap")
    slots, patch, width = owned_x.shape
    per_slab = slots // 2
    rows_total = slabs * per_slab * patch
    full = shares * width
    tiles = full // TILE
    pairs = tiles * (tiles + 1) // 2
    half = shares // 2
    shares_of = (tuple(range(half, shares)), tuple(range(half)))

    def packed(owned, groups, with_ids, after):
        cells = owned.reshape(slots, shares, patch // shares, width)
        return pack(patch_dest, cells, slabs, per_slab, groups, with_ids, after)

    def merged(sent, after):
        return merge(sent[0], swap(sent[1], "space", 1), slabs // CORES, after)

    def to_chips(joined):
        return [joined[0]] + [swap(joined[m], "space", CORES * m) for m in range(1, len(joined))]

    def to_pieces(value, axis="space"):
        return lax.all_to_all(value, axis, split_axis=0, concat_axis=0, tiled=True)

    def place_far(meta, moved, after):
        pieces, meta = settle(
            meta, moved, slots // slabs, per_slab, shares, shares_of[0], 1, after
        )
        return to_pieces(pieces[0], "snap"), meta

    def place(meta, moved, group, cuts, after):
        pieces, _ = settle(meta, moved, slots // slabs, per_slab, shares, (), cuts, after)
        return pieces, [
            swap(piece, "snap", shares_of[group][k // cuts]) if shares_of[group][k // cuts] else piece
            for k, piece in enumerate(pieces)
        ]

    def hops():
        hop = 1
        while hop < shares:
            yield hop
            hop *= 2

    chips = slabs // CORES
    sent_x = packed(owned_x, shares_of, True, [])
    ((same_y, other_y),) = packed(owned_y, (shares_of[0] + shares_of[1],), False, [])
    other_y = swap(other_y, "space", 1)
    joined_near = merged(sent_x[1], [])
    far = to_chips(merged(sent_x[0], []))
    x_far, meta = place_far(None, far, [other_y, joined_near[0]])
    near = to_chips(joined_near)
    y_far = to_chips(merge(same_y, other_y, chips, near[1:3], slice(0, half), shares))
    y_near = to_chips(merge(same_y, other_y, chips, y_far[1:3], slice(half, shares), shares))
    _, x_near = place(meta, near, 1, 1, [])
    x_cells = x_near + [x_far]

    gram_local = gram_blocks(x_cells, y_far[1:2])
    gram = to_pieces(gram_local.reshape(pairs * TILE, TILE))
    settled, y_far = place(meta, y_far, 0, 2, [gram_local])
    gram = sum_pieces(gram, slabs, settled[:1], shares)
    gram = sum_pieces(to_pieces(gram, "snap"), shares, [y_far[0], y_far[2]] + y_near[1:3])
    settled, y_near = place(meta, y_near, 1, 1, [gram])
    y_cells = y_near + y_far
    gram = lax.all_gather(gram, "space", axis=0, tiled=True)

    steps = factor_steps(gram.reshape(pairs, TILE, TILE), tiles, rows_total, settled[:1])
    state = next(steps)
    for _ in range(tiles - 3):
        state = steps.send([])
    cross_local = cross_sum(x_cells, y_cells, [state])
    state = steps.send([cross_local])
    cross = sum_pieces(to_pieces(cross_local), slabs, [state])
    r_factor, inverse, *terms = steps.send([cross])
    tied = [r_factor]
    for hop in hops():
        cross = add(cross, swap(cross, "snap", hop), tied)
        if hop == 1:
            q_basis = basis(x_cells, terms, 0, 2, None, [cross])
            tied = [q_basis]
    q_basis = basis(x_cells, terms, 1, 2, q_basis, [cross])
    same = join([cross] + [swap(cross, "space", m) for m in range(CORES, slabs, CORES)], [q_basis])
    projection = project(inverse, same, swap(same, "space", 1), slabs, math.sqrt(rows_total))
    return q_basis, r_factor, projection


def solution(mesh):
    in_specs = (P("space", None, "snap"), P("space", None, "snap"), P("space"))
    out_specs = (P("space", "snap", None), P(), P())
    return jax.shard_map(body, mesh=mesh, in_specs=in_specs, out_specs=out_specs, check_vma=False)
```

```python
import math

import jax
import jax.numpy as jnp
from jax import lax
from jax.experimental import pallas as pl
from jax.experimental.pallas import tpu as pltpu
from jax.sharding import PartitionSpec as P

TILE = 128
GROUP = 8
CORES = 2
VMEM_BYTES = 32 * 1024 * 1024
GRID_VMEM_BYTES = 56 * 1024 * 1024
HIGHEST = lax.Precision.HIGHEST
SMEM = pl.BlockSpec(memory_space=pltpu.SMEM)
VMEM = pl.BlockSpec(memory_space=pltpu.VMEM)
ANY = pl.BlockSpec(memory_space=pl.ANY)
LIGHT = pl.CostEstimate(flops=1, bytes_accessed=1, transcendentals=0)
ROWS_BY_ROWS = (((0,), (0,)), ((), ()))
LANES_BY_LANES = (((1,), (1,)), ((), ()))


def pack_kernel(slabs, capacity, per_slab, shares_of, dest_ref, owned_ref, *refs):
    out_refs, (ids_ref, count_ref) = refs[:-2], refs[-2:]
    chips = slabs // CORES
    me = lax.axis_index("space")
    mine = lax.axis_index("snap")
    lane = lax.broadcasted_iota(jnp.int32, (1, TILE), 1)
    ids_ref[...] = jnp.full_like(ids_ref, -1)
    for slab in range(slabs):
        count_ref[slab] = 0

    def place(i, _):
        block = dest_ref[i]

        @pl.when(block >= 0)
        def _():
            slab = lax.div(block, per_slab)
            rank = count_ref[slab]
            count_ref[slab] = rank + 1
            here = pl.ds(slab, 1)
            ids_ref[here, :] = jnp.where(lane == rank, block - slab * per_slab, ids_ref[here, :])
            away = slab ^ me
            chip = lax.shift_right_logical(away, 1)
            for core in range(CORES):

                @pl.when((away & 1) == core)
                def _():
                    for group, shares in enumerate(shares_of):
                        out_ref = out_refs[group * CORES + core]
                        at = chip * (out_ref.shape[0] // chips) + rank * len(shares)
                        for k, share in enumerate(shares):
                            out_ref[at + k] = owned_ref[i, mine ^ share]

        return 0

    lax.fori_loop(0, dest_ref.shape[0], place, 0, unroll=2)
    for group, shares in enumerate(shares_of):
        used = capacity * len(shares)
        for away in range(slabs):
            out_ref = out_refs[group * CORES + away % CORES]
            span = out_ref.shape[0] // chips
            if span > used:
                ids = ids_ref[pl.ds(me ^ away, 1), :].astype(jnp.float32)
                tile = jnp.broadcast_to(ids, out_ref.shape[1:]).astype(out_ref.dtype)
                out_ref[away // CORES * span + used] = tile


def pack(dest, owned, slabs, per_slab, shares_of, with_ids, after):
    slots, _, rows, width = owned.shape
    chips = slabs // CORES
    capacity = slots // slabs
    sent = []
    for group, shares in enumerate(shares_of):
        span = capacity * len(shares) + (1 if with_ids and group == 0 else 0)
        sent += [jax.ShapeDtypeStruct((chips * span, rows, width), owned.dtype)] * CORES
    outs = pl.pallas_call(
        lambda *refs: pack_kernel(slabs, capacity, per_slab, shares_of, *refs[len(after) :]),
        out_shape=tuple(sent),
        in_specs=[ANY] * len(after) + [SMEM, VMEM],
        out_specs=(VMEM,) * len(sent),
        scratch_shapes=[
            pltpu.VMEM((slabs, TILE), jnp.int32),
            pltpu.SMEM((slabs,), jnp.int32),
        ],
        compiler_params=pltpu.CompilerParams(vmem_limit_bytes=VMEM_BYTES),
        cost_estimate=LIGHT,
        name="pack",
    )(*after, dest, owned)
    return [outs[at : at + CORES] for at in range(0, len(outs), CORES)]


def merge_kernel(same_ref, other_ref, *out_refs):
    span = same_ref.shape[0] // len(out_refs)
    for chip, out_ref in enumerate(out_refs):
        out_ref[:span] = same_ref[chip * span : (chip + 1) * span]
        out_ref[span:] = other_ref[chip * span : (chip + 1) * span]


def pick_kernel(picked, same_ref, other_ref, *out_refs):
    for chip, out_ref in enumerate(out_refs):
        for owner, ref in enumerate((same_ref, other_ref)):
            out_ref[owner] = ref[chip, :, picked]


def merge(same, other, chips, after, picked=None, of=1):
    tiles, rows, width = same.shape
    if picked is None:
        kernel = merge_kernel
        shape = (CORES * tiles // chips, rows, width)
    else:
        kernel = lambda *refs: pick_kernel(picked, *refs)
        ranks = tiles // chips // of
        shape = (CORES, ranks, picked.stop - picked.start, rows, width)
        same, other = (value.reshape(chips, ranks, of, rows, width) for value in (same, other))
    outs = pl.pallas_call(
        lambda *refs: kernel(*refs[len(after) :]),
        out_shape=(jax.ShapeDtypeStruct(shape, same.dtype),) * chips,
        in_specs=[ANY] * len(after) + [VMEM, VMEM],
        out_specs=(VMEM,) * chips,
        compiler_params=pltpu.CompilerParams(vmem_limit_bytes=VMEM_BYTES),
        cost_estimate=LIGHT,
        name="merge",
    )(*after, same, other)
    return [out.reshape(-1, rows, width) for out in outs]


def settle_kernel(chips, capacity, with_ids, far, cuts, *refs):
    if with_ids:
        moved_refs, out_refs, meta_ref, ids_ref = refs[:chips], refs[chips:-2], refs[-2], refs[-1]
        span = moved_refs[0].shape[0] // CORES
        for source in range(chips * CORES):
            at = source % CORES * span + span - 1
            tile = moved_refs[source // CORES][at].astype(jnp.float32)
            ids_ref[source : source + 1, :] = tile[:1].astype(jnp.int32)
        pltpu.sync_copy(ids_ref, meta_ref)
    else:
        meta_ref, moved_refs, out_refs = refs[0], refs[1 : 1 + chips], refs[1 + chips :]
        span = moved_refs[0].shape[0] // CORES
    mine = lax.axis_index("snap")
    count = len(far) or len(out_refs) // cuts
    for source in range(chips * CORES):
        moved_ref = moved_refs[source // CORES]

        def place(rank, _):
            block = meta_ref[source, rank]

            @pl.when(block >= 0)
            def _():
                at = source % CORES * span + rank * count
                if far:
                    for k in range(count):
                        out_refs[0][mine ^ far[k], block] = moved_ref[at + k]
                else:
                    for k, out_ref in enumerate(out_refs):
                        rows = out_ref.shape[1]
                        cells = slice(k % cuts * rows, (k % cuts + 1) * rows)
                        out_ref[block] = moved_ref[at + k // cuts, cells]

            return 0

        lax.fori_loop(0, capacity, place, 0, unroll=4)


def settle(meta, moved, capacity, per_slab, shares, far, cuts, after):
    with_ids = meta is None
    chips = len(moved)
    rows, width = moved[0].shape[1:]
    if far:
        pieces = (jax.ShapeDtypeStruct((shares, per_slab, rows, width), moved[0].dtype),)
    else:
        piece = jax.ShapeDtypeStruct((per_slab, rows // cuts, width), moved[0].dtype)
        pieces = (piece,) * (shares // 2 * cuts)
    ids = jax.ShapeDtypeStruct((chips * CORES, TILE), jnp.int32)
    outs = pl.pallas_call(
        lambda *refs: settle_kernel(chips, capacity, with_ids, far, cuts, *refs[len(after) :]),
        out_shape=pieces + ((ids,) if with_ids else ()),
        in_specs=[ANY] * len(after) + ([] if with_ids else [SMEM]) + [VMEM] * chips,
        out_specs=(VMEM,) * len(pieces) + ((SMEM,) if with_ids else ()),
        scratch_shapes=[pltpu.VMEM((chips * CORES, TILE), jnp.int32)] if with_ids else [],
        compiler_params=pltpu.CompilerParams(vmem_limit_bytes=VMEM_BYTES),
        cost_estimate=LIGHT,
        name="settle",
    )(*after, *([] if with_ids else [meta]), *moved)
    return list(outs[: len(pieces)]), (outs[-1] if with_ids else meta)


def by_distance(refs):
    near = len(refs) - 1
    mine = lax.axis_index("snap")
    return list(refs[:near]) + [refs[near].at[mine ^ share] for share in range(near, 2 * near)]


def cell_specs(shares, size, rows, width, first):
    near = pl.BlockSpec((size, rows, width), lambda i: (first + i, 0, 0))
    far = pl.BlockSpec((shares, size, rows, width), lambda i: (0, first + i, 0, 0))
    return [near] * (shares // 2) + [far]


def whole_rows(refs):
    blocks, rows, width = refs[0].shape
    return jnp.concatenate([ref[...].reshape(blocks * rows, width) for ref in refs], axis=1)


def tile_of(row, lane, tiles):
    return row * tiles - lax.div(row * (row - 1), 2) + lane - row


def gram_kernel(shares, *refs):
    out_ref, acc_ref = refs[-2:]
    step = pl.program_id(0)

    @pl.when(step == 0)
    def _():
        acc_ref[...] = jnp.zeros_like(acc_ref)

    cells = whole_rows(by_distance(refs[:-2]))
    acc_ref[...] += lax.dot_general(
        cells, cells, ROWS_BY_ROWS, preferred_element_type=jnp.float32
    )

    @pl.when(step == pl.num_programs(0) - 1)
    def _():
        mine = lax.axis_index("snap")
        for a in range(shares):
            for b in range(shares):
                row, lane = mine ^ a, mine ^ b

                @pl.when(row <= lane)
                def _():
                    out_ref[tile_of(row, lane, shares)] = acc_ref[
                        a * TILE : (a + 1) * TILE, b * TILE : (b + 1) * TILE
                    ]


def gram_blocks(cells, after, steps=4):
    shares, blocks, rows, width = cells[-1].shape
    pairs = shares * (shares + 1) // 2
    full = shares * width
    return pl.pallas_call(
        lambda *refs: gram_kernel(shares, *refs[len(after) :]),
        grid=(steps,),
        out_shape=jax.ShapeDtypeStruct((pairs, TILE, TILE), jnp.float32),
        in_specs=[ANY] * len(after) + cell_specs(shares, blocks // steps, rows, width, 0),
        out_specs=pl.BlockSpec((pairs, TILE, TILE), lambda i: (0, 0, 0)),
        scratch_shapes=[pltpu.VMEM((full, full), jnp.float32)],
        compiler_params=pltpu.CompilerParams(vmem_limit_bytes=GRID_VMEM_BYTES),
        cost_estimate=LIGHT,
        name="gram_blocks",
    )(*after, *cells)


def cross_kernel(shares, *refs):
    out_ref, acc_ref = refs[-2:]
    step = pl.program_id(0)

    @pl.when(step == 0)
    def _():
        acc_ref[...] = jnp.zeros_like(acc_ref)

    count = shares // 2 + 1
    rows = refs[0].shape[1]
    y_refs, y_shares = refs[count:-2], []
    while y_refs:
        cuts = rows // y_refs[0].shape[1]
        y_shares.append(jnp.concatenate([ref[...] for ref in y_refs[:cuts]], axis=1))
        y_refs = y_refs[cuts:]
    acc_ref[...] += lax.dot_general(
        whole_rows(by_distance(refs[:count])),
        whole_rows(y_shares),
        ROWS_BY_ROWS,
        preferred_element_type=jnp.float32,
    )

    @pl.when(step == pl.num_programs(0) - 1)
    def _():
        mine = lax.axis_index("snap")
        for a in range(shares):
            rows = pl.ds(pl.multiple_of((mine ^ a) * TILE, TILE), TILE)
            for b in range(shares):
                lanes = pl.ds(pl.multiple_of((mine ^ b) * TILE, TILE), TILE)
                out_ref[rows, lanes] = acc_ref[
                    a * TILE : (a + 1) * TILE, b * TILE : (b + 1) * TILE
                ]


def cross_sum(x_cells, y_cells, after, steps=4):
    shares, blocks, rows, width = x_cells[-1].shape
    full = shares * width
    specs = cell_specs(shares, blocks // steps, rows, width, 0)
    for piece in y_cells:
        specs.append(pl.BlockSpec((blocks // steps, piece.shape[1], width), lambda i: (i, 0, 0)))
    return pl.pallas_call(
        lambda *refs: cross_kernel(shares, *refs[len(after) :]),
        grid=(steps,),
        out_shape=jax.ShapeDtypeStruct((full, full), jnp.float32),
        in_specs=[ANY] * len(after) + specs,
        out_specs=pl.BlockSpec((full, full), lambda i: (0, 0)),
        scratch_shapes=[pltpu.VMEM((full, full), jnp.float32)],
        compiler_params=pltpu.CompilerParams(vmem_limit_bytes=GRID_VMEM_BYTES),
        cost_estimate=LIGHT,
        name="cross_sum",
    )(*after, *x_cells, *y_cells)


def three_terms(value):
    high = value.astype(jnp.bfloat16).astype(jnp.float32)
    rest = value - high
    middle = rest.astype(jnp.bfloat16).astype(jnp.float32)
    return high, middle, rest - middle


def lane_of(row, lane):
    return jnp.broadcast_to(row[:, lane : lane + 1], row.shape)


def row_of(ref, row):
    return jnp.broadcast_to(ref[row : row + 1, :], (GROUP, TILE))


def factor_tile(a_ref, w_ref, u_ref, v_ref):
    panels = TILE // GROUP
    a_rows = [row_of(a_ref, i) for i in range(GROUP)]
    w_rows = [row_of(w_ref, i) for i in range(GROUP)]
    for p in range(panels):
        base = p * GROUP
        small = {
            (i, k): lane_of(a_rows[i], base + k) for i in range(GROUP) for k in range(i, GROUP)
        }
        for j in range(GROUP):
            scale = lax.rsqrt(small[j, j])
            a_rows[j] = a_rows[j] * scale
            w_rows[j] = w_rows[j] * scale
            u_ref[base + j : base + j + 1, :] = a_rows[j][:1]
            v_ref[base + j : base + j + 1, :] = w_rows[j][:1]
            below = {k: small[j, k] * scale for k in range(j + 1, GROUP)}
            for k in range(j + 1, GROUP):
                for m in range(k, GROUP):
                    small[k, m] = small[k, m] - below[k] * below[m]
            for k in range(j + 1, GROUP):
                a_rows[k] = a_rows[k] - below[k] * a_rows[j]
                w_rows[k] = w_rows[k] - below[k] * w_rows[j]
        if p + 1 == panels:
            break
        after = base + GROUP
        next_a = [row_of(a_ref, after + i) for i in range(GROUP)]
        next_w = [row_of(w_ref, after + i) for i in range(GROUP)]
        for i in range(GROUP):
            for k in range(GROUP):
                factor = lane_of(a_rows[k], after + i)
                next_a[i] = next_a[i] - factor * a_rows[k]
                next_w[i] = next_w[i] - factor * w_rows[k]
        if p + 2 < panels:
            done = after + GROUP
            u = u_ref[base:after, :]
            v = v_ref[base:after, :]
            uh, um, ul = three_terms(u)
            vh, vm, vl = three_terms(v)
            left = jnp.concatenate([uh, uh, um, uh, ul, um], axis=0).astype(jnp.bfloat16)
            right_a = jnp.concatenate([uh, um, uh, ul, uh, um], axis=0)
            right_w = jnp.concatenate([vh, vm, vh, vl, vh, vm], axis=0)
            right = jnp.concatenate([right_a, right_w], axis=1).astype(jnp.bfloat16)
            update = lax.dot_general(
                left, right, ROWS_BY_ROWS, preferred_element_type=jnp.float32
            )
            a_ref[done:, :] = a_ref[done:, :] - update[done:, :TILE]
            w_ref[done:, :] = w_ref[done:, :] - update[done:, TILE:]
        a_rows, w_rows = next_a, next_w


def factor_step(tiles, b, wide, a_ref, w_ref, u_ref, v_ref):
    row = lax.broadcasted_iota(jnp.int32, (TILE, TILE), 0)
    lane = lax.broadcasted_iota(jnp.int32, (TILE, TILE), 1)
    a_ref[...] = wide[b, b]
    w_ref[...] = jnp.where(row == lane, 1.0, 0.0)
    factor_tile(a_ref, w_ref, u_ref, v_ref)
    inverse = v_ref[...]
    wide[b, b] = jnp.where(row <= lane, u_ref[...], 0.0)
    wide[b, tiles + b] = inverse
    for j in range(1, tiles):
        wide[b, b + j] = lax.dot(
            inverse, wide[b, b + j], precision=HIGHEST, preferred_element_type=jnp.float32
        )
    for r in range(b + 1, tiles):
        for c in list(range(r, tiles)) + list(range(tiles, tiles + b + 1)):
            update = lax.dot_general(
                wide[b, r],
                wide[b, c],
                ROWS_BY_ROWS,
                precision=HIGHEST,
                preferred_element_type=jnp.float32,
            )
            wide[r, c] = -update if c == tiles + b else wide[r, c] - update


def first_kernel(tiles, rows_total, g_ref, wide, *scratch):
    at = 0
    for a in range(tiles):
        for b in range(a, tiles):
            wide[a, b] = g_ref[at] / rows_total
            at += 1
    factor_step(tiles, 0, wide, *scratch)


def next_kernel(tiles, b, _, wide, *scratch):
    factor_step(tiles, b, wide, *scratch)


def last_kernel(tiles, wide, r_ref, inv_ref, hi_ref, mid_ref, lo_ref, *scratch):
    factor_step(tiles, tiles - 1, wide, *scratch)
    zero = jnp.zeros((TILE, TILE), jnp.float32)
    mine = lax.axis_index("snap")
    for a in range(tiles):
        rows = slice(a * TILE, (a + 1) * TILE)
        for b in range(tiles):
            lanes = slice(b * TILE, (b + 1) * TILE)
            r_ref[rows, lanes] = wide[a, b] if b >= a else zero
            value = wide[a, tiles + b] if b <= a else zero
            inv_ref[rows, lanes] = value
            high, middle, low = three_terms(value)
            lanes = pl.ds(pl.multiple_of((mine ^ b) * TILE, TILE), TILE)
            hi_ref[rows, lanes] = high.astype(jnp.bfloat16)
            mid_ref[rows, lanes] = middle.astype(jnp.bfloat16)
            lo_ref[rows, lanes] = low.astype(jnp.bfloat16)


def factor_call(kernel, out_shape, value, after, aliases, tiles):
    many = isinstance(out_shape, tuple)
    return pl.pallas_call(
        lambda *refs: kernel(*refs[len(after) :]),
        out_shape=out_shape,
        in_specs=[ANY] * len(after) + [VMEM],
        out_specs=(VMEM,) * len(out_shape) if many else VMEM,
        scratch_shapes=[pltpu.VMEM((TILE, TILE), jnp.float32)] * 4,
        input_output_aliases={len(after): 0} if aliases else {},
        compiler_params=pltpu.CompilerParams(vmem_limit_bytes=VMEM_BYTES),
        cost_estimate=LIGHT,
        name="factor",
    )(*after, value)


def factor_steps(blocks, tiles, rows_total, after):
    state = jax.ShapeDtypeStruct((tiles, 2 * tiles, TILE, TILE), jnp.float32)
    full = jax.ShapeDtypeStruct((tiles * TILE, tiles * TILE), jnp.float32)
    term = jax.ShapeDtypeStruct(full.shape, jnp.bfloat16)
    value = factor_call(
        lambda *refs: first_kernel(tiles, rows_total, *refs), state, blocks, after, False, tiles
    )
    for b in range(1, tiles - 1):
        after = yield value
        value = factor_call(
            lambda *refs: next_kernel(tiles, b, *refs), state, value, after, True, tiles
        )
    after = yield value
    yield factor_call(
        lambda *refs: last_kernel(tiles, *refs), (full, full, term, term, term), value, after, False, tiles
    )


def basis_kernel(*refs):
    hi_ref, mid_ref, lo_ref, out_ref = refs[-4:]
    cells = whole_rows(by_distance(refs[:-4]))
    total = lax.dot_general(
        cells, lo_ref[...], LANES_BY_LANES, preferred_element_type=jnp.float32
    )
    total += lax.dot_general(
        cells, mid_ref[...], LANES_BY_LANES, preferred_element_type=jnp.float32
    )
    total += lax.dot_general(
        cells, hi_ref[...], LANES_BY_LANES, preferred_element_type=jnp.float32
    )
    out_ref[...] = total.reshape(out_ref.shape)


def basis(cells, terms, call, calls, filled, after, steps=4):
    shares, blocks, rows, width = cells[-1].shape
    full = shares * width
    size = blocks // calls // steps
    first = call * steps
    term = pl.BlockSpec((full, full), lambda i: (0, 0))
    unread = ([] if filled is None else [filled]) + list(after)
    return pl.pallas_call(
        lambda *refs: basis_kernel(*refs[len(unread) :]),
        grid=(steps,),
        out_shape=jax.ShapeDtypeStruct((blocks, rows, full), jnp.float32),
        in_specs=[ANY] * len(unread) + cell_specs(shares, size, rows, width, first) + [term] * 3,
        out_specs=pl.BlockSpec((size, rows, full), lambda i: (first + i, 0, 0)),
        input_output_aliases={} if filled is None else {0: 0},
        compiler_params=pltpu.CompilerParams(vmem_limit_bytes=GRID_VMEM_BYTES),
        cost_estimate=LIGHT,
        name="basis",
    )(*unread, *cells, *terms)


def sum_kernel(count, copies, value_ref, out_ref):
    rows = value_ref.shape[0] // count
    total = value_ref[:rows]
    for i in range(1, count):
        total += value_ref[i * rows : (i + 1) * rows]
    for i in range(copies):
        out_ref[i * rows : (i + 1) * rows] = total


def sum_pieces(value, count, after, copies=1):
    rows, lanes = value.shape
    return pl.pallas_call(
        lambda *refs: sum_kernel(count, copies, *refs[len(after) :]),
        out_shape=jax.ShapeDtypeStruct((rows // count * copies, lanes), value.dtype),
        in_specs=[ANY] * len(after) + [VMEM],
        out_specs=VMEM,
        cost_estimate=LIGHT,
        name="sum_pieces",
    )(*after, value)


def add_kernel(one_ref, two_ref, out_ref):
    out_ref[...] = one_ref[...] + two_ref[...]


def add(one, two, after):
    return pl.pallas_call(
        lambda *refs: add_kernel(*refs[len(after) :]),
        out_shape=jax.ShapeDtypeStruct(one.shape, one.dtype),
        in_specs=[ANY] * len(after) + [VMEM, VMEM],
        out_specs=VMEM,
        cost_estimate=LIGHT,
        name="add",
    )(*after, one, two)


def join_kernel(*refs):
    rows = refs[0].shape[0]
    for i, ref in enumerate(refs[:-1]):
        refs[-1][i * rows : (i + 1) * rows] = ref[...]


def join(values, after):
    rows, lanes = values[0].shape
    return pl.pallas_call(
        lambda *refs: join_kernel(*refs[len(after) :]),
        out_shape=jax.ShapeDtypeStruct((len(values) * rows, lanes), values[0].dtype),
        in_specs=[ANY] * len(after) + [VMEM] * len(values),
        out_specs=VMEM,
        cost_estimate=LIGHT,
        name="join",
    )(*after, *values)


def projection_kernel(slabs, divisor, inverse_ref, same_ref, other_ref, out_ref, cross_ref):
    me = lax.axis_index("space")
    rows = cross_ref.shape[0] // slabs
    for away in range(slabs):
        at = pl.ds(pl.multiple_of((me ^ away) * rows, rows), rows)
        chip = slice(away // CORES * rows, (away // CORES + 1) * rows)
        cross_ref[at, :] = (other_ref if away % CORES else same_ref)[chip]
    out_ref[...] = (
        lax.dot(
            inverse_ref[...],
            cross_ref[...],
            precision=HIGHEST,
            preferred_element_type=jnp.float32,
        )
        / divisor
    )


def project(inverse, same, other, slabs, divisor):
    return pl.pallas_call(
        lambda *refs: projection_kernel(slabs, divisor, *refs),
        out_shape=jax.ShapeDtypeStruct(inverse.shape, jnp.float32),
        in_specs=[VMEM] * 3,
        out_specs=VMEM,
        scratch_shapes=[pltpu.VMEM(inverse.shape, jnp.float32)],
        compiler_params=pltpu.CompilerParams(vmem_limit_bytes=VMEM_BYTES),
        name="project",
    )(inverse, same, other)


def swap(value, axis, mask):
    return lax.ppermute(value, axis, [(i, i ^ mask) for i in range(lax.axis_size(axis))])


def body(owned_x, owned_y, patch_dest):
    slabs = lax.axis_size("space")
    shares = lax.axis_size("snap")
    slots, patch, width = owned_x.shape
    per_slab = slots // 2
    rows_total = slabs * per_slab * patch
    full = shares * width
    tiles = full // TILE
    pairs = tiles * (tiles + 1) // 2
    half = shares // 2
    shares_of = (tuple(range(half, shares)), tuple(range(half)))

    def packed(owned, groups, with_ids, after):
        cells = owned.reshape(slots, shares, patch // shares, width)
        return pack(patch_dest, cells, slabs, per_slab, groups, with_ids, after)

    def merged(sent, after):
        return merge(sent[0], swap(sent[1], "space", 1), slabs // CORES, after)

    def to_chips(joined):
        return [joined[0]] + [swap(joined[m], "space", CORES * m) for m in range(1, len(joined))]

    def to_pieces(value, axis="space"):
        return lax.all_to_all(value, axis, split_axis=0, concat_axis=0, tiled=True)

    def place_far(meta, moved, after):
        pieces, meta = settle(
            meta, moved, slots // slabs, per_slab, shares, shares_of[0], 1, after
        )
        return to_pieces(pieces[0], "snap"), meta

    def place(meta, moved, group, cuts, after):
        pieces, _ = settle(meta, moved, slots // slabs, per_slab, shares, (), cuts, after)
        return pieces, [
            swap(piece, "snap", shares_of[group][k // cuts]) if shares_of[group][k // cuts] else piece
            for k, piece in enumerate(pieces)
        ]

    def hops():
        hop = 1
        while hop < shares:
            yield hop
            hop *= 2

    chips = slabs // CORES
    sent_x = packed(owned_x, shares_of, True, [])
    ((same_y, other_y),) = packed(owned_y, (shares_of[0] + shares_of[1],), False, [])
    other_y = swap(other_y, "space", 1)
    joined_near = merged(sent_x[1], [])
    far = to_chips(merged(sent_x[0], []))
    x_far, meta = place_far(None, far, [other_y, joined_near[0]])
    near = to_chips(joined_near)
    y_far = to_chips(merge(same_y, other_y, chips, near[1:3], slice(0, half), shares))
    y_near = to_chips(merge(same_y, other_y, chips, y_far[1:3], slice(half, shares), shares))
    _, x_near = place(meta, near, 1, 1, [])
    x_cells = x_near + [x_far]

    gram_local = gram_blocks(x_cells, y_far[1:])
    gram = to_pieces(gram_local.reshape(pairs * TILE, TILE))
    settled, y_far = place(meta, y_far, 0, 2, [gram_local])
    gram = sum_pieces(gram, slabs, settled[:1], shares)
    gram = sum_pieces(to_pieces(gram, "snap"), shares, [y_far[0], y_far[2]] + y_near[1:3])
    settled, y_near = place(meta, y_near, 1, 1, [gram])
    y_cells = y_near + y_far
    gram = lax.all_gather(gram, "space", axis=0, tiled=True)

    steps = factor_steps(gram.reshape(pairs, TILE, TILE), tiles, rows_total, settled[:1])
    state = next(steps)
    for _ in range(tiles - 3):
        state = steps.send([])
    cross_local = cross_sum(x_cells, y_cells, [state])
    state = steps.send([cross_local])
    cross = sum_pieces(to_pieces(cross_local), slabs, [state])
    r_factor, inverse, *terms = steps.send([cross])
    tied = [r_factor]
    for hop in hops():
        cross = add(cross, swap(cross, "snap", hop), tied)
        if hop == 1:
            q_basis = basis(x_cells, terms, 0, 2, None, [cross])
            tied = [q_basis]
    q_basis = basis(x_cells, terms, 1, 2, q_basis, [cross])
    same = join([cross] + [swap(cross, "space", m) for m in range(CORES, slabs, CORES)], [q_basis])
    projection = project(inverse, same, swap(same, "space", 1), slabs, math.sqrt(rows_total))
    return q_basis, r_factor, projection


def solution(mesh):
    in_specs = (P("space", None, "snap"), P("space", None, "snap"), P("space"))
    out_specs = (P("space", "snap", None), P(), P())
    return jax.shard_map(body, mesh=mesh, in_specs=in_specs, out_specs=out_specs, check_vma=False)
```

```python
import math

import jax
import jax.numpy as jnp
from jax import lax
from jax.experimental import pallas as pl
from jax.experimental.pallas import tpu as pltpu
from jax.sharding import PartitionSpec as P

TILE = 128
GROUP = 8
CORES = 2
VMEM_BYTES = 32 * 1024 * 1024
GRID_VMEM_BYTES = 56 * 1024 * 1024
HIGHEST = lax.Precision.HIGHEST
SMEM = pl.BlockSpec(memory_space=pltpu.SMEM)
VMEM = pl.BlockSpec(memory_space=pltpu.VMEM)
ANY = pl.BlockSpec(memory_space=pl.ANY)
LIGHT = pl.CostEstimate(flops=1, bytes_accessed=1, transcendentals=0)
ROWS_BY_ROWS = (((0,), (0,)), ((), ()))
LANES_BY_LANES = (((1,), (1,)), ((), ()))


def pack_kernel(slabs, capacity, per_slab, shares_of, dest_ref, owned_ref, *refs):
    out_refs, (ids_ref, count_ref) = refs[:-2], refs[-2:]
    chips = slabs // CORES
    me = lax.axis_index("space")
    mine = lax.axis_index("snap")
    lane = lax.broadcasted_iota(jnp.int32, (1, TILE), 1)
    ids_ref[...] = jnp.full_like(ids_ref, -1)
    for slab in range(slabs):
        count_ref[slab] = 0

    def place(i, _):
        block = dest_ref[i]

        @pl.when(block >= 0)
        def _():
            slab = lax.div(block, per_slab)
            rank = count_ref[slab]
            count_ref[slab] = rank + 1
            here = pl.ds(slab, 1)
            ids_ref[here, :] = jnp.where(lane == rank, block - slab * per_slab, ids_ref[here, :])
            away = slab ^ me
            chip = lax.shift_right_logical(away, 1)
            for core in range(CORES):

                @pl.when((away & 1) == core)
                def _():
                    for group, shares in enumerate(shares_of):
                        out_ref = out_refs[group * CORES + core]
                        at = chip * (out_ref.shape[0] // chips) + rank * len(shares)
                        for k, share in enumerate(shares):
                            out_ref[at + k] = owned_ref[i, mine ^ share]

        return 0

    lax.fori_loop(0, dest_ref.shape[0], place, 0, unroll=2)
    for group, shares in enumerate(shares_of):
        used = capacity * len(shares)
        for away in range(slabs):
            out_ref = out_refs[group * CORES + away % CORES]
            span = out_ref.shape[0] // chips
            if span > used:
                ids = ids_ref[pl.ds(me ^ away, 1), :].astype(jnp.float32)
                tile = jnp.broadcast_to(ids, out_ref.shape[1:]).astype(out_ref.dtype)
                out_ref[away // CORES * span + used] = tile


def pack(dest, owned, slabs, per_slab, shares_of, with_ids, after):
    slots, _, rows, width = owned.shape
    chips = slabs // CORES
    capacity = slots // slabs
    sent = []
    for group, shares in enumerate(shares_of):
        span = capacity * len(shares) + (1 if with_ids and group == 0 else 0)
        sent += [jax.ShapeDtypeStruct((chips * span, rows, width), owned.dtype)] * CORES
    outs = pl.pallas_call(
        lambda *refs: pack_kernel(slabs, capacity, per_slab, shares_of, *refs[len(after) :]),
        out_shape=tuple(sent),
        in_specs=[ANY] * len(after) + [SMEM, VMEM],
        out_specs=(VMEM,) * len(sent),
        scratch_shapes=[
            pltpu.VMEM((slabs, TILE), jnp.int32),
            pltpu.SMEM((slabs,), jnp.int32),
        ],
        compiler_params=pltpu.CompilerParams(vmem_limit_bytes=VMEM_BYTES),
        cost_estimate=LIGHT,
        name="pack",
    )(*after, dest, owned)
    return [outs[at : at + CORES] for at in range(0, len(outs), CORES)]


def merge_kernel(same_ref, other_ref, *out_refs):
    span = same_ref.shape[0] // len(out_refs)
    for chip, out_ref in enumerate(out_refs):
        out_ref[:span] = same_ref[chip * span : (chip + 1) * span]
        out_ref[span:] = other_ref[chip * span : (chip + 1) * span]


def pick_kernel(picked, same_ref, other_ref, *out_refs):
    for chip, out_ref in enumerate(out_refs):
        for owner, ref in enumerate((same_ref, other_ref)):
            out_ref[owner] = ref[chip, :, picked]


def merge(same, other, chips, after, picked=None, of=1):
    tiles, rows, width = same.shape
    if picked is None:
        kernel = merge_kernel
        shape = (CORES * tiles // chips, rows, width)
    else:
        kernel = lambda *refs: pick_kernel(picked, *refs)
        ranks = tiles // chips // of
        shape = (CORES, ranks, picked.stop - picked.start, rows, width)
        same, other = (value.reshape(chips, ranks, of, rows, width) for value in (same, other))
    outs = pl.pallas_call(
        lambda *refs: kernel(*refs[len(after) :]),
        out_shape=(jax.ShapeDtypeStruct(shape, same.dtype),) * chips,
        in_specs=[ANY] * len(after) + [VMEM, VMEM],
        out_specs=(VMEM,) * chips,
        compiler_params=pltpu.CompilerParams(vmem_limit_bytes=VMEM_BYTES),
        cost_estimate=LIGHT,
        name="merge",
    )(*after, same, other)
    return [out.reshape(-1, rows, width) for out in outs]


def settle_kernel(chips, capacity, with_ids, far, cuts, *refs):
    if with_ids:
        moved_refs, out_refs, meta_ref, ids_ref = refs[:chips], refs[chips:-2], refs[-2], refs[-1]
        span = moved_refs[0].shape[0] // CORES
        for source in range(chips * CORES):
            at = source % CORES * span + span - 1
            tile = moved_refs[source // CORES][at].astype(jnp.float32)
            ids_ref[source : source + 1, :] = tile[:1].astype(jnp.int32)
        pltpu.sync_copy(ids_ref, meta_ref)
    else:
        meta_ref, moved_refs, out_refs = refs[0], refs[1 : 1 + chips], refs[1 + chips :]
        span = moved_refs[0].shape[0] // CORES
    mine = lax.axis_index("snap")
    count = len(far) or len(out_refs) // cuts
    for source in range(chips * CORES):
        moved_ref = moved_refs[source // CORES]

        def place(rank, _):
            block = meta_ref[source, rank]

            @pl.when(block >= 0)
            def _():
                at = source % CORES * span + rank * count
                if far:
                    for k in range(count):
                        out_refs[0][mine ^ far[k], block] = moved_ref[at + k]
                else:
                    for k, out_ref in enumerate(out_refs):
                        rows = out_ref.shape[1]
                        cells = slice(k % cuts * rows, (k % cuts + 1) * rows)
                        out_ref[block] = moved_ref[at + k // cuts, cells]

            return 0

        lax.fori_loop(0, capacity, place, 0, unroll=4)


def settle(meta, moved, capacity, per_slab, shares, far, count, cuts, after):
    with_ids = meta is None
    chips = len(moved)
    rows, width = moved[0].shape[1:]
    if far:
        pieces = (jax.ShapeDtypeStruct((shares, per_slab, rows, width), moved[0].dtype),)
    else:
        piece = jax.ShapeDtypeStruct((per_slab, rows // cuts, width), moved[0].dtype)
        pieces = (piece,) * (count * cuts)
    ids = jax.ShapeDtypeStruct((chips * CORES, TILE), jnp.int32)
    outs = pl.pallas_call(
        lambda *refs: settle_kernel(chips, capacity, with_ids, far, cuts, *refs[len(after) :]),
        out_shape=pieces + ((ids,) if with_ids else ()),
        in_specs=[ANY] * len(after) + ([] if with_ids else [SMEM]) + [VMEM] * chips,
        out_specs=(VMEM,) * len(pieces) + ((SMEM,) if with_ids else ()),
        scratch_shapes=[pltpu.VMEM((chips * CORES, TILE), jnp.int32)] if with_ids else [],
        compiler_params=pltpu.CompilerParams(vmem_limit_bytes=VMEM_BYTES),
        cost_estimate=LIGHT,
        name="settle",
    )(*after, *([] if with_ids else [meta]), *moved)
    return list(outs[: len(pieces)]), (outs[-1] if with_ids else meta)


def by_distance(refs):
    near = len(refs) - 1
    mine = lax.axis_index("snap")
    return list(refs[:near]) + [refs[near].at[mine ^ share] for share in range(near, refs[near].shape[0])]


def cell_specs(shares, size, rows, width, first):
    near = pl.BlockSpec((size, rows, width), lambda i: (first + i, 0, 0))
    far = pl.BlockSpec((shares, size, rows, width), lambda i: (0, first + i, 0, 0))
    return [near, far]


def whole_rows(refs):
    blocks, rows, width = refs[0].shape
    return jnp.concatenate([ref[...].reshape(blocks * rows, width) for ref in refs], axis=1)


def tile_of(row, lane, tiles):
    return row * tiles - lax.div(row * (row - 1), 2) + lane - row


def gram_kernel(shares, *refs):
    out_ref, acc_ref = refs[-2:]
    step = pl.program_id(0)

    @pl.when(step == 0)
    def _():
        acc_ref[...] = jnp.zeros_like(acc_ref)

    cells = whole_rows(by_distance(refs[:-2]))
    acc_ref[...] += lax.dot_general(
        cells, cells, ROWS_BY_ROWS, preferred_element_type=jnp.float32
    )

    @pl.when(step == pl.num_programs(0) - 1)
    def _():
        mine = lax.axis_index("snap")
        for a in range(shares):
            for b in range(shares):
                row, lane = mine ^ a, mine ^ b

                @pl.when(row <= lane)
                def _():
                    out_ref[tile_of(row, lane, shares)] = acc_ref[
                        a * TILE : (a + 1) * TILE, b * TILE : (b + 1) * TILE
                    ]


def gram_blocks(cells, after, steps=4):
    shares, blocks, rows, width = cells[-1].shape
    pairs = shares * (shares + 1) // 2
    full = shares * width
    return pl.pallas_call(
        lambda *refs: gram_kernel(shares, *refs[len(after) :]),
        grid=(steps,),
        out_shape=jax.ShapeDtypeStruct((pairs, TILE, TILE), jnp.float32),
        in_specs=[ANY] * len(after) + cell_specs(shares, blocks // steps, rows, width, 0),
        out_specs=pl.BlockSpec((pairs, TILE, TILE), lambda i: (0, 0, 0)),
        scratch_shapes=[pltpu.VMEM((full, full), jnp.float32)],
        compiler_params=pltpu.CompilerParams(vmem_limit_bytes=GRID_VMEM_BYTES),
        cost_estimate=LIGHT,
        name="gram_blocks",
    )(*after, *cells)


def cross_kernel(shares, *refs):
    out_ref, acc_ref = refs[-2:]
    step = pl.program_id(0)

    @pl.when(step == 0)
    def _():
        acc_ref[...] = jnp.zeros_like(acc_ref)

    count = 2
    rows = refs[0].shape[1]
    y_refs, y_shares = refs[count:-2], []
    while y_refs:
        cuts = rows // y_refs[0].shape[1]
        y_shares.append(jnp.concatenate([ref[...] for ref in y_refs[:cuts]], axis=1))
        y_refs = y_refs[cuts:]
    acc_ref[...] += lax.dot_general(
        whole_rows(by_distance(refs[:count])),
        whole_rows(y_shares),
        ROWS_BY_ROWS,
        preferred_element_type=jnp.float32,
    )

    @pl.when(step == pl.num_programs(0) - 1)
    def _():
        mine = lax.axis_index("snap")
        for a in range(shares):
            rows = pl.ds(pl.multiple_of((mine ^ a) * TILE, TILE), TILE)
            for b in range(shares):
                lanes = pl.ds(pl.multiple_of((mine ^ b) * TILE, TILE), TILE)
                out_ref[rows, lanes] = acc_ref[
                    a * TILE : (a + 1) * TILE, b * TILE : (b + 1) * TILE
                ]


def cross_sum(x_cells, y_cells, after, steps=4):
    shares, blocks, rows, width = x_cells[-1].shape
    full = shares * width
    specs = cell_specs(shares, blocks // steps, rows, width, 0)
    for piece in y_cells:
        specs.append(pl.BlockSpec((blocks // steps, piece.shape[1], width), lambda i: (i, 0, 0)))
    return pl.pallas_call(
        lambda *refs: cross_kernel(shares, *refs[len(after) :]),
        grid=(steps,),
        out_shape=jax.ShapeDtypeStruct((full, full), jnp.float32),
        in_specs=[ANY] * len(after) + specs,
        out_specs=pl.BlockSpec((full, full), lambda i: (0, 0)),
        scratch_shapes=[pltpu.VMEM((full, full), jnp.float32)],
        compiler_params=pltpu.CompilerParams(vmem_limit_bytes=GRID_VMEM_BYTES),
        cost_estimate=LIGHT,
        name="cross_sum",
    )(*after, *x_cells, *y_cells)


def three_terms(value):
    high = value.astype(jnp.bfloat16).astype(jnp.float32)
    rest = value - high
    middle = rest.astype(jnp.bfloat16).astype(jnp.float32)
    return high, middle, rest - middle


def lane_of(row, lane):
    return jnp.broadcast_to(row[:, lane : lane + 1], row.shape)


def row_of(ref, row):
    return jnp.broadcast_to(ref[row : row + 1, :], (GROUP, TILE))


def factor_tile(a_ref, w_ref, u_ref, v_ref):
    panels = TILE // GROUP
    a_rows = [row_of(a_ref, i) for i in range(GROUP)]
    w_rows = [row_of(w_ref, i) for i in range(GROUP)]
    for p in range(panels):
        base = p * GROUP
        small = {
            (i, k): lane_of(a_rows[i], base + k) for i in range(GROUP) for k in range(i, GROUP)
        }
        for j in range(GROUP):
            scale = lax.rsqrt(small[j, j])
            a_rows[j] = a_rows[j] * scale
            w_rows[j] = w_rows[j] * scale
            u_ref[base + j : base + j + 1, :] = a_rows[j][:1]
            v_ref[base + j : base + j + 1, :] = w_rows[j][:1]
            below = {k: small[j, k] * scale for k in range(j + 1, GROUP)}
            for k in range(j + 1, GROUP):
                for m in range(k, GROUP):
                    small[k, m] = small[k, m] - below[k] * below[m]
            for k in range(j + 1, GROUP):
                a_rows[k] = a_rows[k] - below[k] * a_rows[j]
                w_rows[k] = w_rows[k] - below[k] * w_rows[j]
        if p + 1 == panels:
            break
        after = base + GROUP
        next_a = [row_of(a_ref, after + i) for i in range(GROUP)]
        next_w = [row_of(w_ref, after + i) for i in range(GROUP)]
        for i in range(GROUP):
            for k in range(GROUP):
                factor = lane_of(a_rows[k], after + i)
                next_a[i] = next_a[i] - factor * a_rows[k]
                next_w[i] = next_w[i] - factor * w_rows[k]
        if p + 2 < panels:
            done = after + GROUP
            u = u_ref[base:after, :]
            v = v_ref[base:after, :]
            uh, um, ul = three_terms(u)
            vh, vm, vl = three_terms(v)
            left = jnp.concatenate([uh, uh, um, uh, ul, um], axis=0).astype(jnp.bfloat16)
            right_a = jnp.concatenate([uh, um, uh, ul, uh, um], axis=0)
            right_w = jnp.concatenate([vh, vm, vh, vl, vh, vm], axis=0)
            right = jnp.concatenate([right_a, right_w], axis=1).astype(jnp.bfloat16)
            update = lax.dot_general(
                left, right, ROWS_BY_ROWS, preferred_element_type=jnp.float32
            )
            a_ref[done:, :] = a_ref[done:, :] - update[done:, :TILE]
            w_ref[done:, :] = w_ref[done:, :] - update[done:, TILE:]
        a_rows, w_rows = next_a, next_w


def factor_step(tiles, b, wide, a_ref, w_ref, u_ref, v_ref):
    row = lax.broadcasted_iota(jnp.int32, (TILE, TILE), 0)
    lane = lax.broadcasted_iota(jnp.int32, (TILE, TILE), 1)
    a_ref[...] = wide[b, b]
    w_ref[...] = jnp.where(row == lane, 1.0, 0.0)
    factor_tile(a_ref, w_ref, u_ref, v_ref)
    inverse = v_ref[...]
    wide[b, b] = jnp.where(row <= lane, u_ref[...], 0.0)
    wide[b, tiles + b] = inverse
    for j in range(1, tiles):
        wide[b, b + j] = lax.dot(
            inverse, wide[b, b + j], precision=HIGHEST, preferred_element_type=jnp.float32
        )
    for r in range(b + 1, tiles):
        for c in list(range(r, tiles)) + list(range(tiles, tiles + b + 1)):
            update = lax.dot_general(
                wide[b, r],
                wide[b, c],
                ROWS_BY_ROWS,
                precision=HIGHEST,
                preferred_element_type=jnp.float32,
            )
            wide[r, c] = -update if c == tiles + b else wide[r, c] - update


def first_kernel(tiles, rows_total, g_ref, wide, *scratch):
    at = 0
    for a in range(tiles):
        for b in range(a, tiles):
            wide[a, b] = g_ref[at] / rows_total
            at += 1
    factor_step(tiles, 0, wide, *scratch)


def next_kernel(tiles, b, _, wide, *scratch):
    factor_step(tiles, b, wide, *scratch)


def last_kernel(tiles, wide, r_ref, inv_ref, hi_ref, mid_ref, lo_ref, *scratch):
    factor_step(tiles, tiles - 1, wide, *scratch)
    zero = jnp.zeros((TILE, TILE), jnp.float32)
    mine = lax.axis_index("snap")
    for a in range(tiles):
        rows = slice(a * TILE, (a + 1) * TILE)
        for b in range(tiles):
            lanes = slice(b * TILE, (b + 1) * TILE)
            r_ref[rows, lanes] = wide[a, b] if b >= a else zero
            value = wide[a, tiles + b] if b <= a else zero
            inv_ref[rows, lanes] = value
            high, middle, low = three_terms(value)
            lanes = pl.ds(pl.multiple_of((mine ^ b) * TILE, TILE), TILE)
            hi_ref[rows, lanes] = high.astype(jnp.bfloat16)
            mid_ref[rows, lanes] = middle.astype(jnp.bfloat16)
            lo_ref[rows, lanes] = low.astype(jnp.bfloat16)


def factor_call(kernel, out_shape, value, after, aliases, tiles):
    many = isinstance(out_shape, tuple)
    return pl.pallas_call(
        lambda *refs: kernel(*refs[len(after) :]),
        out_shape=out_shape,
        in_specs=[ANY] * len(after) + [VMEM],
        out_specs=(VMEM,) * len(out_shape) if many else VMEM,
        scratch_shapes=[pltpu.VMEM((TILE, TILE), jnp.float32)] * 4,
        input_output_aliases={len(after): 0} if aliases else {},
        compiler_params=pltpu.CompilerParams(vmem_limit_bytes=VMEM_BYTES),
        cost_estimate=LIGHT,
        name="factor",
    )(*after, value)


def factor_steps(blocks, tiles, rows_total, after):
    state = jax.ShapeDtypeStruct((tiles, 2 * tiles, TILE, TILE), jnp.float32)
    full = jax.ShapeDtypeStruct((tiles * TILE, tiles * TILE), jnp.float32)
    term = jax.ShapeDtypeStruct(full.shape, jnp.bfloat16)
    value = factor_call(
        lambda *refs: first_kernel(tiles, rows_total, *refs), state, blocks, after, False, tiles
    )
    for b in range(1, tiles - 1):
        after = yield value
        value = factor_call(
            lambda *refs: next_kernel(tiles, b, *refs), state, value, after, True, tiles
        )
    after = yield value
    yield factor_call(
        lambda *refs: last_kernel(tiles, *refs), (full, full, term, term, term), value, after, False, tiles
    )


def basis_kernel(*refs):
    hi_ref, mid_ref, lo_ref, out_ref = refs[-4:]
    cells = whole_rows(by_distance(refs[:-4]))
    total = lax.dot_general(
        cells, lo_ref[...], LANES_BY_LANES, preferred_element_type=jnp.float32
    )
    total += lax.dot_general(
        cells, mid_ref[...], LANES_BY_LANES, preferred_element_type=jnp.float32
    )
    total += lax.dot_general(
        cells, hi_ref[...], LANES_BY_LANES, preferred_element_type=jnp.float32
    )
    out_ref[...] = total.reshape(out_ref.shape)


def basis(cells, terms, call, calls, filled, after, steps=4):
    shares, blocks, rows, width = cells[-1].shape
    full = shares * width
    size = blocks // calls // steps
    first = call * steps
    term = pl.BlockSpec((full, full), lambda i: (0, 0))
    unread = ([] if filled is None else [filled]) + list(after)
    return pl.pallas_call(
        lambda *refs: basis_kernel(*refs[len(unread) :]),
        grid=(steps,),
        out_shape=jax.ShapeDtypeStruct((blocks, rows, full), jnp.float32),
        in_specs=[ANY] * len(unread) + cell_specs(shares, size, rows, width, first) + [term] * 3,
        out_specs=pl.BlockSpec((size, rows, full), lambda i: (first + i, 0, 0)),
        input_output_aliases={} if filled is None else {0: 0},
        compiler_params=pltpu.CompilerParams(vmem_limit_bytes=GRID_VMEM_BYTES),
        cost_estimate=LIGHT,
        name="basis",
    )(*unread, *cells, *terms)


def sum_kernel(count, copies, value_ref, out_ref):
    rows = value_ref.shape[0] // count
    total = value_ref[:rows]
    for i in range(1, count):
        total += value_ref[i * rows : (i + 1) * rows]
    for i in range(copies):
        out_ref[i * rows : (i + 1) * rows] = total


def sum_pieces(value, count, after, copies=1):
    rows, lanes = value.shape
    return pl.pallas_call(
        lambda *refs: sum_kernel(count, copies, *refs[len(after) :]),
        out_shape=jax.ShapeDtypeStruct((rows // count * copies, lanes), value.dtype),
        in_specs=[ANY] * len(after) + [VMEM],
        out_specs=VMEM,
        cost_estimate=LIGHT,
        name="sum_pieces",
    )(*after, value)


def add_kernel(one_ref, two_ref, out_ref):
    out_ref[...] = one_ref[...] + two_ref[...]


def add(one, two, after):
    return pl.pallas_call(
        lambda *refs: add_kernel(*refs[len(after) :]),
        out_shape=jax.ShapeDtypeStruct(one.shape, one.dtype),
        in_specs=[ANY] * len(after) + [VMEM, VMEM],
        out_specs=VMEM,
        cost_estimate=LIGHT,
        name="add",
    )(*after, one, two)


def join_kernel(*refs):
    rows = refs[0].shape[0]
    for i, ref in enumerate(refs[:-1]):
        refs[-1][i * rows : (i + 1) * rows] = ref[...]


def join(values, after):
    rows, lanes = values[0].shape
    return pl.pallas_call(
        lambda *refs: join_kernel(*refs[len(after) :]),
        out_shape=jax.ShapeDtypeStruct((len(values) * rows, lanes), values[0].dtype),
        in_specs=[ANY] * len(after) + [VMEM] * len(values),
        out_specs=VMEM,
        cost_estimate=LIGHT,
        name="join",
    )(*after, *values)


def projection_kernel(slabs, divisor, inverse_ref, same_ref, other_ref, out_ref, cross_ref):
    me = lax.axis_index("space")
    rows = cross_ref.shape[0] // slabs
    for away in range(slabs):
        at = pl.ds(pl.multiple_of((me ^ away) * rows, rows), rows)
        chip = slice(away // CORES * rows, (away // CORES + 1) * rows)
        cross_ref[at, :] = (other_ref if away % CORES else same_ref)[chip]
    out_ref[...] = (
        lax.dot(
            inverse_ref[...],
            cross_ref[...],
            precision=HIGHEST,
            preferred_element_type=jnp.float32,
        )
        / divisor
    )


def project(inverse, same, other, slabs, divisor):
    return pl.pallas_call(
        lambda *refs: projection_kernel(slabs, divisor, *refs),
        out_shape=jax.ShapeDtypeStruct(inverse.shape, jnp.float32),
        in_specs=[VMEM] * 3,
        out_specs=VMEM,
        scratch_shapes=[pltpu.VMEM(inverse.shape, jnp.float32)],
        compiler_params=pltpu.CompilerParams(vmem_limit_bytes=VMEM_BYTES),
        name="project",
    )(inverse, same, other)


def swap(value, axis, mask):
    return lax.ppermute(value, axis, [(i, i ^ mask) for i in range(lax.axis_size(axis))])


def body(owned_x, owned_y, patch_dest):
    slabs = lax.axis_size("space")
    shares = lax.axis_size("snap")
    slots, patch, width = owned_x.shape
    per_slab = slots // 2
    rows_total = slabs * per_slab * patch
    full = shares * width
    tiles = full // TILE
    pairs = tiles * (tiles + 1) // 2
    shares_of = (tuple(range(1, shares)), (0,))
    away = len(shares_of[0])

    def packed(owned, groups, with_ids, after):
        cells = owned.reshape(slots, shares, patch // shares, width)
        return pack(patch_dest, cells, slabs, per_slab, groups, with_ids, after)

    def merged(sent, after):
        return merge(sent[0], swap(sent[1], "space", 1), slabs // CORES, after)

    def to_chips(joined):
        return [joined[0]] + [swap(joined[m], "space", CORES * m) for m in range(1, len(joined))]

    def to_pieces(value, axis="space"):
        return lax.all_to_all(value, axis, split_axis=0, concat_axis=0, tiled=True)

    def place_far(meta, moved, after):
        pieces, meta = settle(
            meta, moved, slots // slabs, per_slab, shares, shares_of[0], 0, 1, after
        )
        return pieces, to_pieces(pieces[0], "snap"), meta

    def place(meta, moved, group, cuts, after):
        count = len(shares_of[group])
        pieces, _ = settle(meta, moved, slots // slabs, per_slab, shares, (), count, cuts, after)
        return pieces, [
            swap(piece, "snap", shares_of[group][k // cuts]) if shares_of[group][k // cuts] else piece
            for k, piece in enumerate(pieces)
        ]

    def hops():
        hop = 1
        while hop < shares:
            yield hop
            hop *= 2

    chips = slabs // CORES
    sent_x = packed(owned_x, shares_of, True, [])
    ((same_y, other_y),) = packed(owned_y, (shares_of[0] + shares_of[1],), False, [])
    other_y = swap(other_y, "space", 1)
    far = to_chips(merged(sent_x[0], []))
    near = to_chips(merged(sent_x[1], far[1:3]))
    settled, x_far, meta = place_far(None, far, [other_y])
    after = settled + near[1:2]
    y_far = to_chips(merge(same_y, other_y, chips, after, slice(0, away), shares))
    y_near = to_chips(merge(same_y, other_y, chips, y_far[1:3], slice(away, shares), shares))
    _, x_near = place(meta, near, 1, 1, [])
    x_cells = x_near + [x_far]

    settled, y_far = place(meta, y_far, 0, 2, x_near)
    gram_local = gram_blocks(x_cells, settled[:1])
    gram = to_pieces(gram_local.reshape(pairs * TILE, TILE))
    gram = sum_pieces(gram, slabs, [y_far[2], y_far[4]] + y_near[1:], shares)
    gram = sum_pieces(to_pieces(gram, "snap"), shares, [])
    settled, y_near = place(meta, y_near, 1, 1, [gram])
    y_cells = y_near + y_far
    gram = lax.all_gather(gram, "space", axis=0, tiled=True)

    steps = factor_steps(gram.reshape(pairs, TILE, TILE), tiles, rows_total, [])
    state = next(steps)
    for _ in range(tiles - 3):
        state = steps.send([])
    cross_local = cross_sum(x_cells, y_cells, [state])
    state = steps.send([cross_local])
    cross = sum_pieces(to_pieces(cross_local), slabs, [state])
    r_factor, inverse, *terms = steps.send([cross])
    tied = [r_factor]
    for hop in hops():
        cross = add(cross, swap(cross, "snap", hop), tied)
        if hop == 1:
            q_basis = basis(x_cells, terms, 0, 2, None, [cross])
            tied = [q_basis]
    q_basis = basis(x_cells, terms, 1, 2, q_basis, [cross])
    same = join([cross] + [swap(cross, "space", m) for m in range(CORES, slabs, CORES)], [q_basis])
    projection = project(inverse, same, swap(same, "space", 1), slabs, math.sqrt(rows_total))
    return q_basis, r_factor, projection


def solution(mesh):
    in_specs = (P("space", None, "snap"), P("space", None, "snap"), P("space"))
    out_specs = (P("space", "snap", None), P(), P())
    return jax.shard_map(body, mesh=mesh, in_specs=in_specs, out_specs=out_specs, check_vma=False)
```

```python
import math

import jax
import jax.numpy as jnp
from jax import lax
from jax.experimental import pallas as pl
from jax.experimental.pallas import tpu as pltpu
from jax.sharding import PartitionSpec as P

TILE = 128
GROUP = 8
CORES = 2
VMEM_BYTES = 32 * 1024 * 1024
GRID_VMEM_BYTES = 56 * 1024 * 1024
HIGHEST = lax.Precision.HIGHEST
SMEM = pl.BlockSpec(memory_space=pltpu.SMEM)
VMEM = pl.BlockSpec(memory_space=pltpu.VMEM)
ANY = pl.BlockSpec(memory_space=pl.ANY)
LIGHT = pl.CostEstimate(flops=1, bytes_accessed=1, transcendentals=0)
ROWS_BY_ROWS = (((0,), (0,)), ((), ()))
LANES_BY_LANES = (((1,), (1,)), ((), ()))


def pack_kernel(slabs, capacity, per_slab, shares_of, dest_ref, owned_ref, *refs):
    out_refs, (ids_ref, count_ref) = refs[:-2], refs[-2:]
    chips = slabs // CORES
    me = lax.axis_index("space")
    mine = lax.axis_index("snap")
    lane = lax.broadcasted_iota(jnp.int32, (1, TILE), 1)
    ids_ref[...] = jnp.full_like(ids_ref, -1)
    for slab in range(slabs):
        count_ref[slab] = 0

    def place(i, _):
        block = dest_ref[i]

        @pl.when(block >= 0)
        def _():
            slab = lax.div(block, per_slab)
            rank = count_ref[slab]
            count_ref[slab] = rank + 1
            here = pl.ds(slab, 1)
            ids_ref[here, :] = jnp.where(lane == rank, block - slab * per_slab, ids_ref[here, :])
            away = slab ^ me
            chip = lax.shift_right_logical(away, 1)
            for core in range(CORES):

                @pl.when((away & 1) == core)
                def _():
                    for group, shares in enumerate(shares_of):
                        out_ref = out_refs[group * CORES + core]
                        at = chip * (out_ref.shape[0] // chips) + rank * len(shares)
                        for k, share in enumerate(shares):
                            out_ref[at + k] = owned_ref[i, mine ^ share]

        return 0

    lax.fori_loop(0, dest_ref.shape[0], place, 0, unroll=2)
    for group, shares in enumerate(shares_of):
        used = capacity * len(shares)
        for away in range(slabs):
            out_ref = out_refs[group * CORES + away % CORES]
            span = out_ref.shape[0] // chips
            if span > used:
                ids = ids_ref[pl.ds(me ^ away, 1), :].astype(jnp.float32)
                tile = jnp.broadcast_to(ids, out_ref.shape[1:]).astype(out_ref.dtype)
                out_ref[away // CORES * span + used] = tile


def pack(dest, owned, slabs, per_slab, shares_of, with_ids, after):
    slots, _, rows, width = owned.shape
    chips = slabs // CORES
    capacity = slots // slabs
    sent = []
    for group, shares in enumerate(shares_of):
        span = capacity * len(shares) + (1 if with_ids and group == 0 else 0)
        sent += [jax.ShapeDtypeStruct((chips * span, rows, width), owned.dtype)] * CORES
    outs = pl.pallas_call(
        lambda *refs: pack_kernel(slabs, capacity, per_slab, shares_of, *refs[len(after) :]),
        out_shape=tuple(sent),
        in_specs=[ANY] * len(after) + [SMEM, VMEM],
        out_specs=(VMEM,) * len(sent),
        scratch_shapes=[
            pltpu.VMEM((slabs, TILE), jnp.int32),
            pltpu.SMEM((slabs,), jnp.int32),
        ],
        compiler_params=pltpu.CompilerParams(vmem_limit_bytes=VMEM_BYTES),
        cost_estimate=LIGHT,
        name="pack",
    )(*after, dest, owned)
    return [outs[at : at + CORES] for at in range(0, len(outs), CORES)]


def merge_kernel(same_ref, other_ref, *out_refs):
    span = same_ref.shape[0] // len(out_refs)
    for chip, out_ref in enumerate(out_refs):
        out_ref[:span] = same_ref[chip * span : (chip + 1) * span]
        out_ref[span:] = other_ref[chip * span : (chip + 1) * span]


def merge(same, other, chips, after):
    tiles, rows, width = same.shape
    out = jax.ShapeDtypeStruct((CORES * tiles // chips, rows, width), same.dtype)
    return pl.pallas_call(
        lambda *refs: merge_kernel(*refs[len(after) :]),
        out_shape=(out,) * chips,
        in_specs=[ANY] * len(after) + [VMEM, VMEM],
        out_specs=(VMEM,) * chips,
        compiler_params=pltpu.CompilerParams(vmem_limit_bytes=VMEM_BYTES),
        cost_estimate=LIGHT,
        name="merge",
    )(*after, same, other)


def settle_kernel(chips, capacity, with_ids, far, cuts, *refs):
    if with_ids:
        moved_refs, out_refs, meta_ref, ids_ref = refs[:chips], refs[chips:-2], refs[-2], refs[-1]
        span = moved_refs[0].shape[0] // CORES
        for source in range(chips * CORES):
            at = source % CORES * span + span - 1
            tile = moved_refs[source // CORES][at].astype(jnp.float32)
            ids_ref[source : source + 1, :] = tile[:1].astype(jnp.int32)
        pltpu.sync_copy(ids_ref, meta_ref)
    else:
        meta_ref, moved_refs, out_refs = refs[0], refs[1 : 1 + chips], refs[1 + chips :]
        span = moved_refs[0].shape[0] // CORES
    mine = lax.axis_index("snap")
    count = len(far) or len(out_refs) // cuts
    for source in range(chips * CORES):
        moved_ref = moved_refs[source // CORES]

        def place(rank, _):
            block = meta_ref[source, rank]

            @pl.when(block >= 0)
            def _():
                at = source % CORES * span + rank * count
                if far:
                    for k in range(count):
                        out_refs[0][mine ^ far[k], block] = moved_ref[at + k]
                else:
                    for k, out_ref in enumerate(out_refs):
                        rows = out_ref.shape[1]
                        cells = slice(k % cuts * rows, (k % cuts + 1) * rows)
                        out_ref[block] = moved_ref[at + k // cuts, cells]

            return 0

        lax.fori_loop(0, capacity, place, 0, unroll=4)


def settle(meta, moved, capacity, per_slab, shares, far, count, cuts, after):
    with_ids = meta is None
    chips = len(moved)
    rows, width = moved[0].shape[1:]
    if far:
        pieces = (jax.ShapeDtypeStruct((shares, per_slab, rows, width), moved[0].dtype),)
    else:
        piece = jax.ShapeDtypeStruct((per_slab, rows // cuts, width), moved[0].dtype)
        pieces = (piece,) * (count * cuts)
    ids = jax.ShapeDtypeStruct((chips * CORES, TILE), jnp.int32)
    outs = pl.pallas_call(
        lambda *refs: settle_kernel(chips, capacity, with_ids, far, cuts, *refs[len(after) :]),
        out_shape=pieces + ((ids,) if with_ids else ()),
        in_specs=[ANY] * len(after) + ([] if with_ids else [SMEM]) + [VMEM] * chips,
        out_specs=(VMEM,) * len(pieces) + ((SMEM,) if with_ids else ()),
        scratch_shapes=[pltpu.VMEM((chips * CORES, TILE), jnp.int32)] if with_ids else [],
        compiler_params=pltpu.CompilerParams(vmem_limit_bytes=VMEM_BYTES),
        cost_estimate=LIGHT,
        name="settle",
    )(*after, *([] if with_ids else [meta]), *moved)
    return list(outs[: len(pieces)]), (outs[-1] if with_ids else meta)


def by_distance(refs):
    near = len(refs) - 1
    mine = lax.axis_index("snap")
    return list(refs[:near]) + [refs[near].at[mine ^ share] for share in range(near, refs[near].shape[0])]


def cell_specs(shares, size, rows, width, first):
    near = pl.BlockSpec((size, rows, width), lambda i: (first + i, 0, 0))
    far = pl.BlockSpec((shares, size, rows, width), lambda i: (0, first + i, 0, 0))
    return [near, far]


def whole_rows(refs):
    blocks, rows, width = refs[0].shape
    return jnp.concatenate([ref[...].reshape(blocks * rows, width) for ref in refs], axis=1)


def tile_of(row, lane, tiles):
    return row * tiles - lax.div(row * (row - 1), 2) + lane - row


def gram_kernel(shares, *refs):
    out_ref, acc_ref = refs[-2:]
    step = pl.program_id(0)

    @pl.when(step == 0)
    def _():
        acc_ref[...] = jnp.zeros_like(acc_ref)

    cells = whole_rows(by_distance(refs[:-2]))
    acc_ref[...] += lax.dot_general(
        cells, cells, ROWS_BY_ROWS, preferred_element_type=jnp.float32
    )

    @pl.when(step == pl.num_programs(0) - 1)
    def _():
        mine = lax.axis_index("snap")
        for a in range(shares):
            for b in range(shares):
                row, lane = mine ^ a, mine ^ b

                @pl.when(row <= lane)
                def _():
                    out_ref[tile_of(row, lane, shares)] = acc_ref[
                        a * TILE : (a + 1) * TILE, b * TILE : (b + 1) * TILE
                    ]


def gram_blocks(cells, after, steps=4):
    shares, blocks, rows, width = cells[-1].shape
    pairs = shares * (shares + 1) // 2
    full = shares * width
    return pl.pallas_call(
        lambda *refs: gram_kernel(shares, *refs[len(after) :]),
        grid=(steps,),
        out_shape=jax.ShapeDtypeStruct((pairs, TILE, TILE), jnp.float32),
        in_specs=[ANY] * len(after) + cell_specs(shares, blocks // steps, rows, width, 0),
        out_specs=pl.BlockSpec((pairs, TILE, TILE), lambda i: (0, 0, 0)),
        scratch_shapes=[pltpu.VMEM((full, full), jnp.float32)],
        compiler_params=pltpu.CompilerParams(vmem_limit_bytes=GRID_VMEM_BYTES),
        cost_estimate=LIGHT,
        name="gram_blocks",
    )(*after, *cells)


def cross_kernel(shares, *refs):
    out_ref, acc_ref = refs[-2:]
    step = pl.program_id(0)

    @pl.when(step == 0)
    def _():
        acc_ref[...] = jnp.zeros_like(acc_ref)

    y_ref = refs[2]
    acc_ref[...] += lax.dot_general(
        whole_rows(by_distance(refs[:2])),
        whole_rows([y_ref.at[share] for share in range(shares)]),
        ROWS_BY_ROWS,
        preferred_element_type=jnp.float32,
    )

    @pl.when(step == pl.num_programs(0) - 1)
    def _():
        mine = lax.axis_index("snap")
        for a in range(shares):
            rows = pl.ds(pl.multiple_of((mine ^ a) * TILE, TILE), TILE)
            out_ref[rows, :] = acc_ref[a * TILE : (a + 1) * TILE, :]


def cross_sum(x_cells, y_cells, after, steps=4):
    shares, blocks, rows, width = x_cells[-1].shape
    full = shares * width
    specs = cell_specs(shares, blocks // steps, rows, width, 0)
    return pl.pallas_call(
        lambda *refs: cross_kernel(shares, *refs[len(after) :]),
        grid=(steps,),
        out_shape=jax.ShapeDtypeStruct((full, full), jnp.float32),
        in_specs=[ANY] * len(after) + specs + specs[-1:],
        out_specs=pl.BlockSpec((full, full), lambda i: (0, 0)),
        scratch_shapes=[pltpu.VMEM((full, full), jnp.float32)],
        compiler_params=pltpu.CompilerParams(vmem_limit_bytes=GRID_VMEM_BYTES),
        cost_estimate=LIGHT,
        name="cross_sum",
    )(*after, *x_cells, y_cells)


def three_terms(value):
    high = value.astype(jnp.bfloat16).astype(jnp.float32)
    rest = value - high
    middle = rest.astype(jnp.bfloat16).astype(jnp.float32)
    return high, middle, rest - middle


def lane_of(row, lane):
    return jnp.broadcast_to(row[:, lane : lane + 1], row.shape)


def row_of(ref, row):
    return jnp.broadcast_to(ref[row : row + 1, :], (GROUP, TILE))


def factor_tile(a_ref, w_ref, u_ref, v_ref):
    panels = TILE // GROUP
    a_rows = [row_of(a_ref, i) for i in range(GROUP)]
    w_rows = [row_of(w_ref, i) for i in range(GROUP)]
    for p in range(panels):
        base = p * GROUP
        small = {
            (i, k): lane_of(a_rows[i], base + k) for i in range(GROUP) for k in range(i, GROUP)
        }
        for j in range(GROUP):
            scale = lax.rsqrt(small[j, j])
            a_rows[j] = a_rows[j] * scale
            w_rows[j] = w_rows[j] * scale
            u_ref[base + j : base + j + 1, :] = a_rows[j][:1]
            v_ref[base + j : base + j + 1, :] = w_rows[j][:1]
            below = {k: small[j, k] * scale for k in range(j + 1, GROUP)}
            for k in range(j + 1, GROUP):
                for m in range(k, GROUP):
                    small[k, m] = small[k, m] - below[k] * below[m]
            for k in range(j + 1, GROUP):
                a_rows[k] = a_rows[k] - below[k] * a_rows[j]
                w_rows[k] = w_rows[k] - below[k] * w_rows[j]
        if p + 1 == panels:
            break
        after = base + GROUP
        next_a = [row_of(a_ref, after + i) for i in range(GROUP)]
        next_w = [row_of(w_ref, after + i) for i in range(GROUP)]
        for i in range(GROUP):
            for k in range(GROUP):
                factor = lane_of(a_rows[k], after + i)
                next_a[i] = next_a[i] - factor * a_rows[k]
                next_w[i] = next_w[i] - factor * w_rows[k]
        if p + 2 < panels:
            done = after + GROUP
            u = u_ref[base:after, :]
            v = v_ref[base:after, :]
            uh, um, ul = three_terms(u)
            vh, vm, vl = three_terms(v)
            left = jnp.concatenate([uh, uh, um, uh, ul, um], axis=0).astype(jnp.bfloat16)
            right_a = jnp.concatenate([uh, um, uh, ul, uh, um], axis=0)
            right_w = jnp.concatenate([vh, vm, vh, vl, vh, vm], axis=0)
            right = jnp.concatenate([right_a, right_w], axis=1).astype(jnp.bfloat16)
            update = lax.dot_general(
                left, right, ROWS_BY_ROWS, preferred_element_type=jnp.float32
            )
            a_ref[done:, :] = a_ref[done:, :] - update[done:, :TILE]
            w_ref[done:, :] = w_ref[done:, :] - update[done:, TILE:]
        a_rows, w_rows = next_a, next_w


def factor_step(tiles, b, wide, a_ref, w_ref, u_ref, v_ref):
    row = lax.broadcasted_iota(jnp.int32, (TILE, TILE), 0)
    lane = lax.broadcasted_iota(jnp.int32, (TILE, TILE), 1)
    a_ref[...] = wide[b, b]
    w_ref[...] = jnp.where(row == lane, 1.0, 0.0)
    factor_tile(a_ref, w_ref, u_ref, v_ref)
    inverse = v_ref[...]
    wide[b, b] = jnp.where(row <= lane, u_ref[...], 0.0)
    wide[b, tiles + b] = inverse
    for j in range(1, tiles):
        wide[b, b + j] = lax.dot(
            inverse, wide[b, b + j], precision=HIGHEST, preferred_element_type=jnp.float32
        )
    for r in range(b + 1, tiles):
        for c in list(range(r, tiles)) + list(range(tiles, tiles + b + 1)):
            update = lax.dot_general(
                wide[b, r],
                wide[b, c],
                ROWS_BY_ROWS,
                precision=HIGHEST,
                preferred_element_type=jnp.float32,
            )
            wide[r, c] = -update if c == tiles + b else wide[r, c] - update


def first_kernel(tiles, rows_total, g_ref, wide, *scratch):
    at = 0
    for a in range(tiles):
        for b in range(a, tiles):
            wide[a, b] = g_ref[at] / rows_total
            at += 1
    factor_step(tiles, 0, wide, *scratch)


def next_kernel(tiles, b, _, wide, *scratch):
    factor_step(tiles, b, wide, *scratch)


def last_kernel(tiles, wide, r_ref, inv_ref, hi_ref, mid_ref, lo_ref, *scratch):
    factor_step(tiles, tiles - 1, wide, *scratch)
    zero = jnp.zeros((TILE, TILE), jnp.float32)
    mine = lax.axis_index("snap")
    for a in range(tiles):
        rows = slice(a * TILE, (a + 1) * TILE)
        for b in range(tiles):
            lanes = slice(b * TILE, (b + 1) * TILE)
            r_ref[rows, lanes] = wide[a, b] if b >= a else zero
            value = wide[a, tiles + b] if b <= a else zero
            inv_ref[rows, lanes] = value
            high, middle, low = three_terms(value)
            lanes = pl.ds(pl.multiple_of((mine ^ b) * TILE, TILE), TILE)
            hi_ref[rows, lanes] = high.astype(jnp.bfloat16)
            mid_ref[rows, lanes] = middle.astype(jnp.bfloat16)
            lo_ref[rows, lanes] = low.astype(jnp.bfloat16)


def factor_call(kernel, out_shape, value, after, aliases, tiles):
    many = isinstance(out_shape, tuple)
    return pl.pallas_call(
        lambda *refs: kernel(*refs[len(after) :]),
        out_shape=out_shape,
        in_specs=[ANY] * len(after) + [VMEM],
        out_specs=(VMEM,) * len(out_shape) if many else VMEM,
        scratch_shapes=[pltpu.VMEM((TILE, TILE), jnp.float32)] * 4,
        input_output_aliases={len(after): 0} if aliases else {},
        compiler_params=pltpu.CompilerParams(vmem_limit_bytes=VMEM_BYTES),
        cost_estimate=LIGHT,
        name="factor",
    )(*after, value)


def factor_steps(blocks, tiles, rows_total, after):
    state = jax.ShapeDtypeStruct((tiles, 2 * tiles, TILE, TILE), jnp.float32)
    full = jax.ShapeDtypeStruct((tiles * TILE, tiles * TILE), jnp.float32)
    term = jax.ShapeDtypeStruct(full.shape, jnp.bfloat16)
    value = factor_call(
        lambda *refs: first_kernel(tiles, rows_total, *refs), state, blocks, after, False, tiles
    )
    for b in range(1, tiles - 1):
        after = yield value
        value = factor_call(
            lambda *refs: next_kernel(tiles, b, *refs), state, value, after, True, tiles
        )
    after = yield value
    yield factor_call(
        lambda *refs: last_kernel(tiles, *refs), (full, full, term, term, term), value, after, False, tiles
    )


def basis_kernel(*refs):
    hi_ref, mid_ref, lo_ref, out_ref = refs[-4:]
    cells = whole_rows(by_distance(refs[:-4]))
    total = lax.dot_general(
        cells, lo_ref[...], LANES_BY_LANES, preferred_element_type=jnp.float32
    )
    total += lax.dot_general(
        cells, mid_ref[...], LANES_BY_LANES, preferred_element_type=jnp.float32
    )
    total += lax.dot_general(
        cells, hi_ref[...], LANES_BY_LANES, preferred_element_type=jnp.float32
    )
    out_ref[...] = total.reshape(out_ref.shape)


def basis(cells, terms, call, calls, filled, after, steps=4):
    shares, blocks, rows, width = cells[-1].shape
    full = shares * width
    size = blocks // calls // steps
    first = call * steps
    term = pl.BlockSpec((full, full), lambda i: (0, 0))
    unread = ([] if filled is None else [filled]) + list(after)
    return pl.pallas_call(
        lambda *refs: basis_kernel(*refs[len(unread) :]),
        grid=(steps,),
        out_shape=jax.ShapeDtypeStruct((blocks, rows, full), jnp.float32),
        in_specs=[ANY] * len(unread) + cell_specs(shares, size, rows, width, first) + [term] * 3,
        out_specs=pl.BlockSpec((size, rows, full), lambda i: (first + i, 0, 0)),
        input_output_aliases={} if filled is None else {0: 0},
        compiler_params=pltpu.CompilerParams(vmem_limit_bytes=GRID_VMEM_BYTES),
        cost_estimate=LIGHT,
        name="basis",
    )(*unread, *cells, *terms)


def sum_kernel(count, copies, value_ref, out_ref):
    rows = value_ref.shape[0] // count
    total = value_ref[:rows]
    for i in range(1, count):
        total += value_ref[i * rows : (i + 1) * rows]
    for i in range(copies):
        out_ref[i * rows : (i + 1) * rows] = total


def sum_pieces(value, count, after, copies=1):
    rows, lanes = value.shape
    return pl.pallas_call(
        lambda *refs: sum_kernel(count, copies, *refs[len(after) :]),
        out_shape=jax.ShapeDtypeStruct((rows // count * copies, lanes), value.dtype),
        in_specs=[ANY] * len(after) + [VMEM],
        out_specs=VMEM,
        cost_estimate=LIGHT,
        name="sum_pieces",
    )(*after, value)


def add_kernel(one_ref, two_ref, out_ref):
    out_ref[...] = one_ref[...] + two_ref[...]


def add(one, two, after):
    return pl.pallas_call(
        lambda *refs: add_kernel(*refs[len(after) :]),
        out_shape=jax.ShapeDtypeStruct(one.shape, one.dtype),
        in_specs=[ANY] * len(after) + [VMEM, VMEM],
        out_specs=VMEM,
        cost_estimate=LIGHT,
        name="add",
    )(*after, one, two)


def join_kernel(*refs):
    rows = refs[0].shape[0]
    for i, ref in enumerate(refs[:-1]):
        refs[-1][i * rows : (i + 1) * rows] = ref[...]


def join(values, after):
    rows, lanes = values[0].shape
    return pl.pallas_call(
        lambda *refs: join_kernel(*refs[len(after) :]),
        out_shape=jax.ShapeDtypeStruct((len(values) * rows, lanes), values[0].dtype),
        in_specs=[ANY] * len(after) + [VMEM] * len(values),
        out_specs=VMEM,
        cost_estimate=LIGHT,
        name="join",
    )(*after, *values)


def projection_kernel(slabs, divisor, inverse_ref, same_ref, other_ref, out_ref, cross_ref):
    me = lax.axis_index("space")
    rows = cross_ref.shape[0] // slabs
    for away in range(slabs):
        at = pl.ds(pl.multiple_of((me ^ away) * rows, rows), rows)
        chip = slice(away // CORES * rows, (away // CORES + 1) * rows)
        cross_ref[at, :] = (other_ref if away % CORES else same_ref)[chip]
    out_ref[...] = (
        lax.dot(
            inverse_ref[...],
            cross_ref[...],
            precision=HIGHEST,
            preferred_element_type=jnp.float32,
        )
        / divisor
    )


def project(inverse, same, other, slabs, divisor):
    return pl.pallas_call(
        lambda *refs: projection_kernel(slabs, divisor, *refs),
        out_shape=jax.ShapeDtypeStruct(inverse.shape, jnp.float32),
        in_specs=[VMEM] * 3,
        out_specs=VMEM,
        scratch_shapes=[pltpu.VMEM(inverse.shape, jnp.float32)],
        compiler_params=pltpu.CompilerParams(vmem_limit_bytes=VMEM_BYTES),
        name="project",
    )(inverse, same, other)


def swap(value, axis, mask):
    return lax.ppermute(value, axis, [(i, i ^ mask) for i in range(lax.axis_size(axis))])


def body(owned_x, owned_y, patch_dest):
    slabs = lax.axis_size("space")
    shares = lax.axis_size("snap")
    slots, patch, width = owned_x.shape
    per_slab = slots // 2
    rows_total = slabs * per_slab * patch
    full = shares * width
    tiles = full // TILE
    pairs = tiles * (tiles + 1) // 2
    shares_of = (tuple(range(1, shares)), (0,))

    def packed(owned, groups, with_ids, after):
        cells = owned.reshape(slots, shares, patch // shares, width)
        return pack(patch_dest, cells, slabs, per_slab, groups, with_ids, after)

    def merged(sent, after):
        return merge(sent[0], swap(sent[1], "space", 1), slabs // CORES, after)

    def to_chips(joined):
        return [joined[0]] + [swap(joined[m], "space", CORES * m) for m in range(1, len(joined))]

    def to_pieces(value, axis="space"):
        return lax.all_to_all(value, axis, split_axis=0, concat_axis=0, tiled=True)

    def place_far(meta, moved, group, after):
        pieces, meta = settle(
            meta, moved, slots // slabs, per_slab, shares, group, 0, 1, after
        )
        return pieces, to_pieces(pieces[0], "snap"), meta

    def place_own(meta, moved):
        (piece,), _ = settle(meta, moved, slots // slabs, per_slab, shares, (), 1, 1, [])
        return piece

    def hops():
        hop = 1
        while hop < shares:
            yield hop
            hop *= 2

    sent_x = packed(owned_x, shares_of, True, [])
    (sent_y,) = packed(owned_y, (tuple(range(shares)),), False, [])
    far = to_chips(merged(sent_x[0], []))
    near = to_chips(merged(sent_x[1], far[1:3]))
    settled, x_far, meta = place_far(None, far, shares_of[0], [])
    moved_y = to_chips(merged(sent_y, settled + near[1:]))
    x_cells = [place_own(meta, near), x_far]

    gram_local = gram_blocks(x_cells, moved_y[1:2])
    gram = to_pieces(gram_local.reshape(pairs * TILE, TILE))
    gram = to_pieces(sum_pieces(gram, slabs, [], shares), "snap")
    settled, y_cells, _ = place_far(meta, moved_y, tuple(range(shares)), [gram])
    gram = sum_pieces(gram, shares, settled)
    gram = lax.all_gather(gram, "space", axis=0, tiled=True)

    steps = factor_steps(gram.reshape(pairs, TILE, TILE), tiles, rows_total, [])
    state = next(steps)
    for _ in range(1, tiles):
        state = steps.send([])
    r_factor, inverse, *terms = state
    q_basis = basis(x_cells, terms, 0, 1, None, [], 8)

    cross_local = cross_sum(x_cells, y_cells, [q_basis])
    cross = sum_pieces(to_pieces(cross_local), slabs, [])
    for hop in hops():
        cross = add(cross, swap(cross, "snap", hop), [])
    same = join([cross] + [swap(cross, "space", m) for m in range(CORES, slabs, CORES)], [])
    projection = project(inverse, same, swap(same, "space", 1), slabs, math.sqrt(rows_total))
    return q_basis, r_factor, projection


def solution(mesh):
    in_specs = (P("space", None, "snap"), P("space", None, "snap"), P("space"))
    out_specs = (P("space", "snap", None), P(), P())
    return jax.shard_map(body, mesh=mesh, in_specs=in_specs, out_specs=out_specs, check_vma=False)
```

```python
import math

import jax
import jax.numpy as jnp
from jax import lax
from jax.experimental import pallas as pl
from jax.experimental.pallas import tpu as pltpu
from jax.sharding import PartitionSpec as P

TILE = 128
GROUP = 8
CORES = 2
CELL_TILE = 16
VMEM_BYTES = 32 * 1024 * 1024
HIGHEST = lax.Precision.HIGHEST
SMEM = pl.BlockSpec(memory_space=pltpu.SMEM)
VMEM = pl.BlockSpec(memory_space=pltpu.VMEM)
ANY = pl.BlockSpec(memory_space=pl.ANY)
ROWS_BY_ROWS = (((0,), (0,)), ((), ()))
LANES_BY_LANES = (((1,), (1,)), ((), ()))


def cost(flops, bytes_accessed, transcendentals):
    return pl.CostEstimate(
        flops=flops,
        bytes_accessed=bytes_accessed,
        transcendentals=transcendentals,
    )


def pack_kernel(slabs, capacity, per_slab, dest_ref, owned_ref, *refs):
    out_refs, (ids_ref, count_ref) = refs[:CORES], refs[CORES:]
    chips = slabs // CORES
    tiles = owned_ref.shape[1]
    used = capacity * tiles
    span = out_refs[0].shape[0] // chips
    me = lax.axis_index("space")
    lane = lax.broadcasted_iota(jnp.int32, (1, TILE), 1)
    ids_ref[...] = jnp.full_like(ids_ref, -1)
    for slab in range(slabs):
        count_ref[slab] = 0

    def place(i, _):
        block = dest_ref[i]

        @pl.when(block >= 0)
        def _():
            slab = lax.div(block, per_slab)
            rank = count_ref[slab]
            count_ref[slab] = rank + 1
            here = pl.ds(slab, 1)
            ids_ref[here, :] = jnp.where(lane == rank, block - slab * per_slab, ids_ref[here, :])
            away = slab ^ me
            at = pl.ds(lax.shift_right_logical(away, 1) * span + rank * tiles, tiles)
            for core in range(CORES):

                @pl.when((away & 1) == core)
                def _():
                    out_refs[core][at] = owned_ref[i]

        return 0

    lax.fori_loop(0, dest_ref.shape[0], place, 0, unroll=2)
    if span > used:
        for away in range(slabs):
            out_ref = out_refs[away % CORES]
            ids = ids_ref[pl.ds(me ^ away, 1), :].astype(jnp.float32)
            tile = jnp.broadcast_to(ids, out_ref.shape[1:]).astype(out_ref.dtype)
            out_ref[away // CORES * span + used] = tile


def pack(dest, owned, slabs, per_slab, with_ids):
    slots, tiles, rows, width = owned.shape
    chips = slabs // CORES
    capacity = slots // slabs
    span = capacity * tiles + (1 if with_ids else 0)
    sent = jax.ShapeDtypeStruct((chips * span, rows, width), owned.dtype)
    return pl.pallas_call(
        lambda *refs: pack_kernel(slabs, capacity, per_slab, *refs),
        out_shape=(sent,) * CORES,
        in_specs=[SMEM, VMEM],
        out_specs=(VMEM,) * CORES,
        scratch_shapes=[
            pltpu.VMEM((slabs, TILE), jnp.int32),
            pltpu.SMEM((slabs,), jnp.int32),
        ],
        compiler_params=pltpu.CompilerParams(vmem_limit_bytes=VMEM_BYTES),
        cost_estimate=cost(flops=0, bytes_accessed=2 * owned.size * 2, transcendentals=0),
        name="pack",
    )(dest, owned)


def merge_kernel(same_ref, other_ref, *out_refs):
    span = same_ref.shape[0] // len(out_refs)
    for chip, out_ref in enumerate(out_refs):
        out_ref[:span] = same_ref[chip * span : (chip + 1) * span]
        out_ref[span:] = other_ref[chip * span : (chip + 1) * span]


def merge(same, other, chips, after):
    tiles, rows, width = same.shape
    out = jax.ShapeDtypeStruct((CORES * tiles // chips, rows, width), same.dtype)
    return pl.pallas_call(
        lambda *refs: merge_kernel(*refs[len(after) :]),
        out_shape=(out,) * chips,
        in_specs=[ANY] * len(after) + [VMEM, VMEM],
        out_specs=(VMEM,) * chips,
        compiler_params=pltpu.CompilerParams(vmem_limit_bytes=VMEM_BYTES),
        cost_estimate=cost(flops=0, bytes_accessed=8 * same.size, transcendentals=0),
        name="merge",
    )(*after, same, other)


def settle_kernel(chips, capacity, parts, first, *refs):
    if first:
        moved_refs, (out_ref, meta_ref, ids_ref) = refs[:chips], refs[chips:]
        span = moved_refs[0].shape[0] // CORES
        for source in range(chips * CORES):
            at = source % CORES * span + span - 1
            tile = moved_refs[source // CORES][at].astype(jnp.float32)
            ids_ref[source : source + 1, :] = tile[:1].astype(jnp.int32)
        pltpu.sync_copy(ids_ref, meta_ref)
        shares = out_ref.shape[0]
    else:
        meta_ref, moved_refs, out_refs = refs[0], refs[1 : 1 + chips], refs[1 + chips :]
        span = moved_refs[0].shape[0] // CORES
        shares = len(out_refs) // parts
    tiles = shares * parts
    rows = moved_refs[0].shape[1]
    mine = lax.axis_index("snap")
    for source in range(chips * CORES):
        moved_ref = moved_refs[source // CORES]

        def place(rank, _):
            block = meta_ref[source, rank]

            @pl.when(block >= 0)
            def _():
                at = source % CORES * span + rank * tiles
                for share in range(shares):
                    if first:
                        for k in range(parts):
                            cells = slice(k * rows, (k + 1) * rows)
                            out_ref[share, block, cells] = moved_ref[at + share * parts + k]
                    else:
                        for k in range(parts):
                            cells = moved_ref[at + (mine ^ share) * parts + k]
                            out_refs[k * shares + share][block] = cells

            return 0

        lax.fori_loop(0, capacity, place, 0, unroll=4)


def settle(meta, moved, capacity, per_slab, shares, parts, after):
    first = meta is None
    chips = len(moved)
    rows, width = moved[0].shape[1:]
    if first:
        pieces = (
            jax.ShapeDtypeStruct((shares, per_slab, parts * rows, width), moved[0].dtype),
            jax.ShapeDtypeStruct((chips * CORES, TILE), jnp.int32),
        )
    else:
        pieces = (jax.ShapeDtypeStruct((per_slab, rows, width), moved[0].dtype),) * (shares * parts)
    return pl.pallas_call(
        lambda *refs: settle_kernel(chips, capacity, parts, first, *refs[len(after) :]),
        out_shape=pieces,
        in_specs=[ANY] * len(after) + ([] if first else [SMEM]) + [VMEM] * chips,
        out_specs=(VMEM, SMEM) if first else (VMEM,) * len(pieces),
        scratch_shapes=[pltpu.VMEM((chips * CORES, TILE), jnp.int32)] if first else [],
        compiler_params=pltpu.CompilerParams(vmem_limit_bytes=VMEM_BYTES),
        cost_estimate=cost(
            flops=0, bytes_accessed=2 * chips * moved[0].size, transcendentals=0
        ),
        name="settle",
    )(*after, *([] if first else [meta]), *moved)


def whole_rows(refs):
    blocks, rows, width = refs[0].shape
    return jnp.concatenate([ref[...].reshape(blocks * rows, width) for ref in refs], axis=1)


def joint_rows(ref):
    return whole_rows([ref.at[share] for share in range(ref.shape[0])])


def gram_kernel(x_ref, out_ref):
    shares = x_ref.shape[0]

    @pl.when(pl.program_id(0) == 0)
    def _():
        out_ref[...] = jnp.zeros_like(out_ref)

    cells = joint_rows(x_ref)
    at = 0
    for a in range(shares):
        product = lax.dot_general(
            cells[:, a * TILE : (a + 1) * TILE],
            cells[:, a * TILE :],
            ROWS_BY_ROWS,
            preferred_element_type=jnp.float32,
        )
        for b in range(a, shares):
            out_ref[at] += product[:, (b - a) * TILE : (b - a + 1) * TILE]
            at += 1


def gram_blocks(cells, after, steps=4):
    shares, blocks, rows, width = cells.shape
    pairs = shares * (shares + 1) // 2
    full = shares * width
    spec = pl.BlockSpec((shares, blocks // steps, rows, width), lambda i: (0, i, 0, 0))
    return pl.pallas_call(
        lambda *refs: gram_kernel(*refs[len(after) :]),
        grid=(steps,),
        out_shape=jax.ShapeDtypeStruct((pairs, TILE, TILE), jnp.float32),
        in_specs=[ANY] * len(after) + [spec],
        out_specs=pl.BlockSpec((pairs, TILE, TILE), lambda i: (0, 0, 0)),
        compiler_params=pltpu.CompilerParams(vmem_limit_bytes=VMEM_BYTES),
        cost_estimate=cost(
            flops=2 * blocks * rows * full * full,
            bytes_accessed=2 * blocks * rows * full,
            transcendentals=0,
        ),
        name="gram_blocks",
    )(*after, cells)


def cross_kernel(parts, shares, *refs):
    x_ref, (out_ref, acc_ref) = refs[0], refs[-2:]
    step = pl.program_id(0)

    @pl.when(step == 0)
    def _():
        acc_ref[...] = jnp.zeros_like(acc_ref)

    rows = x_ref.shape[2] // parts
    for part in range(parts):
        cells = slice(part * rows, (part + 1) * rows)
        acc_ref[...] += lax.dot_general(
            whole_rows([x_ref.at[share, :, cells] for share in range(shares)]),
            whole_rows(refs[1 + part * shares : 1 + (part + 1) * shares]),
            ROWS_BY_ROWS,
            preferred_element_type=jnp.float32,
        )

    @pl.when(step == pl.num_programs(0) - 1)
    def _():
        mine = lax.axis_index("snap")
        for b in range(shares):
            lanes = pl.ds(pl.multiple_of((mine ^ b) * TILE, TILE), TILE)
            out_ref[:, lanes] = acc_ref[:, b * TILE : (b + 1) * TILE]


def cross_sum(x_cells, y_cells, after, steps=4):
    parts = len(y_cells)
    shares, blocks, cells, width = x_cells.shape
    spec = pl.BlockSpec((blocks // steps, cells // parts, width), lambda i: (i, 0, 0))
    joint = pl.BlockSpec((shares, blocks // steps, cells, width), lambda i: (0, i, 0, 0))
    full = shares * width
    return pl.pallas_call(
        lambda *refs: cross_kernel(parts, shares, *refs[len(after) :]),
        grid=(steps,),
        out_shape=jax.ShapeDtypeStruct((full, full), jnp.float32),
        in_specs=[ANY] * len(after) + [joint] + [spec] * (parts * shares),
        out_specs=pl.BlockSpec((full, full), lambda i: (0, 0)),
        scratch_shapes=[pltpu.VMEM((full, full), jnp.float32)],
        compiler_params=pltpu.CompilerParams(vmem_limit_bytes=VMEM_BYTES),
        cost_estimate=cost(
            flops=2 * blocks * cells * full * full,
            bytes_accessed=4 * blocks * cells * full,
            transcendentals=0,
        ),
        name="cross_sum",
    )(*after, x_cells, *[piece for part in y_cells for piece in part])


def three_terms(value):
    high = value.astype(jnp.bfloat16).astype(jnp.float32)
    rest = value - high
    middle = rest.astype(jnp.bfloat16).astype(jnp.float32)
    return high, middle, rest - middle


def lane_of(row, lane):
    return jnp.broadcast_to(row[:, lane : lane + 1], row.shape)


def row_of(ref, row):
    return jnp.broadcast_to(ref[row : row + 1, :], (GROUP, TILE))


def factor_tile(a_ref, w_ref, u_ref, v_ref):
    panels = TILE // GROUP
    a_rows = [row_of(a_ref, i) for i in range(GROUP)]
    w_rows = [row_of(w_ref, i) for i in range(GROUP)]
    for p in range(panels):
        base = p * GROUP
        small = {
            (i, k): lane_of(a_rows[i], base + k) for i in range(GROUP) for k in range(i, GROUP)
        }
        for j in range(GROUP):
            scale = lax.rsqrt(small[j, j])
            a_rows[j] = a_rows[j] * scale
            w_rows[j] = w_rows[j] * scale
            u_ref[base + j : base + j + 1, :] = a_rows[j][:1]
            v_ref[base + j : base + j + 1, :] = w_rows[j][:1]
            below = {k: small[j, k] * scale for k in range(j + 1, GROUP)}
            for k in range(j + 1, GROUP):
                for m in range(k, GROUP):
                    small[k, m] = small[k, m] - below[k] * below[m]
            for k in range(j + 1, GROUP):
                a_rows[k] = a_rows[k] - below[k] * a_rows[j]
                w_rows[k] = w_rows[k] - below[k] * w_rows[j]
        if p + 1 == panels:
            break
        after = base + GROUP
        next_a = [row_of(a_ref, after + i) for i in range(GROUP)]
        next_w = [row_of(w_ref, after + i) for i in range(GROUP)]
        for i in range(GROUP):
            for k in range(GROUP):
                factor = lane_of(a_rows[k], after + i)
                next_a[i] = next_a[i] - factor * a_rows[k]
                next_w[i] = next_w[i] - factor * w_rows[k]
        if p + 2 < panels:
            done = after + GROUP
            u = u_ref[base:after, :]
            v = v_ref[base:after, :]
            uh, um, ul = three_terms(u)
            vh, vm, vl = three_terms(v)
            left = jnp.concatenate([uh, uh, um, uh, ul, um], axis=0).astype(jnp.bfloat16)
            right_a = jnp.concatenate([uh, um, uh, ul, uh, um], axis=0)
            right_w = jnp.concatenate([vh, vm, vh, vl, vh, vm], axis=0)
            right = jnp.concatenate([right_a, right_w], axis=1).astype(jnp.bfloat16)
            update = lax.dot_general(
                left, right, ROWS_BY_ROWS, preferred_element_type=jnp.float32
            )
            a_ref[done:, :] = a_ref[done:, :] - update[done:, :TILE]
            w_ref[done:, :] = w_ref[done:, :] - update[done:, TILE:]
        a_rows, w_rows = next_a, next_w


def factor_step(tiles, b, wide, a_ref, w_ref, u_ref, v_ref):
    row = lax.broadcasted_iota(jnp.int32, (TILE, TILE), 0)
    lane = lax.broadcasted_iota(jnp.int32, (TILE, TILE), 1)
    a_ref[...] = wide[b, b]
    w_ref[...] = jnp.where(row == lane, 1.0, 0.0)
    factor_tile(a_ref, w_ref, u_ref, v_ref)
    inverse = v_ref[...]
    wide[b, b] = jnp.where(row <= lane, u_ref[...], 0.0)
    wide[b, tiles + b] = inverse
    for j in range(1, tiles):
        wide[b, b + j] = lax.dot(
            inverse, wide[b, b + j], precision=HIGHEST, preferred_element_type=jnp.float32
        )
    for r in range(b + 1, tiles):
        for c in list(range(r, tiles)) + list(range(tiles, tiles + b + 1)):
            update = lax.dot_general(
                wide[b, r],
                wide[b, c],
                ROWS_BY_ROWS,
                precision=HIGHEST,
                preferred_element_type=jnp.float32,
            )
            wide[r, c] = -update if c == tiles + b else wide[r, c] - update


def first_kernel(tiles, rows_total, g_ref, wide, *scratch):
    at = 0
    for a in range(tiles):
        for b in range(a, tiles):
            wide[a, b] = g_ref[at] / rows_total
            at += 1
    factor_step(tiles, 0, wide, *scratch)


def next_kernel(tiles, b, _, wide, *scratch):
    factor_step(tiles, b, wide, *scratch)


def last_kernel(tiles, wide, r_ref, inv_ref, hi_ref, mid_ref, lo_ref, *scratch):
    factor_step(tiles, tiles - 1, wide, *scratch)
    zero = jnp.zeros((TILE, TILE), jnp.float32)
    for a in range(tiles):
        rows = slice(a * TILE, (a + 1) * TILE)
        for b in range(tiles):
            lanes = slice(b * TILE, (b + 1) * TILE)
            r_ref[rows, lanes] = wide[a, b] if b >= a else zero
            value = wide[a, tiles + b] if b <= a else zero
            inv_ref[rows, lanes] = value
            high, middle, low = three_terms(value)
            hi_ref[rows, lanes] = high.astype(jnp.bfloat16)
            mid_ref[rows, lanes] = middle.astype(jnp.bfloat16)
            lo_ref[rows, lanes] = low.astype(jnp.bfloat16)


def factor_call(kernel, out_shape, value, after, aliases, tiles):
    many = isinstance(out_shape, tuple)
    return pl.pallas_call(
        lambda *refs: kernel(*refs[len(after) :]),
        out_shape=out_shape,
        in_specs=[ANY] * len(after) + [VMEM],
        out_specs=(VMEM,) * len(out_shape) if many else VMEM,
        scratch_shapes=[pltpu.VMEM((TILE, TILE), jnp.float32)] * 4,
        input_output_aliases={len(after): 0} if aliases else {},
        compiler_params=pltpu.CompilerParams(vmem_limit_bytes=VMEM_BYTES),
        cost_estimate=cost(
            flops=7 * 10**9, bytes_accessed=value.size * 4, transcendentals=TILE
        ),
        name="factor",
    )(*after, value)


def factor_steps(blocks, tiles, rows_total, after):
    state = jax.ShapeDtypeStruct((tiles, 2 * tiles, TILE, TILE), jnp.float32)
    full = jax.ShapeDtypeStruct((tiles * TILE, tiles * TILE), jnp.float32)
    term = jax.ShapeDtypeStruct(full.shape, jnp.bfloat16)
    value = factor_call(
        lambda *refs: first_kernel(tiles, rows_total, *refs), state, blocks, after, False, tiles
    )
    for b in range(1, tiles - 1):
        after = yield value
        value = factor_call(
            lambda *refs: next_kernel(tiles, b, *refs), state, value, after, True, tiles
        )
    after = yield value
    yield factor_call(
        lambda *refs: last_kernel(tiles, *refs), (full, full, term, term, term), value, after, False, tiles
    )


def basis_kernel(*refs):
    hi_ref, mid_ref, lo_ref, out_ref = refs[-4:]
    cells = joint_rows(refs[0])
    total = lax.dot_general(
        cells, lo_ref[...], LANES_BY_LANES, preferred_element_type=jnp.float32
    )
    total += lax.dot_general(
        cells, mid_ref[...], LANES_BY_LANES, preferred_element_type=jnp.float32
    )
    total += lax.dot_general(
        cells, hi_ref[...], LANES_BY_LANES, preferred_element_type=jnp.float32
    )
    out_ref[...] = total.reshape(out_ref.shape)


def basis(cells, terms, call, calls, filled, after, steps=4):
    shares, blocks, rows, width = cells.shape
    full = shares * width
    size = blocks // calls // steps
    first = call * steps
    spec = pl.BlockSpec((shares, size, rows, width), lambda i: (0, first + i, 0, 0))
    term = pl.BlockSpec((full, full), lambda i: (0, 0))
    unread = ([] if filled is None else [filled]) + list(after)
    return pl.pallas_call(
        lambda *refs: basis_kernel(*refs[len(unread) :]),
        grid=(steps,),
        out_shape=jax.ShapeDtypeStruct((blocks, rows, full), jnp.float32),
        in_specs=[ANY] * len(unread) + [spec] + [term] * 3,
        out_specs=pl.BlockSpec((size, rows, full), lambda i: (first + i, 0, 0)),
        input_output_aliases={} if filled is None else {0: 0},
        compiler_params=pltpu.CompilerParams(vmem_limit_bytes=VMEM_BYTES),
        cost_estimate=cost(
            flops=6 * blocks * rows * full * full // calls,
            bytes_accessed=6 * blocks * rows * full // calls,
            transcendentals=0,
        ),
        name="basis",
    )(*unread, cells, *terms)


def sum_kernel(count, value_ref, out_ref):
    rows = out_ref.shape[0]
    total = value_ref[:rows]
    for i in range(1, count):
        total += value_ref[i * rows : (i + 1) * rows]
    out_ref[...] = total


def sum_pieces(value, count, after):
    rows, lanes = value.shape
    return pl.pallas_call(
        lambda *refs: sum_kernel(count, *refs[len(after) :]),
        out_shape=jax.ShapeDtypeStruct((rows // count, lanes), value.dtype),
        in_specs=[ANY] * len(after) + [VMEM],
        out_specs=VMEM,
        cost_estimate=cost(flops=value.size, bytes_accessed=4 * value.size, transcendentals=0),
        name="sum_pieces",
    )(*after, value)


def add_kernel(one_ref, two_ref, out_ref):
    out_ref[...] = one_ref[...] + two_ref[...]


def add(one, two, after):
    return pl.pallas_call(
        lambda *refs: add_kernel(*refs[len(after) :]),
        out_shape=jax.ShapeDtypeStruct(one.shape, one.dtype),
        in_specs=[ANY] * len(after) + [VMEM, VMEM],
        out_specs=VMEM,
        cost_estimate=cost(flops=one.size, bytes_accessed=12 * one.size, transcendentals=0),
        name="add",
    )(*after, one, two)


def join_kernel(*refs):
    rows = refs[0].shape[0]
    for i, ref in enumerate(refs[:-1]):
        refs[-1][i * rows : (i + 1) * rows] = ref[...]


def join(values, after):
    rows, lanes = values[0].shape
    return pl.pallas_call(
        lambda *refs: join_kernel(*refs[len(after) :]),
        out_shape=jax.ShapeDtypeStruct((len(values) * rows, lanes), values[0].dtype),
        in_specs=[ANY] * len(after) + [VMEM] * len(values),
        out_specs=VMEM,
        name="join",
    )(*after, *values)


def projection_kernel(slabs, divisor, inverse_ref, same_ref, other_ref, out_ref, cross_ref):
    me = lax.axis_index("space")
    rows = cross_ref.shape[0] // slabs
    for away in range(slabs):
        at = pl.ds(pl.multiple_of((me ^ away) * rows, rows), rows)
        chip = slice(away // CORES * rows, (away // CORES + 1) * rows)
        cross_ref[at, :] = (other_ref if away % CORES else same_ref)[chip]
    out_ref[...] = (
        lax.dot(
            inverse_ref[...],
            cross_ref[...],
            precision=HIGHEST,
            preferred_element_type=jnp.float32,
        )
        / divisor
    )


def project(inverse, same, other, slabs, divisor):
    return pl.pallas_call(
        lambda *refs: projection_kernel(slabs, divisor, *refs),
        out_shape=jax.ShapeDtypeStruct(inverse.shape, jnp.float32),
        in_specs=[VMEM] * 3,
        out_specs=VMEM,
        scratch_shapes=[pltpu.VMEM(inverse.shape, jnp.float32)],
        compiler_params=pltpu.CompilerParams(vmem_limit_bytes=VMEM_BYTES),
        name="project",
    )(inverse, same, other)


def swap(value, axis, mask):
    return lax.ppermute(value, axis, [(i, i ^ mask) for i in range(lax.axis_size(axis))])


def body(owned_x, owned_y, patch_dest):
    slabs = lax.axis_size("space")
    shares = lax.axis_size("snap")
    slots, patch, width = owned_x.shape
    per_slab = slots // 2
    parts = patch // shares // CELL_TILE
    rows_total = slabs * per_slab * patch
    full = shares * width
    tiles = full // TILE
    pairs = tiles * (tiles + 1) // 2

    def packed(owned, with_ids):
        tiles = owned.reshape(slots, patch // CELL_TILE, CELL_TILE, width)
        return pack(patch_dest, tiles, slabs, per_slab, with_ids)

    def merged(sent, after):
        return merge(sent[0], swap(sent[1], "space", 1), slabs // CORES, after)

    def to_chips(joined):
        return [joined[0]] + [swap(joined[m], "space", CORES * m) for m in range(1, len(joined))]

    def to_rows(pieces):
        return [pieces[0]] + [swap(pieces[r], "snap", r) for r in range(1, shares)]

    def place(meta, moved, after):
        return settle(meta, moved, slots // slabs, per_slab, shares, parts, after)

    def to_pieces(value):
        return lax.all_to_all(value, "space", split_axis=0, concat_axis=0, tiled=True)

    def hops():
        hop = 1
        while hop < shares:
            yield hop
            hop *= 2

    moved_x = to_chips(merged(packed(owned_x, True), []))
    joined_y = merged(packed(owned_y, False), moved_x[1:3])
    moved_y = to_chips(joined_y)
    pieces, meta = place(None, moved_x, joined_y[:1])
    x_cells = lax.all_to_all(pieces, "snap", split_axis=0, concat_axis=0, tiled=True)

    gram_local = gram_blocks(x_cells, moved_y[1:2])
    gram = to_pieces(gram_local.reshape(pairs * TILE, TILE))
    pieces = place(meta, moved_y, [gram_local])
    y_cells = [to_rows(pieces[part * shares : (part + 1) * shares]) for part in range(parts)]
    gram = sum_pieces(gram, slabs, y_cells[0][2:])
    for hop in hops():
        gram = add(gram, swap(gram, "snap", hop), [] if hop == 1 else y_cells[1][2:3])
    gram = lax.all_gather(gram, "space", axis=0, tiled=True)

    steps = factor_steps(gram.reshape(pairs, TILE, TILE), tiles, rows_total, [])
    state = next(steps)
    for _ in range(tiles - 3):
        state = steps.send([])
    cross_local = cross_sum(x_cells, y_cells, [state])
    state = steps.send([cross_local])
    cross = sum_pieces(to_pieces(cross_local), slabs, [state])
    r_factor, inverse, *terms = steps.send([cross])
    tied = [r_factor]
    for hop in hops():
        cross = add(cross, swap(cross, "snap", hop), tied)
        if hop == 1:
            q_basis = basis(x_cells, terms, 0, 2, None, [cross])
            tied = [q_basis]
    q_basis = basis(x_cells, terms, 1, 2, q_basis, [cross])
    same = join([cross] + [swap(cross, "space", m) for m in range(CORES, slabs, CORES)], [q_basis])
    projection = project(inverse, same, swap(same, "space", 1), slabs, math.sqrt(rows_total))
    return q_basis, r_factor, projection


def solution(mesh):
    in_specs = (P("space", None, "snap"), P("space", None, "snap"), P("space"))
    out_specs = (P("space", "snap", None), P(), P())
    return jax.shard_map(body, mesh=mesh, in_specs=in_specs, out_specs=out_specs, check_vma=False)
```

```python
import math

import jax
import jax.numpy as jnp
from jax import lax
from jax.experimental import pallas as pl
from jax.experimental.pallas import tpu as pltpu
from jax.sharding import PartitionSpec as P

TILE = 128
GROUP = 8
CORES = 2
CELL_TILE = 16
VMEM_BYTES = 32 * 1024 * 1024
HIGHEST = lax.Precision.HIGHEST
SMEM = pl.BlockSpec(memory_space=pltpu.SMEM)
VMEM = pl.BlockSpec(memory_space=pltpu.VMEM)
ANY = pl.BlockSpec(memory_space=pl.ANY)
ROWS_BY_ROWS = (((0,), (0,)), ((), ()))
LANES_BY_LANES = (((1,), (1,)), ((), ()))


def cost(flops, bytes_accessed, transcendentals):
    return pl.CostEstimate(
        flops=flops,
        bytes_accessed=bytes_accessed,
        transcendentals=transcendentals,
    )


def pack_kernel(slabs, capacity, per_slab, dest_ref, owned_ref, *refs):
    out_refs, (ids_ref, count_ref) = refs[:CORES], refs[CORES:]
    chips = slabs // CORES
    tiles = owned_ref.shape[1]
    used = capacity * tiles
    span = out_refs[0].shape[0] // chips
    me = lax.axis_index("space")
    lane = lax.broadcasted_iota(jnp.int32, (1, TILE), 1)
    ids_ref[...] = jnp.full_like(ids_ref, -1)
    for slab in range(slabs):
        count_ref[slab] = 0

    def place(i, _):
        block = dest_ref[i]

        @pl.when(block >= 0)
        def _():
            slab = lax.div(block, per_slab)
            rank = count_ref[slab]
            count_ref[slab] = rank + 1
            here = pl.ds(slab, 1)
            ids_ref[here, :] = jnp.where(lane == rank, block - slab * per_slab, ids_ref[here, :])
            away = slab ^ me
            at = pl.ds(lax.shift_right_logical(away, 1) * span + rank * tiles, tiles)
            for core in range(CORES):

                @pl.when((away & 1) == core)
                def _():
                    out_refs[core][at] = owned_ref[i]

        return 0

    lax.fori_loop(0, dest_ref.shape[0], place, 0, unroll=2)
    if span > used:
        for away in range(slabs):
            out_ref = out_refs[away % CORES]
            ids = ids_ref[pl.ds(me ^ away, 1), :].astype(jnp.float32)
            tile = jnp.broadcast_to(ids, out_ref.shape[1:]).astype(out_ref.dtype)
            out_ref[away // CORES * span + used] = tile


def pack(dest, owned, slabs, per_slab, with_ids):
    slots, tiles, rows, width = owned.shape
    chips = slabs // CORES
    capacity = slots // slabs
    span = capacity * tiles + (1 if with_ids else 0)
    sent = jax.ShapeDtypeStruct((chips * span, rows, width), owned.dtype)
    return pl.pallas_call(
        lambda *refs: pack_kernel(slabs, capacity, per_slab, *refs),
        out_shape=(sent,) * CORES,
        in_specs=[SMEM, VMEM],
        out_specs=(VMEM,) * CORES,
        scratch_shapes=[
            pltpu.VMEM((slabs, TILE), jnp.int32),
            pltpu.SMEM((slabs,), jnp.int32),
        ],
        compiler_params=pltpu.CompilerParams(vmem_limit_bytes=VMEM_BYTES),
        cost_estimate=cost(flops=0, bytes_accessed=2 * owned.size * 2, transcendentals=0),
        name="pack",
    )(dest, owned)


def merge_kernel(same_ref, other_ref, *out_refs):
    span = same_ref.shape[0] // len(out_refs)
    for chip, out_ref in enumerate(out_refs):
        out_ref[:span] = same_ref[chip * span : (chip + 1) * span]
        out_ref[span:] = other_ref[chip * span : (chip + 1) * span]


def merge(same, other, chips, after):
    tiles, rows, width = same.shape
    out = jax.ShapeDtypeStruct((CORES * tiles // chips, rows, width), same.dtype)
    return pl.pallas_call(
        lambda *refs: merge_kernel(*refs[len(after) :]),
        out_shape=(out,) * chips,
        in_specs=[ANY] * len(after) + [VMEM, VMEM],
        out_specs=(VMEM,) * chips,
        compiler_params=pltpu.CompilerParams(vmem_limit_bytes=VMEM_BYTES),
        cost_estimate=cost(flops=0, bytes_accessed=8 * same.size, transcendentals=0),
        name="merge",
    )(*after, same, other)


def settle_kernel(chips, capacity, parts, first, *refs):
    if first:
        moved_refs, (out_ref, meta_ref, ids_ref) = refs[:chips], refs[chips:]
        span = moved_refs[0].shape[0] // CORES
        for source in range(chips * CORES):
            at = source % CORES * span + span - 1
            tile = moved_refs[source // CORES][at].astype(jnp.float32)
            ids_ref[source : source + 1, :] = tile[:1].astype(jnp.int32)
        pltpu.sync_copy(ids_ref, meta_ref)
        shares = out_ref.shape[0]
    else:
        meta_ref, moved_refs, out_refs = refs[0], refs[1 : 1 + chips], refs[1 + chips :]
        span = moved_refs[0].shape[0] // CORES
        shares = len(out_refs) // parts
    tiles = shares * parts
    rows = moved_refs[0].shape[1]
    mine = lax.axis_index("snap")
    for source in range(chips * CORES):
        moved_ref = moved_refs[source // CORES]

        def place(rank, _):
            block = meta_ref[source, rank]

            @pl.when(block >= 0)
            def _():
                at = source % CORES * span + rank * tiles
                for share in range(shares):
                    if first:
                        for k in range(parts):
                            cells = slice(k * rows, (k + 1) * rows)
                            out_ref[share, block, cells] = moved_ref[at + share * parts + k]
                    else:
                        for k in range(parts):
                            cells = moved_ref[at + (mine ^ share) * parts + k]
                            out_refs[k * shares + share][block] = cells

            return 0

        lax.fori_loop(0, capacity, place, 0, unroll=4)


def settle(meta, moved, capacity, per_slab, shares, parts, after):
    first = meta is None
    chips = len(moved)
    rows, width = moved[0].shape[1:]
    if first:
        pieces = (
            jax.ShapeDtypeStruct((shares, per_slab, parts * rows, width), moved[0].dtype),
            jax.ShapeDtypeStruct((chips * CORES, TILE), jnp.int32),
        )
    else:
        pieces = (jax.ShapeDtypeStruct((per_slab, rows, width), moved[0].dtype),) * (shares * parts)
    return pl.pallas_call(
        lambda *refs: settle_kernel(chips, capacity, parts, first, *refs[len(after) :]),
        out_shape=pieces,
        in_specs=[ANY] * len(after) + ([] if first else [SMEM]) + [VMEM] * chips,
        out_specs=(VMEM, SMEM) if first else (VMEM,) * len(pieces),
        scratch_shapes=[pltpu.VMEM((chips * CORES, TILE), jnp.int32)] if first else [],
        compiler_params=pltpu.CompilerParams(vmem_limit_bytes=VMEM_BYTES),
        cost_estimate=cost(
            flops=0, bytes_accessed=2 * chips * moved[0].size, transcendentals=0
        ),
        name="settle",
    )(*after, *([] if first else [meta]), *moved)


def whole_rows(refs):
    blocks, rows, width = refs[0].shape
    return jnp.concatenate([ref[...].reshape(blocks * rows, width) for ref in refs], axis=1)


def joint_rows(ref):
    return whole_rows([ref.at[share] for share in range(ref.shape[0])])


def gram_kernel(x_ref, out_ref):
    shares = x_ref.shape[0]

    @pl.when(pl.program_id(0) == 0)
    def _():
        out_ref[...] = jnp.zeros_like(out_ref)

    cells = joint_rows(x_ref)
    at = 0
    for a in range(shares):
        product = lax.dot_general(
            cells[:, a * TILE : (a + 1) * TILE],
            cells[:, a * TILE :],
            ROWS_BY_ROWS,
            preferred_element_type=jnp.float32,
        )
        for b in range(a, shares):
            out_ref[at] += product[:, (b - a) * TILE : (b - a + 1) * TILE]
            at += 1


def gram_blocks(cells, after, steps=4):
    shares, blocks, rows, width = cells.shape
    pairs = shares * (shares + 1) // 2
    full = shares * width
    spec = pl.BlockSpec((shares, blocks // steps, rows, width), lambda i: (0, i, 0, 0))
    return pl.pallas_call(
        lambda *refs: gram_kernel(*refs[len(after) :]),
        grid=(steps,),
        out_shape=jax.ShapeDtypeStruct((pairs, TILE, TILE), jnp.float32),
        in_specs=[ANY] * len(after) + [spec],
        out_specs=pl.BlockSpec((pairs, TILE, TILE), lambda i: (0, 0, 0)),
        compiler_params=pltpu.CompilerParams(vmem_limit_bytes=VMEM_BYTES),
        cost_estimate=cost(
            flops=2 * blocks * rows * full * full,
            bytes_accessed=2 * blocks * rows * full,
            transcendentals=0,
        ),
        name="gram_blocks",
    )(*after, cells)


def cross_kernel(parts, shares, *refs):
    x_ref, (out_ref, acc_ref) = refs[0], refs[-2:]
    step = pl.program_id(0)

    @pl.when(step == 0)
    def _():
        acc_ref[...] = jnp.zeros_like(acc_ref)

    rows = x_ref.shape[2] // parts
    for part in range(parts):
        cells = slice(part * rows, (part + 1) * rows)
        acc_ref[...] += lax.dot_general(
            whole_rows([x_ref.at[share, :, cells] for share in range(shares)]),
            whole_rows(refs[1 + part * shares : 1 + (part + 1) * shares]),
            ROWS_BY_ROWS,
            preferred_element_type=jnp.float32,
        )

    @pl.when(step == pl.num_programs(0) - 1)
    def _():
        mine = lax.axis_index("snap")
        for b in range(shares):
            lanes = pl.ds(pl.multiple_of((mine ^ b) * TILE, TILE), TILE)
            out_ref[:, lanes] = acc_ref[:, b * TILE : (b + 1) * TILE]


def cross_sum(x_cells, y_cells, after, steps=4):
    parts = len(y_cells)
    shares, blocks, cells, width = x_cells.shape
    spec = pl.BlockSpec((blocks // steps, cells // parts, width), lambda i: (i, 0, 0))
    joint = pl.BlockSpec((shares, blocks // steps, cells, width), lambda i: (0, i, 0, 0))
    full = shares * width
    return pl.pallas_call(
        lambda *refs: cross_kernel(parts, shares, *refs[len(after) :]),
        grid=(steps,),
        out_shape=jax.ShapeDtypeStruct((full, full), jnp.float32),
        in_specs=[ANY] * len(after) + [joint] + [spec] * (parts * shares),
        out_specs=pl.BlockSpec((full, full), lambda i: (0, 0)),
        scratch_shapes=[pltpu.VMEM((full, full), jnp.float32)],
        compiler_params=pltpu.CompilerParams(vmem_limit_bytes=VMEM_BYTES),
        cost_estimate=cost(
            flops=2 * blocks * cells * full * full,
            bytes_accessed=4 * blocks * cells * full,
            transcendentals=0,
        ),
        name="cross_sum",
    )(*after, x_cells, *[piece for part in y_cells for piece in part])


def three_terms(value):
    high = value.astype(jnp.bfloat16).astype(jnp.float32)
    rest = value - high
    middle = rest.astype(jnp.bfloat16).astype(jnp.float32)
    return high, middle, rest - middle


def lane_of(row, lane):
    return jnp.broadcast_to(row[:, lane : lane + 1], row.shape)


def row_of(ref, row):
    return jnp.broadcast_to(ref[row : row + 1, :], (GROUP, TILE))


def factor_tile(a_ref, w_ref, u_ref, v_ref):
    panels = TILE // GROUP
    a_rows = [row_of(a_ref, i) for i in range(GROUP)]
    w_rows = [row_of(w_ref, i) for i in range(GROUP)]
    for p in range(panels):
        base = p * GROUP
        small = {
            (i, k): lane_of(a_rows[i], base + k) for i in range(GROUP) for k in range(i, GROUP)
        }
        for j in range(GROUP):
            scale = lax.rsqrt(small[j, j])
            a_rows[j] = a_rows[j] * scale
            w_rows[j] = w_rows[j] * scale
            u_ref[base + j : base + j + 1, :] = a_rows[j][:1]
            v_ref[base + j : base + j + 1, :] = w_rows[j][:1]
            below = {k: small[j, k] * scale for k in range(j + 1, GROUP)}
            for k in range(j + 1, GROUP):
                for m in range(k, GROUP):
                    small[k, m] = small[k, m] - below[k] * below[m]
            for k in range(j + 1, GROUP):
                a_rows[k] = a_rows[k] - below[k] * a_rows[j]
                w_rows[k] = w_rows[k] - below[k] * w_rows[j]
        if p + 1 == panels:
            break
        after = base + GROUP
        next_a = [row_of(a_ref, after + i) for i in range(GROUP)]
        next_w = [row_of(w_ref, after + i) for i in range(GROUP)]
        for i in range(GROUP):
            for k in range(GROUP):
                factor = lane_of(a_rows[k], after + i)
                next_a[i] = next_a[i] - factor * a_rows[k]
                next_w[i] = next_w[i] - factor * w_rows[k]
        if p + 2 < panels:
            done = after + GROUP
            u = u_ref[base:after, :]
            v = v_ref[base:after, :]
            uh, um, ul = three_terms(u)
            vh, vm, vl = three_terms(v)
            left = jnp.concatenate([uh, uh, um, uh, ul, um], axis=0).astype(jnp.bfloat16)
            right_a = jnp.concatenate([uh, um, uh, ul, uh, um], axis=0)
            right_w = jnp.concatenate([vh, vm, vh, vl, vh, vm], axis=0)
            right = jnp.concatenate([right_a, right_w], axis=1).astype(jnp.bfloat16)
            update = lax.dot_general(
                left, right, ROWS_BY_ROWS, preferred_element_type=jnp.float32
            )
            a_ref[done:, :] = a_ref[done:, :] - update[done:, :TILE]
            w_ref[done:, :] = w_ref[done:, :] - update[done:, TILE:]
        a_rows, w_rows = next_a, next_w


def factor_step(tiles, b, wide, a_ref, w_ref, u_ref, v_ref):
    row = lax.broadcasted_iota(jnp.int32, (TILE, TILE), 0)
    lane = lax.broadcasted_iota(jnp.int32, (TILE, TILE), 1)
    a_ref[...] = wide[b, b]
    w_ref[...] = jnp.where(row == lane, 1.0, 0.0)
    factor_tile(a_ref, w_ref, u_ref, v_ref)
    inverse = v_ref[...]
    wide[b, b] = jnp.where(row <= lane, u_ref[...], 0.0)
    wide[b, tiles + b] = inverse
    for j in range(1, tiles):
        wide[b, b + j] = lax.dot(
            inverse, wide[b, b + j], precision=HIGHEST, preferred_element_type=jnp.float32
        )
    for r in range(b + 1, tiles):
        for c in list(range(r, tiles)) + list(range(tiles, tiles + b + 1)):
            update = lax.dot_general(
                wide[b, r],
                wide[b, c],
                ROWS_BY_ROWS,
                precision=HIGHEST,
                preferred_element_type=jnp.float32,
            )
            wide[r, c] = -update if c == tiles + b else wide[r, c] - update


def first_kernel(tiles, rows_total, g_ref, wide, *scratch):
    at = 0
    for a in range(tiles):
        for b in range(a, tiles):
            wide[a, b] = g_ref[at] / rows_total
            at += 1
    factor_step(tiles, 0, wide, *scratch)


def next_kernel(tiles, b, _, wide, *scratch):
    factor_step(tiles, b, wide, *scratch)


def last_kernel(tiles, wide, r_ref, inv_ref, hi_ref, mid_ref, lo_ref, *scratch):
    factor_step(tiles, tiles - 1, wide, *scratch)
    zero = jnp.zeros((TILE, TILE), jnp.float32)
    for a in range(tiles):
        rows = slice(a * TILE, (a + 1) * TILE)
        for b in range(tiles):
            lanes = slice(b * TILE, (b + 1) * TILE)
            r_ref[rows, lanes] = wide[a, b] if b >= a else zero
            value = wide[a, tiles + b] if b <= a else zero
            inv_ref[rows, lanes] = value
            high, middle, low = three_terms(value)
            hi_ref[rows, lanes] = high.astype(jnp.bfloat16)
            mid_ref[rows, lanes] = middle.astype(jnp.bfloat16)
            lo_ref[rows, lanes] = low.astype(jnp.bfloat16)


def factor_call(kernel, out_shape, value, after, aliases, tiles):
    many = isinstance(out_shape, tuple)
    return pl.pallas_call(
        lambda *refs: kernel(*refs[len(after) :]),
        out_shape=out_shape,
        in_specs=[ANY] * len(after) + [VMEM],
        out_specs=(VMEM,) * len(out_shape) if many else VMEM,
        scratch_shapes=[pltpu.VMEM((TILE, TILE), jnp.float32)] * 4,
        input_output_aliases={len(after): 0} if aliases else {},
        compiler_params=pltpu.CompilerParams(vmem_limit_bytes=VMEM_BYTES),
        cost_estimate=cost(
            flops=7 * 10**9, bytes_accessed=value.size * 4, transcendentals=TILE
        ),
        name="factor",
    )(*after, value)


def factor_steps(blocks, tiles, rows_total, after):
    state = jax.ShapeDtypeStruct((tiles, 2 * tiles, TILE, TILE), jnp.float32)
    full = jax.ShapeDtypeStruct((tiles * TILE, tiles * TILE), jnp.float32)
    term = jax.ShapeDtypeStruct(full.shape, jnp.bfloat16)
    value = factor_call(
        lambda *refs: first_kernel(tiles, rows_total, *refs), state, blocks, after, False, tiles
    )
    for b in range(1, tiles - 1):
        after = yield value
        value = factor_call(
            lambda *refs: next_kernel(tiles, b, *refs), state, value, after, True, tiles
        )
    after = yield value
    yield factor_call(
        lambda *refs: last_kernel(tiles, *refs), (full, full, term, term, term), value, after, False, tiles
    )


def basis_kernel(*refs):
    hi_ref, mid_ref, lo_ref, out_ref = refs[-4:]
    cells = joint_rows(refs[0])
    total = lax.dot_general(
        cells, lo_ref[...], LANES_BY_LANES, preferred_element_type=jnp.float32
    )
    total += lax.dot_general(
        cells, mid_ref[...], LANES_BY_LANES, preferred_element_type=jnp.float32
    )
    total += lax.dot_general(
        cells, hi_ref[...], LANES_BY_LANES, preferred_element_type=jnp.float32
    )
    out_ref[...] = total.reshape(out_ref.shape)


def basis(cells, terms, call, calls, filled, after, steps=4):
    shares, blocks, rows, width = cells.shape
    full = shares * width
    size = blocks // calls // steps
    first = call * steps
    spec = pl.BlockSpec((shares, size, rows, width), lambda i: (0, first + i, 0, 0))
    term = pl.BlockSpec((full, full), lambda i: (0, 0))
    unread = ([] if filled is None else [filled]) + list(after)
    return pl.pallas_call(
        lambda *refs: basis_kernel(*refs[len(unread) :]),
        grid=(steps,),
        out_shape=jax.ShapeDtypeStruct((blocks, rows, full), jnp.float32),
        in_specs=[ANY] * len(unread) + [spec] + [term] * 3,
        out_specs=pl.BlockSpec((size, rows, full), lambda i: (first + i, 0, 0)),
        input_output_aliases={} if filled is None else {0: 0},
        compiler_params=pltpu.CompilerParams(vmem_limit_bytes=VMEM_BYTES),
        cost_estimate=cost(
            flops=6 * blocks * rows * full * full // calls,
            bytes_accessed=6 * blocks * rows * full // calls,
            transcendentals=0,
        ),
        name="basis",
    )(*unread, cells, *terms)


def sum_kernel(count, value_ref, out_ref):
    rows = out_ref.shape[0]
    total = value_ref[:rows]
    for i in range(1, count):
        total += value_ref[i * rows : (i + 1) * rows]
    out_ref[...] = total


def sum_pieces(value, count, after):
    rows, lanes = value.shape
    return pl.pallas_call(
        lambda *refs: sum_kernel(count, *refs[len(after) :]),
        out_shape=jax.ShapeDtypeStruct((rows // count, lanes), value.dtype),
        in_specs=[ANY] * len(after) + [VMEM],
        out_specs=VMEM,
        cost_estimate=cost(flops=value.size, bytes_accessed=4 * value.size, transcendentals=0),
        name="sum_pieces",
    )(*after, value)


def add_kernel(one_ref, two_ref, out_ref):
    out_ref[...] = one_ref[...] + two_ref[...]


def add(one, two, after):
    return pl.pallas_call(
        lambda *refs: add_kernel(*refs[len(after) :]),
        out_shape=jax.ShapeDtypeStruct(one.shape, one.dtype),
        in_specs=[ANY] * len(after) + [VMEM, VMEM],
        out_specs=VMEM,
        cost_estimate=cost(flops=one.size, bytes_accessed=12 * one.size, transcendentals=0),
        name="add",
    )(*after, one, two)


def join_kernel(*refs):
    rows = refs[0].shape[0]
    for i, ref in enumerate(refs[:-1]):
        refs[-1][i * rows : (i + 1) * rows] = ref[...]


def join(values, after):
    rows, lanes = values[0].shape
    return pl.pallas_call(
        lambda *refs: join_kernel(*refs[len(after) :]),
        out_shape=jax.ShapeDtypeStruct((len(values) * rows, lanes), values[0].dtype),
        in_specs=[ANY] * len(after) + [VMEM] * len(values),
        out_specs=VMEM,
        name="join",
    )(*after, *values)


def projection_kernel(slabs, divisor, inverse_ref, same_ref, other_ref, out_ref, cross_ref):
    me = lax.axis_index("space")
    rows = cross_ref.shape[0] // slabs
    for away in range(slabs):
        at = pl.ds(pl.multiple_of((me ^ away) * rows, rows), rows)
        chip = slice(away // CORES * rows, (away // CORES + 1) * rows)
        cross_ref[at, :] = (other_ref if away % CORES else same_ref)[chip]
    out_ref[...] = (
        lax.dot(
            inverse_ref[...],
            cross_ref[...],
            precision=HIGHEST,
            preferred_element_type=jnp.float32,
        )
        / divisor
    )


def project(inverse, same, other, slabs, divisor):
    return pl.pallas_call(
        lambda *refs: projection_kernel(slabs, divisor, *refs),
        out_shape=jax.ShapeDtypeStruct(inverse.shape, jnp.float32),
        in_specs=[VMEM] * 3,
        out_specs=VMEM,
        scratch_shapes=[pltpu.VMEM(inverse.shape, jnp.float32)],
        compiler_params=pltpu.CompilerParams(vmem_limit_bytes=VMEM_BYTES),
        name="project",
    )(inverse, same, other)


def swap(value, axis, mask):
    return lax.ppermute(value, axis, [(i, i ^ mask) for i in range(lax.axis_size(axis))])


def body(owned_x, owned_y, patch_dest):
    slabs = lax.axis_size("space")
    shares = lax.axis_size("snap")
    slots, patch, width = owned_x.shape
    per_slab = slots // 2
    parts = patch // shares // CELL_TILE
    rows_total = slabs * per_slab * patch
    full = shares * width
    tiles = full // TILE
    pairs = tiles * (tiles + 1) // 2

    def packed(owned, with_ids):
        tiles = owned.reshape(slots, patch // CELL_TILE, CELL_TILE, width)
        return pack(patch_dest, tiles, slabs, per_slab, with_ids)

    def merged(sent, after):
        return merge(sent[0], swap(sent[1], "space", 1), slabs // CORES, after)

    def to_chips(joined):
        return [joined[0]] + [swap(joined[m], "space", CORES * m) for m in range(1, len(joined))]

    def to_rows(pieces):
        return [pieces[0]] + [swap(pieces[r], "snap", r) for r in range(1, shares)]

    def place(meta, moved, after):
        return settle(meta, moved, slots // slabs, per_slab, shares, parts, after)

    def to_pieces(value):
        return lax.all_to_all(value, "space", split_axis=0, concat_axis=0, tiled=True)

    def hops():
        hop = 1
        while hop < shares:
            yield hop
            hop *= 2

    moved_x = to_chips(merged(packed(owned_x, True), []))
    joined_y = merged(packed(owned_y, False), moved_x[1:3])
    moved_y = to_chips(joined_y)
    pieces, meta = place(None, moved_x, joined_y[:1])
    x_cells = lax.all_to_all(pieces, "snap", split_axis=0, concat_axis=0, tiled=True)

    gram_local = gram_blocks(x_cells, moved_y[1:2])
    gram = to_pieces(gram_local.reshape(pairs * TILE, TILE))
    pieces = place(meta, moved_y, [gram_local])
    y_cells = [to_rows(pieces[part * shares : (part + 1) * shares]) for part in range(parts)]
    gram = sum_pieces(gram, slabs, pieces[:1])
    for hop in hops():
        gram = add(gram, swap(gram, "snap", hop), y_cells[0][hop : hop + 1])
    gram = lax.all_gather(gram, "space", axis=0, tiled=True)

    steps = factor_steps(gram.reshape(pairs, TILE, TILE), tiles, rows_total, [])
    state = next(steps)
    for _ in range(tiles - 2):
        state = steps.send([])
    cross_local = cross_sum(x_cells, y_cells, [state])
    cross = to_pieces(cross_local)
    r_factor, inverse, *terms = steps.send([cross_local])

    q_basis = basis(x_cells, terms, 0, 2, None, [])
    cross = sum_pieces(cross, slabs, [q_basis])
    q_basis = basis(x_cells, terms, 1, 2, q_basis, [cross])
    for hop in hops():
        cross = add(cross, swap(cross, "snap", hop), [q_basis] if hop == 1 else [])
    same = join([cross] + [swap(cross, "space", m) for m in range(CORES, slabs, CORES)], [])
    projection = project(inverse, same, swap(same, "space", 1), slabs, math.sqrt(rows_total))
    return q_basis, r_factor, projection


def solution(mesh):
    in_specs = (P("space", None, "snap"), P("space", None, "snap"), P("space"))
    out_specs = (P("space", "snap", None), P(), P())
    return jax.shard_map(body, mesh=mesh, in_specs=in_specs, out_specs=out_specs, check_vma=False)
```

```python
import math

import jax
import jax.numpy as jnp
from jax import lax
from jax.experimental import pallas as pl
from jax.experimental.pallas import tpu as pltpu
from jax.sharding import PartitionSpec as P

TILE = 128
GROUP = 8
CORES = 2
CELL_TILE = 16
VMEM_BYTES = 32 * 1024 * 1024
HIGHEST = lax.Precision.HIGHEST
SMEM = pl.BlockSpec(memory_space=pltpu.SMEM)
VMEM = pl.BlockSpec(memory_space=pltpu.VMEM)
ANY = pl.BlockSpec(memory_space=pl.ANY)
ROWS_BY_ROWS = (((0,), (0,)), ((), ()))
LANES_BY_LANES = (((1,), (1,)), ((), ()))


def cost(flops, bytes_accessed, transcendentals):
    return pl.CostEstimate(
        flops=flops,
        bytes_accessed=bytes_accessed,
        transcendentals=transcendentals,
    )


def pack_kernel(slabs, capacity, per_slab, dest_ref, owned_ref, *refs):
    out_refs, (ids_ref, count_ref) = refs[:CORES], refs[CORES:]
    chips = slabs // CORES
    tiles = owned_ref.shape[1]
    used = capacity * tiles
    span = out_refs[0].shape[0] // chips
    me = lax.axis_index("space")
    lane = lax.broadcasted_iota(jnp.int32, (1, TILE), 1)
    ids_ref[...] = jnp.full_like(ids_ref, -1)
    for slab in range(slabs):
        count_ref[slab] = 0

    def place(i, _):
        block = dest_ref[i]

        @pl.when(block >= 0)
        def _():
            slab = lax.div(block, per_slab)
            rank = count_ref[slab]
            count_ref[slab] = rank + 1
            here = pl.ds(slab, 1)
            ids_ref[here, :] = jnp.where(lane == rank, block - slab * per_slab, ids_ref[here, :])
            away = slab ^ me
            at = pl.ds(lax.shift_right_logical(away, 1) * span + rank * tiles, tiles)
            for core in range(CORES):

                @pl.when((away & 1) == core)
                def _():
                    out_refs[core][at] = owned_ref[i]

        return 0

    lax.fori_loop(0, dest_ref.shape[0], place, 0, unroll=2)
    if span > used:
        for away in range(slabs):
            out_ref = out_refs[away % CORES]
            ids = ids_ref[pl.ds(me ^ away, 1), :].astype(jnp.float32)
            tile = jnp.broadcast_to(ids, out_ref.shape[1:]).astype(out_ref.dtype)
            out_ref[away // CORES * span + used] = tile


def pack(dest, owned, slabs, per_slab, with_ids):
    slots, tiles, rows, width = owned.shape
    chips = slabs // CORES
    capacity = slots // slabs
    span = capacity * tiles + (1 if with_ids else 0)
    sent = jax.ShapeDtypeStruct((chips * span, rows, width), owned.dtype)
    return pl.pallas_call(
        lambda *refs: pack_kernel(slabs, capacity, per_slab, *refs),
        out_shape=(sent,) * CORES,
        in_specs=[SMEM, VMEM],
        out_specs=(VMEM,) * CORES,
        scratch_shapes=[
            pltpu.VMEM((slabs, TILE), jnp.int32),
            pltpu.SMEM((slabs,), jnp.int32),
        ],
        compiler_params=pltpu.CompilerParams(vmem_limit_bytes=VMEM_BYTES),
        cost_estimate=cost(flops=0, bytes_accessed=2 * owned.size * 2, transcendentals=0),
        name="pack",
    )(dest, owned)


def merge_kernel(same_ref, other_ref, *out_refs):
    span = same_ref.shape[0] // len(out_refs)
    for chip, out_ref in enumerate(out_refs):
        out_ref[:span] = same_ref[chip * span : (chip + 1) * span]
        out_ref[span:] = other_ref[chip * span : (chip + 1) * span]


def merge(same, other, chips, after):
    tiles, rows, width = same.shape
    out = jax.ShapeDtypeStruct((CORES * tiles // chips, rows, width), same.dtype)
    return pl.pallas_call(
        lambda *refs: merge_kernel(*refs[len(after) :]),
        out_shape=(out,) * chips,
        in_specs=[ANY] * len(after) + [VMEM, VMEM],
        out_specs=(VMEM,) * chips,
        compiler_params=pltpu.CompilerParams(vmem_limit_bytes=VMEM_BYTES),
        cost_estimate=cost(flops=0, bytes_accessed=8 * same.size, transcendentals=0),
        name="merge",
    )(*after, same, other)


def settle_kernel(chips, capacity, parts, first, *refs):
    if first:
        moved_refs, (out_ref, meta_ref, ids_ref) = refs[:chips], refs[chips:]
        span = moved_refs[0].shape[0] // CORES
        for source in range(chips * CORES):
            at = source % CORES * span + span - 1
            tile = moved_refs[source // CORES][at].astype(jnp.float32)
            ids_ref[source : source + 1, :] = tile[:1].astype(jnp.int32)
        pltpu.sync_copy(ids_ref, meta_ref)
        shares = out_ref.shape[0]
    else:
        meta_ref, moved_refs, out_refs = refs[0], refs[1 : 1 + chips], refs[1 + chips :]
        span = moved_refs[0].shape[0] // CORES
        shares = len(out_refs) // parts
    tiles = shares * parts
    rows = moved_refs[0].shape[1]
    mine = lax.axis_index("snap")
    for source in range(chips * CORES):
        moved_ref = moved_refs[source // CORES]

        def place(rank, _):
            block = meta_ref[source, rank]

            @pl.when(block >= 0)
            def _():
                at = source % CORES * span + rank * tiles
                for share in range(shares):
                    if first:
                        for k in range(parts):
                            cells = slice(k * rows, (k + 1) * rows)
                            out_ref[share, block, cells] = moved_ref[at + share * parts + k]
                    else:
                        for k in range(parts):
                            cells = moved_ref[at + (mine ^ share) * parts + k]
                            out_refs[k * shares + share][block] = cells

            return 0

        lax.fori_loop(0, capacity, place, 0, unroll=4)


def settle(meta, moved, capacity, per_slab, shares, parts, after):
    first = meta is None
    chips = len(moved)
    rows, width = moved[0].shape[1:]
    if first:
        pieces = (
            jax.ShapeDtypeStruct((shares, per_slab, parts * rows, width), moved[0].dtype),
            jax.ShapeDtypeStruct((chips * CORES, TILE), jnp.int32),
        )
    else:
        pieces = (jax.ShapeDtypeStruct((per_slab, rows, width), moved[0].dtype),) * (shares * parts)
    return pl.pallas_call(
        lambda *refs: settle_kernel(chips, capacity, parts, first, *refs[len(after) :]),
        out_shape=pieces,
        in_specs=[ANY] * len(after) + ([] if first else [SMEM]) + [VMEM] * chips,
        out_specs=(VMEM, SMEM) if first else (VMEM,) * len(pieces),
        scratch_shapes=[pltpu.VMEM((chips * CORES, TILE), jnp.int32)] if first else [],
        compiler_params=pltpu.CompilerParams(vmem_limit_bytes=VMEM_BYTES),
        cost_estimate=cost(
            flops=0, bytes_accessed=2 * chips * moved[0].size, transcendentals=0
        ),
        name="settle",
    )(*after, *([] if first else [meta]), *moved)


def whole_rows(refs):
    blocks, rows, width = refs[0].shape
    return jnp.concatenate([ref[...].reshape(blocks * rows, width) for ref in refs], axis=1)


def joint_rows(ref):
    return whole_rows([ref.at[share] for share in range(ref.shape[0])])


def gram_kernel(x_ref, out_ref):
    shares = x_ref.shape[0]

    @pl.when(pl.program_id(0) == 0)
    def _():
        out_ref[...] = jnp.zeros_like(out_ref)

    cells = joint_rows(x_ref)
    at = 0
    for a in range(shares):
        product = lax.dot_general(
            cells[:, a * TILE : (a + 1) * TILE],
            cells[:, a * TILE :],
            ROWS_BY_ROWS,
            preferred_element_type=jnp.float32,
        )
        for b in range(a, shares):
            out_ref[at] += product[:, (b - a) * TILE : (b - a + 1) * TILE]
            at += 1


def gram_blocks(cells, after, steps=4):
    shares, blocks, rows, width = cells.shape
    pairs = shares * (shares + 1) // 2
    full = shares * width
    spec = pl.BlockSpec((shares, blocks // steps, rows, width), lambda i: (0, i, 0, 0))
    return pl.pallas_call(
        lambda *refs: gram_kernel(*refs[len(after) :]),
        grid=(steps,),
        out_shape=jax.ShapeDtypeStruct((pairs, TILE, TILE), jnp.float32),
        in_specs=[ANY] * len(after) + [spec],
        out_specs=pl.BlockSpec((pairs, TILE, TILE), lambda i: (0, 0, 0)),
        compiler_params=pltpu.CompilerParams(vmem_limit_bytes=VMEM_BYTES),
        cost_estimate=cost(
            flops=2 * blocks * rows * full * full,
            bytes_accessed=2 * blocks * rows * full,
            transcendentals=0,
        ),
        name="gram_blocks",
    )(*after, cells)


def cross_kernel(parts, shares, *refs):
    x_ref, (out_ref, acc_ref) = refs[0], refs[-2:]
    step = pl.program_id(0)

    @pl.when(step == 0)
    def _():
        acc_ref[...] = jnp.zeros_like(acc_ref)

    rows = x_ref.shape[2] // parts
    for part in range(parts):
        cells = slice(part * rows, (part + 1) * rows)
        acc_ref[...] += lax.dot_general(
            whole_rows([x_ref.at[share, :, cells] for share in range(shares)]),
            whole_rows(refs[1 + part * shares : 1 + (part + 1) * shares]),
            ROWS_BY_ROWS,
            preferred_element_type=jnp.float32,
        )

    @pl.when(step == pl.num_programs(0) - 1)
    def _():
        mine = lax.axis_index("snap")
        for b in range(shares):
            lanes = pl.ds(pl.multiple_of((mine ^ b) * TILE, TILE), TILE)
            out_ref[:, lanes] = acc_ref[:, b * TILE : (b + 1) * TILE]


def cross_sum(x_cells, y_cells, after, steps=4):
    parts = len(y_cells)
    shares, blocks, cells, width = x_cells.shape
    spec = pl.BlockSpec((blocks // steps, cells // parts, width), lambda i: (i, 0, 0))
    joint = pl.BlockSpec((shares, blocks // steps, cells, width), lambda i: (0, i, 0, 0))
    full = shares * width
    return pl.pallas_call(
        lambda *refs: cross_kernel(parts, shares, *refs[len(after) :]),
        grid=(steps,),
        out_shape=jax.ShapeDtypeStruct((full, full), jnp.float32),
        in_specs=[ANY] * len(after) + [joint] + [spec] * (parts * shares),
        out_specs=pl.BlockSpec((full, full), lambda i: (0, 0)),
        scratch_shapes=[pltpu.VMEM((full, full), jnp.float32)],
        compiler_params=pltpu.CompilerParams(vmem_limit_bytes=VMEM_BYTES),
        cost_estimate=cost(
            flops=2 * blocks * cells * full * full,
            bytes_accessed=4 * blocks * cells * full,
            transcendentals=0,
        ),
        name="cross_sum",
    )(*after, x_cells, *[piece for part in y_cells for piece in part])


def three_terms(value):
    high = value.astype(jnp.bfloat16).astype(jnp.float32)
    rest = value - high
    middle = rest.astype(jnp.bfloat16).astype(jnp.float32)
    return high, middle, rest - middle


def lane_of(row, lane):
    return jnp.broadcast_to(row[:, lane : lane + 1], row.shape)


def row_of(ref, row):
    return jnp.broadcast_to(ref[row : row + 1, :], (GROUP, TILE))


def factor_tile(a_ref, w_ref, u_ref, v_ref):
    panels = TILE // GROUP
    a_rows = [row_of(a_ref, i) for i in range(GROUP)]
    w_rows = [row_of(w_ref, i) for i in range(GROUP)]
    for p in range(panels):
        base = p * GROUP
        small = {
            (i, k): lane_of(a_rows[i], base + k) for i in range(GROUP) for k in range(i, GROUP)
        }
        for j in range(GROUP):
            scale = lax.rsqrt(small[j, j])
            a_rows[j] = a_rows[j] * scale
            w_rows[j] = w_rows[j] * scale
            u_ref[base + j : base + j + 1, :] = a_rows[j][:1]
            v_ref[base + j : base + j + 1, :] = w_rows[j][:1]
            below = {k: small[j, k] * scale for k in range(j + 1, GROUP)}
            for k in range(j + 1, GROUP):
                for m in range(k, GROUP):
                    small[k, m] = small[k, m] - below[k] * below[m]
            for k in range(j + 1, GROUP):
                a_rows[k] = a_rows[k] - below[k] * a_rows[j]
                w_rows[k] = w_rows[k] - below[k] * w_rows[j]
        if p + 1 == panels:
            break
        after = base + GROUP
        next_a = [row_of(a_ref, after + i) for i in range(GROUP)]
        next_w = [row_of(w_ref, after + i) for i in range(GROUP)]
        for i in range(GROUP):
            for k in range(GROUP):
                factor = lane_of(a_rows[k], after + i)
                next_a[i] = next_a[i] - factor * a_rows[k]
                next_w[i] = next_w[i] - factor * w_rows[k]
        if p + 2 < panels:
            done = after + GROUP
            u = u_ref[base:after, :]
            v = v_ref[base:after, :]
            uh, um, ul = three_terms(u)
            vh, vm, vl = three_terms(v)
            left = jnp.concatenate([uh, uh, um, uh, ul, um], axis=0).astype(jnp.bfloat16)
            right_a = jnp.concatenate([uh, um, uh, ul, uh, um], axis=0)
            right_w = jnp.concatenate([vh, vm, vh, vl, vh, vm], axis=0)
            right = jnp.concatenate([right_a, right_w], axis=1).astype(jnp.bfloat16)
            update = lax.dot_general(
                left, right, ROWS_BY_ROWS, preferred_element_type=jnp.float32
            )
            a_ref[done:, :] = a_ref[done:, :] - update[done:, :TILE]
            w_ref[done:, :] = w_ref[done:, :] - update[done:, TILE:]
        a_rows, w_rows = next_a, next_w


def factor_step(tiles, b, wide, a_ref, w_ref, u_ref, v_ref):
    row = lax.broadcasted_iota(jnp.int32, (TILE, TILE), 0)
    lane = lax.broadcasted_iota(jnp.int32, (TILE, TILE), 1)
    a_ref[...] = wide[b, b]
    w_ref[...] = jnp.where(row == lane, 1.0, 0.0)
    factor_tile(a_ref, w_ref, u_ref, v_ref)
    inverse = v_ref[...]
    wide[b, b] = jnp.where(row <= lane, u_ref[...], 0.0)
    wide[b, tiles + b] = inverse
    for j in range(1, tiles):
        wide[b, b + j] = lax.dot(
            inverse, wide[b, b + j], precision=HIGHEST, preferred_element_type=jnp.float32
        )
    for r in range(b + 1, tiles):
        for c in list(range(r, tiles)) + list(range(tiles, tiles + b + 1)):
            update = lax.dot_general(
                wide[b, r],
                wide[b, c],
                ROWS_BY_ROWS,
                precision=HIGHEST,
                preferred_element_type=jnp.float32,
            )
            wide[r, c] = -update if c == tiles + b else wide[r, c] - update


def first_kernel(tiles, rows_total, g_ref, wide, *scratch):
    at = 0
    for a in range(tiles):
        for b in range(a, tiles):
            wide[a, b] = g_ref[at] / rows_total
            at += 1
    factor_step(tiles, 0, wide, *scratch)


def next_kernel(tiles, b, _, wide, *scratch):
    factor_step(tiles, b, wide, *scratch)


def last_kernel(tiles, wide, r_ref, inv_ref, hi_ref, mid_ref, lo_ref, *scratch):
    factor_step(tiles, tiles - 1, wide, *scratch)
    zero = jnp.zeros((TILE, TILE), jnp.float32)
    for a in range(tiles):
        rows = slice(a * TILE, (a + 1) * TILE)
        for b in range(tiles):
            lanes = slice(b * TILE, (b + 1) * TILE)
            r_ref[rows, lanes] = wide[a, b] if b >= a else zero
            value = wide[a, tiles + b] if b <= a else zero
            inv_ref[rows, lanes] = value
            high, middle, low = three_terms(value)
            hi_ref[rows, lanes] = high.astype(jnp.bfloat16)
            mid_ref[rows, lanes] = middle.astype(jnp.bfloat16)
            lo_ref[rows, lanes] = low.astype(jnp.bfloat16)


def factor_call(kernel, out_shape, value, after, aliases, tiles):
    many = isinstance(out_shape, tuple)
    return pl.pallas_call(
        lambda *refs: kernel(*refs[len(after) :]),
        out_shape=out_shape,
        in_specs=[ANY] * len(after) + [VMEM],
        out_specs=(VMEM,) * len(out_shape) if many else VMEM,
        scratch_shapes=[pltpu.VMEM((TILE, TILE), jnp.float32)] * 4,
        input_output_aliases={len(after): 0} if aliases else {},
        compiler_params=pltpu.CompilerParams(vmem_limit_bytes=VMEM_BYTES),
        cost_estimate=cost(
            flops=7 * 10**9, bytes_accessed=value.size * 4, transcendentals=TILE
        ),
        name="factor",
    )(*after, value)


def factor_steps(blocks, tiles, rows_total, after):
    state = jax.ShapeDtypeStruct((tiles, 2 * tiles, TILE, TILE), jnp.float32)
    full = jax.ShapeDtypeStruct((tiles * TILE, tiles * TILE), jnp.float32)
    term = jax.ShapeDtypeStruct(full.shape, jnp.bfloat16)
    value = factor_call(
        lambda *refs: first_kernel(tiles, rows_total, *refs), state, blocks, after, False, tiles
    )
    for b in range(1, tiles - 1):
        after = yield value
        value = factor_call(
            lambda *refs: next_kernel(tiles, b, *refs), state, value, after, True, tiles
        )
    after = yield value
    yield factor_call(
        lambda *refs: last_kernel(tiles, *refs), (full, full, term, term, term), value, after, False, tiles
    )


def basis_kernel(*refs):
    hi_ref, mid_ref, lo_ref, out_ref = refs[-4:]
    cells = joint_rows(refs[0])
    total = lax.dot_general(
        cells, lo_ref[...], LANES_BY_LANES, preferred_element_type=jnp.float32
    )
    total += lax.dot_general(
        cells, mid_ref[...], LANES_BY_LANES, preferred_element_type=jnp.float32
    )
    total += lax.dot_general(
        cells, hi_ref[...], LANES_BY_LANES, preferred_element_type=jnp.float32
    )
    out_ref[...] = total.reshape(out_ref.shape)


def basis(cells, terms, call, calls, filled, after, steps=4):
    shares, blocks, rows, width = cells.shape
    full = shares * width
    size = blocks // calls // steps
    first = call * steps
    spec = pl.BlockSpec((shares, size, rows, width), lambda i: (0, first + i, 0, 0))
    term = pl.BlockSpec((full, full), lambda i: (0, 0))
    unread = ([] if filled is None else [filled]) + list(after)
    return pl.pallas_call(
        lambda *refs: basis_kernel(*refs[len(unread) :]),
        grid=(steps,),
        out_shape=jax.ShapeDtypeStruct((blocks, rows, full), jnp.float32),
        in_specs=[ANY] * len(unread) + [spec] + [term] * 3,
        out_specs=pl.BlockSpec((size, rows, full), lambda i: (first + i, 0, 0)),
        input_output_aliases={} if filled is None else {0: 0},
        compiler_params=pltpu.CompilerParams(vmem_limit_bytes=VMEM_BYTES),
        cost_estimate=cost(
            flops=6 * blocks * rows * full * full // calls,
            bytes_accessed=6 * blocks * rows * full // calls,
            transcendentals=0,
        ),
        name="basis",
    )(*unread, cells, *terms)


def sum_kernel(count, value_ref, out_ref):
    rows = out_ref.shape[0]
    total = value_ref[:rows]
    for i in range(1, count):
        total += value_ref[i * rows : (i + 1) * rows]
    out_ref[...] = total


def sum_pieces(value, count, after):
    rows, lanes = value.shape
    return pl.pallas_call(
        lambda *refs: sum_kernel(count, *refs[len(after) :]),
        out_shape=jax.ShapeDtypeStruct((rows // count, lanes), value.dtype),
        in_specs=[ANY] * len(after) + [VMEM],
        out_specs=VMEM,
        cost_estimate=cost(flops=value.size, bytes_accessed=4 * value.size, transcendentals=0),
        name="sum_pieces",
    )(*after, value)


def add_kernel(one_ref, two_ref, out_ref):
    out_ref[...] = one_ref[...] + two_ref[...]


def add(one, two, after):
    return pl.pallas_call(
        lambda *refs: add_kernel(*refs[len(after) :]),
        out_shape=jax.ShapeDtypeStruct(one.shape, one.dtype),
        in_specs=[ANY] * len(after) + [VMEM, VMEM],
        out_specs=VMEM,
        cost_estimate=cost(flops=one.size, bytes_accessed=12 * one.size, transcendentals=0),
        name="add",
    )(*after, one, two)


def join_kernel(*refs):
    rows = refs[0].shape[0]
    for i, ref in enumerate(refs[:-1]):
        refs[-1][i * rows : (i + 1) * rows] = ref[...]


def join(values, after):
    rows, lanes = values[0].shape
    return pl.pallas_call(
        lambda *refs: join_kernel(*refs[len(after) :]),
        out_shape=jax.ShapeDtypeStruct((len(values) * rows, lanes), values[0].dtype),
        in_specs=[ANY] * len(after) + [VMEM] * len(values),
        out_specs=VMEM,
        name="join",
    )(*after, *values)


def projection_kernel(slabs, divisor, inverse_ref, same_ref, other_ref, out_ref, cross_ref):
    me = lax.axis_index("space")
    rows = cross_ref.shape[0] // slabs
    for away in range(slabs):
        at = pl.ds(pl.multiple_of((me ^ away) * rows, rows), rows)
        chip = slice(away // CORES * rows, (away // CORES + 1) * rows)
        cross_ref[at, :] = (other_ref if away % CORES else same_ref)[chip]
    out_ref[...] = (
        lax.dot(
            inverse_ref[...],
            cross_ref[...],
            precision=HIGHEST,
            preferred_element_type=jnp.float32,
        )
        / divisor
    )


def project(inverse, same, other, slabs, divisor):
    return pl.pallas_call(
        lambda *refs: projection_kernel(slabs, divisor, *refs),
        out_shape=jax.ShapeDtypeStruct(inverse.shape, jnp.float32),
        in_specs=[VMEM] * 3,
        out_specs=VMEM,
        scratch_shapes=[pltpu.VMEM(inverse.shape, jnp.float32)],
        compiler_params=pltpu.CompilerParams(vmem_limit_bytes=VMEM_BYTES),
        name="project",
    )(inverse, same, other)


def swap(value, axis, mask):
    return lax.ppermute(value, axis, [(i, i ^ mask) for i in range(lax.axis_size(axis))])


def body(owned_x, owned_y, patch_dest):
    slabs = lax.axis_size("space")
    shares = lax.axis_size("snap")
    slots, patch, width = owned_x.shape
    per_slab = slots // 2
    parts = patch // shares // CELL_TILE
    rows_total = slabs * per_slab * patch
    full = shares * width
    tiles = full // TILE
    pairs = tiles * (tiles + 1) // 2

    def packed(owned, with_ids):
        tiles = owned.reshape(slots, patch // CELL_TILE, CELL_TILE, width)
        return pack(patch_dest, tiles, slabs, per_slab, with_ids)

    def merged(sent, after):
        return merge(sent[0], swap(sent[1], "space", 1), slabs // CORES, after)

    def to_chips(joined):
        return [joined[0]] + [swap(joined[m], "space", CORES * m) for m in range(1, len(joined))]

    def to_rows(pieces):
        return [pieces[0]] + [swap(pieces[r], "snap", r) for r in range(1, shares)]

    def place(meta, moved, after):
        return settle(meta, moved, slots // slabs, per_slab, shares, parts, after)

    def to_pieces(value):
        return lax.all_to_all(value, "space", split_axis=0, concat_axis=0, tiled=True)

    def hops():
        hop = 1
        while hop < shares:
            yield hop
            hop *= 2

    moved_x = to_chips(merged(packed(owned_x, True), []))
    joined_y = merged(packed(owned_y, False), moved_x[1:3])
    moved_y = to_chips(joined_y)
    pieces, meta = place(None, moved_x, joined_y[:1])
    x_cells = lax.all_to_all(pieces, "snap", split_axis=0, concat_axis=0, tiled=True)

    gram_local = gram_blocks(x_cells, moved_y[1:2])
    gram = to_pieces(gram_local.reshape(pairs * TILE, TILE))
    pieces = place(meta, moved_y, [gram_local])
    y_cells = [to_rows(pieces[part * shares : (part + 1) * shares]) for part in range(parts)]
    gram = sum_pieces(gram, slabs, pieces[:1])
    for hop in hops():
        gram = add(gram, swap(gram, "snap", hop), [] if hop == 1 else y_cells[0][1:3])
    gram = lax.all_gather(gram, "space", axis=0, tiled=True)

    steps = factor_steps(gram.reshape(pairs, TILE, TILE), tiles, rows_total, [])
    state = next(steps)
    for _ in range(tiles - 3):
        state = steps.send([])
    cross_local = cross_sum(x_cells, y_cells, [state])
    cross = to_pieces(cross_local)
    state = steps.send([cross_local])
    r_factor, inverse, *terms = steps.send([])

    cross = sum_pieces(cross, slabs, [r_factor])
    q_basis = None
    for call, hop in enumerate(hops()):
        q_basis = basis(x_cells, terms, call, 2, q_basis, [cross])
        cross = add(cross, swap(cross, "snap", hop), [q_basis])
    same = join([cross] + [swap(cross, "space", m) for m in range(CORES, slabs, CORES)], [])
    projection = project(inverse, same, swap(same, "space", 1), slabs, math.sqrt(rows_total))
    return q_basis, r_factor, projection


def solution(mesh):
    in_specs = (P("space", None, "snap"), P("space", None, "snap"), P("space"))
    out_specs = (P("space", "snap", None), P(), P())
    return jax.shard_map(body, mesh=mesh, in_specs=in_specs, out_specs=out_specs, check_vma=False)
```
